32 devices in a mesh: parts: 2 (over y), req: 4 (over z), tp: 4 (over x, core).
Axes of the slice: x: 2, y: 2, z: 4, core: 2. Of those that a mesh axis runs over, the one named last changes fastest.
Arguments:
- mixer_in: bfloat16 [8192, 8192], P(('parts', 'req'), 'tp'), parts along dimension 0, may hold values from -6 to 6
- maps_in: bfloat16 [8192, 8, 512], P(('parts', 'req'), 'tp'), parts along dimension 0, may hold values from -6 to 6
- delta_raw: bfloat16 [8192, 128], P(('parts', 'req'), 'tp'), parts along dimension 0, may hold values from -5 to 1.5
- conv_cache: bfloat16 [32, 3, 8192], P(('parts', 'req'), None, 'tp'), parts along dimension 0, may hold values from -6 to 6
- maps_cache: bfloat16 [32, 3, 8, 512], P(('parts', 'req'), None, 'tp'), parts along dimension 0, may hold values from -6 to 6
- conv_weight: bfloat16 [4, 8192], P(None, 'tp'), may hold values from -3 to 3
- maps_weight: bfloat16 [4, 8, 512], P(None, 'tp'), may hold values from -3 to 3
- decay_log: float32 [128], P('tp'), may hold values from -3.5 to 0.7
- skip_gain: float32 [128], P('tp'), may hold values from 0.5 to 2
- state_pool: bfloat16 [512, 128, 4, 256], P(('parts', 'req'), 'tp'), parts along dimension 0, may hold values from -0.59765625 to 0.59765625
- queries: bfloat16 [8192, 32, 128], P(('parts', 'req'), 'tp'), parts along dimension 0, may hold values from -7 to 7
- suffix_keyvals: bfloat16 [8192, 8, 256], P(('parts', 'req'), 'tp'), parts along dimension 0, may hold values from -7 to 7
- page_pool: bfloat16 [512, 64, 8, 256], P(('parts', 'req'), None, 'tp'), parts along dimension 0, may hold values from -6 to 6
- prefix_tokens: int32 [32], P('parts'), parts along dimension 0, may hold values from 1 to 1024, as said below
- page_place: int32 [32, 16], P('parts'), parts along dimension 0, may hold values from 0 to 255, as said below
- state_place: int32 [32, 16], P('parts'), parts along dimension 0, may hold values from 0 to 255, as said below
- store_place: int32 [32, 16], P('parts'), parts along dimension 0, may hold values from 0 to 255, as said below
Outputs:
- mixer_out: bfloat16 [8192, 8192], P(('parts', 'req'), 'tp'), parts along dimension 0
- attention_out: bfloat16 [8192, 32, 128], P(('parts', 'req'), 'tp'), parts along dimension 0
- stored_states: bfloat16 [512, 128, 4, 256], P(('parts', 'req'), 'tp'), parts along dimension 0
The draws below stay inside these ranges and needn't reach their ends.
There are 2 independent parts, one for each index of `parts`. The reference program is written for one: setup_inputs(seed, part) draws one part's arguments, and reference() takes and returns one part's arrays. A program takes and returns all parts, laid end to end along the dimension named above; an argument that names none is the same for every part. Nothing has to cross between parts.
Inputs may be any that keep to these rules, and one draw needn't show every extreme that they name: `prefix_tokens`: tokens of request r already cached. Some request has exactly 1024. `page_place`: row of page_pool holding page j of request r: an index along req times 4 * 16, plus a slot. Every row is named exactly once; of the entries of the 4 requests of one index of req, exactly 16 lie on each index of req. Pages from prefix_tokens on are unused. `state_place`: row of state_pool holding head channels j * 4 to (j + 1) * 4 - 1 of request r's state: an index along req times 4 * 16, plus a slot. Every row is named exactly once; of the entries of the 4 requests of one index of req, exactly 16 lie on each index of req. `store_place`: row of stored_states receiving page j of request r's final state, laid out as in state_place, with the same two properties.
All inputs are finite; a program needn't handle non-finite values.
Results may differ from the reference program's by a relative error of at most 0.0062.
Values may be sent and summed in bfloat16 or wider, within the bound.
No kernel may reach another device: no remote copies, remote signals or barrier semaphores. Data moves between devices by JAX's collectives and lax.ppermute only.
A program may use at most 128 MiB of HBM per device.

```python
import math
import jax
import jax.numpy as jnp
from jax import lax

SSM_HEADS = 128
SSM_HDIM = 64
STATE = 256
GROUPS = 8
CONV = 4
Q_HEADS = 32
KV_HEADS = 8
HEAD_DIM = 128
PAGE = 64
PAGES_MAX = 16
PAGE_ROWS = 4
APPENDED_LENGTH = 256
REQUESTS_PER_IDX = 4
STATE_PAGES = 16
REQUESTS = 16
APPENDED_SUM = 4096


def place_table(key, entries, devices):
    first_key, second_key = jax.random.split(key)
    orders = jax.vmap(lambda part_key: jax.random.permutation(part_key, entries))(jax.random.split(first_key, devices))
    owners = orders % devices
    order_rank = orders // devices
    capacity = entries // devices
    shuffles = jax.vmap(lambda part_key: jax.random.permutation(part_key, entries))(jax.random.split(second_key, devices))
    sender = jnp.arange(devices)[:, None]
    slot_index = shuffles[owners, sender * capacity + order_rank]
    return (owners * entries + slot_index).astype(jnp.int32)


def draw_page_place(key, part):
    key = jax.random.fold_in(key, 11)
    return place_table(key, REQUESTS_PER_IDX * PAGES_MAX, REQUESTS // REQUESTS_PER_IDX).reshape(REQUESTS, PAGES_MAX)


def draw_state_place(key, part):
    key = jax.random.fold_in(key, 12)
    return place_table(key, REQUESTS_PER_IDX * STATE_PAGES, REQUESTS // REQUESTS_PER_IDX).reshape(REQUESTS, STATE_PAGES)


def draw_store_place(key, part):
    key = jax.random.fold_in(key, 13)
    return place_table(key, REQUESTS_PER_IDX * STATE_PAGES, REQUESTS // REQUESTS_PER_IDX).reshape(REQUESTS, STATE_PAGES)


def draw_prefix_tokens(key, part):
    key = jax.random.fold_in(key, 14)
    level_key, length_key, chosen_key = jax.random.split(key, 3)
    longest = PAGES_MAX * PAGE
    levels = jax.random.randint(level_key, (REQUESTS,), 0, 4)
    upper_bounds = longest // 2 ** levels
    lengths = 1 + jax.random.randint(length_key, (REQUESTS,), 0, longest) % upper_bounds
    chosen = jax.random.randint(chosen_key, (), 0, REQUESTS)
    return lengths.at[chosen].set(longest).astype(jnp.int32)


def draw_queries(key, part):
    key = jax.random.fold_in(key, 21)
    shape = (APPENDED_SUM, Q_HEADS, HEAD_DIM)
    values = jnp.clip(jax.random.normal(key, shape), -6.0, 6.0)
    return values.astype(jnp.bfloat16)


def draw_suffix_keyvals(key, part):
    key = jax.random.fold_in(key, 22)
    shape = (APPENDED_SUM, KV_HEADS, 2 * HEAD_DIM)
    values = jnp.clip(jax.random.normal(key, shape), -6.0, 6.0)
    return values.astype(jnp.bfloat16)


def draw_decay_log(key, part):
    key = jax.random.fold_in(key, 31)
    pick_key, fast_key, slow_key = jax.random.split(key, 3)
    fast_share = 0.5
    quick = jax.random.uniform(pick_key, (SSM_HEADS,)) < fast_share
    fast_rate = jnp.exp(jax.random.uniform(fast_key, (SSM_HEADS,), minval=math.log(1.2), maxval=math.log(2.0)))
    slow_rate = jnp.exp(jax.random.uniform(slow_key, (SSM_HEADS,), minval=math.log(0.13), maxval=math.log(0.2)))
    return jnp.log(jnp.where(quick, fast_rate, slow_rate)).astype(jnp.float32)


def draw_delta_raw(key, part):
    key = jax.random.fold_in(key, 41)
    starting_seed, clustered_seed = jax.random.split(key)
    starting_amount = jax.random.uniform(starting_seed, (APPENDED_SUM, SSM_HEADS), minval=-5.0, maxval=-3.5)
    clustered_batches = jax.random.uniform(clustered_seed, (APPENDED_SUM, 1)) < 2.0 / APPENDED_LENGTH
    return jnp.where(clustered_batches, 1.5, starting_amount).astype(jnp.bfloat16)


def steps_of(stream_key, dims, cuts, low, largest):
    def one(dim, blocks):
        heights = jax.random.uniform(jax.random.fold_in(jax.random.fold_in(stream_key, 6), dim), (blocks,), jnp.float32, low / len(cuts), largest / len(cuts))
        return jnp.repeat(jnp.exp(heights), dims[dim] // blocks).reshape((-1,) + (1,) * (len(dims) - dim - 1))

    level = one(*cuts[0])
    for cut in cuts[1:]:
        level = level * one(*cut)
    return level


def normal_values(rng, dims, width, limit, cuts=(), kind=jnp.bfloat16):
    values = jax.random.normal(rng, dims, jnp.float32) * width
    if len(cuts) > 0:
        values = steps_of(rng, dims, cuts, -0.22, 0.18) * values
    return jnp.clip(values, min=-limit, max=limit).astype(kind)


def setup_inputs(seed: int = 0, part: int = 0) -> dict:
    arg_keys = jax.random.split(jax.random.key(seed), 18)
    part_splits = jax.random.split(jax.random.fold_in(arg_keys[17], part), 18)
    mixer_in = normal_values(part_splits[0], (APPENDED_SUM, SSM_HEADS * SSM_HDIM), 1.0, 6.0, ((0, 4), (1, 4)))
    maps_in = normal_values(part_splits[1], (APPENDED_SUM, GROUPS, 2 * STATE), 1.0, 6.0, ((0, 4), (1, 4)))
    delta_raw = draw_delta_raw(jax.random.fold_in(jax.random.fold_in(arg_keys[17], part), 71), part)
    conv_cache = normal_values(part_splits[3], (REQUESTS, CONV - 1, SSM_HEADS * SSM_HDIM), 1.0, 6.0, ((0, 4), (2, 4)))
    maps_cache = normal_values(part_splits[4], (REQUESTS, CONV - 1, GROUPS, 2 * STATE), 1.0, 6.0, ((0, 4), (2, 4)))
    conv_weight = normal_values(arg_keys[5], (CONV, SSM_HEADS * SSM_HDIM), CONV ** -0.5, 3.0, ((1, 4),))
    maps_weight = normal_values(arg_keys[6], (CONV, GROUPS, 2 * STATE), CONV ** -0.5, 3.0, ((1, 4),))
    decay_log = draw_decay_log(jax.random.fold_in(arg_keys[17], 71), part)
    skip_gain = jnp.clip(jnp.exp(math.log(2.0) - 1.3862944 * jax.random.uniform(arg_keys[8], (SSM_HEADS,), jnp.float32) ** steps_of(arg_keys[8], (SSM_HEADS,), ((0, 4),), -0.2, 0.2)), 0.5, 2.0)
    state_pool = normal_values(part_splits[9], (REQUESTS * STATE_PAGES, SSM_HEADS, PAGE_ROWS, STATE), 0.1, 0.59765625, ((0, 4), (1, 4)))
    queries = draw_queries(jax.random.fold_in(jax.random.fold_in(arg_keys[17], part), 71), part)
    suffix_keyvals = draw_suffix_keyvals(jax.random.fold_in(jax.random.fold_in(arg_keys[17], part), 71), part)
    page_pool = normal_values(part_splits[12], (REQUESTS * PAGES_MAX, PAGE, KV_HEADS, 2 * HEAD_DIM), 1.0, 6.0, ((0, 4), (2, 4)))
    prefix_tokens = draw_prefix_tokens(jax.random.fold_in(jax.random.fold_in(arg_keys[17], part), 71), part)
    page_place = draw_page_place(jax.random.fold_in(jax.random.fold_in(arg_keys[17], part), 71), part)
    state_place = draw_state_place(jax.random.fold_in(jax.random.fold_in(arg_keys[17], part), 71), part)
    store_place = draw_store_place(jax.random.fold_in(jax.random.fold_in(arg_keys[17], part), 71), part)
    return dict(mixer_in=mixer_in, maps_in=maps_in, delta_raw=delta_raw, conv_cache=conv_cache, maps_cache=maps_cache, conv_weight=conv_weight, maps_weight=maps_weight, decay_log=decay_log, skip_gain=skip_gain, state_pool=state_pool, queries=queries, suffix_keyvals=suffix_keyvals, page_pool=page_pool, prefix_tokens=prefix_tokens, page_place=page_place, state_place=state_place, store_place=store_place)


def product(access_pattern, former, latter):
    return jnp.einsum(access_pattern, former.astype(jnp.float32), latter.astype(jnp.float32), precision=lax.Precision.HIGHEST)


def conv_silu(sequence, cache, weight):
    length = sequence.shape[0]
    joined = jnp.concatenate([cache.astype(jnp.float32), sequence.astype(jnp.float32)], axis=0)
    summed = jnp.zeros(sequence.shape, jnp.float32)
    for offset in range(weight.shape[0]):
        summed = summed + weight[offset].astype(jnp.float32) * joined[offset:offset + length]
    return jax.nn.silu(summed).astype(jnp.bfloat16)


def mixer(inputs, map_inputs, deltas, cache_conv, cache_maps, weight_conv, weight_maps, decay_log, skip_gain, prior):
    length = inputs.shape[0]
    groups = map_inputs.shape[1]
    state_size = map_inputs.shape[2] // 2
    head_count = deltas.shape[1]
    per_group = head_count // groups
    page_count = prior.shape[0]
    row_count = prior.shape[3]
    conv_values = conv_silu(inputs, cache_conv, weight_conv)
    conv_maps = conv_silu(map_inputs, cache_maps, weight_maps)
    input_map = conv_maps[:, :, :state_size]
    output_map = conv_maps[:, :, state_size:]
    delta_t = jax.nn.softplus(deltas.astype(jnp.float32))
    log_decay = jnp.cumsum(-delta_t * jnp.exp(decay_log)[None, :], axis=0)
    intersection = product('tgn,sgn->gts', output_map, input_map)
    decay_heads = log_decay.T.reshape(groups, per_group, length)
    gaps_log = decay_heads[:, :, :, None] - decay_heads[:, :, None, :]
    causal = jnp.arange(length)[:, None] >= jnp.arange(length)[None, :]
    decays = jnp.where(causal, jnp.exp(jnp.where(causal, gaps_log, 0.0)), 0.0)
    delta_heads = delta_t.T.reshape(groups, per_group, 1, length)
    mixing = (intersection[:, None] * decays * delta_heads).astype(jnp.bfloat16)
    values = conv_values.reshape(length, groups, per_group, page_count, row_count)
    within = product('gkts,sgkpq->tgkpq', mixing, values)
    carried = product('tgn,pgkqn->tgkpq', output_map, prior)
    growth = jnp.exp(log_decay).reshape(length, groups, per_group)
    skip_heads = skip_gain.reshape(groups, per_group)
    result = within + growth[:, :, :, None, None] * carried + skip_heads[None, :, :, None, None] * values.astype(jnp.float32)
    mixer_out = result.reshape(length, -1).astype(jnp.bfloat16)
    tail_scale = jnp.exp(log_decay[-1][None, :] - log_decay) * delta_t
    scaled = (values.astype(jnp.float32) * tail_scale.reshape(length, groups, per_group)[:, :, :, None, None]).astype(jnp.bfloat16)
    update = product('tgkpq,tgn->pgkqn', scaled, input_map)
    final_growth = jnp.exp(log_decay[-1]).reshape(groups, per_group)
    final_state = final_growth[None, :, :, None, None] * prior.astype(jnp.float32) + update
    return mixer_out, final_state.astype(jnp.bfloat16)


def attend(query_block, fresh_kv, pages, cached):
    length = query_block.shape[0]
    head_dim = query_block.shape[2]
    kv_count = fresh_kv.shape[1]
    per_kv = query_block.shape[1] // kv_count
    prefix = pages.shape[0]
    key_rows = jnp.concatenate([pages[:, :, :head_dim], fresh_kv[:, :, :head_dim]], axis=0)
    value_rows = jnp.concatenate([pages[:, :, head_dim:], fresh_kv[:, :, head_dim:]], axis=0)
    grouped = query_block.reshape(length, kv_count, per_kv, head_dim)
    scores = product('tkgd,jkd->kgtj', grouped, key_rows) * (head_dim ** -0.5)
    positions = jnp.arange(prefix + length)[None, :]
    allowed = jnp.where(positions < prefix, positions < cached, positions - prefix <= jnp.arange(length)[:, None])
    scores = jnp.where(allowed, scores, -jnp.inf)
    row_max = jnp.max(scores, axis=-1, keepdims=True)
    exponent = jnp.exp(scores - row_max)
    row_total = jnp.sum(exponent, axis=-1)
    mixture_shares = exponent.astype(jnp.bfloat16)
    attended = product('kgtj,jkd->tkgd', mixture_shares, value_rows) / row_total.transpose(2, 0, 1)[:, :, :, None]
    return attended.reshape(length, -1, head_dim).astype(jnp.bfloat16)


def reference(mixer_in, maps_in, delta_raw, conv_cache, maps_cache, conv_weight, maps_weight, decay_log, skip_gain, state_pool, queries, suffix_keyvals, page_pool, prefix_tokens, page_place, state_place, store_place):
    per_group = SSM_HEADS // GROUPS

    def mamba_request(request):
        inputs, map_inputs, deltas, cache_conv, cache_maps, places = request
        prior = state_pool[places].reshape(STATE_PAGES, GROUPS, per_group, PAGE_ROWS, STATE)
        return mixer(inputs, map_inputs, deltas, cache_conv, cache_maps, conv_weight, maps_weight, decay_log, skip_gain, prior)

    outputs, finals = lax.map(mamba_request, (mixer_in.reshape(REQUESTS, APPENDED_LENGTH, -1), maps_in.reshape(REQUESTS, APPENDED_LENGTH, GROUPS, 2 * STATE), delta_raw.reshape(REQUESTS, APPENDED_LENGTH, SSM_HEADS), conv_cache, maps_cache, state_place))
    mixer_out = outputs.reshape(APPENDED_SUM, -1)
    stored_states = jnp.zeros(state_pool.shape, jnp.bfloat16).at[store_place.reshape(-1)].set(finals.reshape(state_pool.shape))

    def attention_request(request):
        query_block, fresh_kv, places, cached = request
        pages = page_pool[places].reshape(PAGES_MAX * PAGE, KV_HEADS, 2 * HEAD_DIM)
        return attend(query_block, fresh_kv, pages, cached)

    attention_out = lax.map(attention_request, (queries.reshape(REQUESTS, APPENDED_LENGTH, Q_HEADS, HEAD_DIM), suffix_keyvals.reshape(REQUESTS, APPENDED_LENGTH, KV_HEADS, 2 * HEAD_DIM), page_place, prefix_tokens))
    return mixer_out, attention_out.reshape(APPENDED_SUM, Q_HEADS, HEAD_DIM), stored_states
```

```python
import functools

import jax
import jax.numpy as jnp
from jax import lax
from jax.experimental import pallas as pl
from jax.experimental.pallas import tpu as pltpu
from jax.sharding import PartitionSpec as P

APPENDED_LENGTH = 256
REQUESTS_PER_IDX = 4
VMEM_LIMIT = 48 * 1024 * 1024
SHARES = (7, 8, 9, 10, 11, 12, 13, 16)
HIDDEN = (((1,), (1,)), ((), ()))


def params():
    return pltpu.CompilerParams(vmem_limit_bytes=VMEM_LIMIT)


def any_spec():
    return pl.BlockSpec(memory_space=pl.ANY)


def own_entries(place_ref, base, slots, position, row, emit):
    for j in range(place_ref.shape[1]):
        slot = place_ref[row, j] - base
        mine = (slot >= 0) & (slot < slots)

        @pl.when(mine)
        def _(slot=slot, position=position, j=j):
            emit(position, slot)

        position = position + jnp.where(mine, 1, 0)
    return position


def gather_kernel(capacity, me_ref, place_ref, pool_ref, out_ref, sem):
    slots = pool_ref.shape[0]
    base = me_ref[0] * slots

    def row_step(row, position):
        position = jnp.where(row % REQUESTS_PER_IDX == 0, 0, position)
        first = (row // REQUESTS_PER_IDX) * capacity

        def emit(at, slot):
            pltpu.make_async_copy(pool_ref.at[slot], out_ref.at[first + at], sem).start()

        return own_entries(place_ref, base, slots, position, row, emit)

    lax.fori_loop(0, place_ref.shape[0], row_step, jnp.int32(0))
    pltpu.make_async_copy(pool_ref, out_ref, sem).wait()


def scatter_kernel(capacity, me_ref, place_ref, got_ref, out_ref, sem):
    slots = out_ref.shape[0]
    base = me_ref[0] * slots

    def row_step(row, position):
        position = jnp.where(row % REQUESTS_PER_IDX == 0, 0, position)
        first = (row // REQUESTS_PER_IDX) * capacity

        def emit(at, slot):
            pltpu.make_async_copy(got_ref.at[first + at], out_ref.at[slot], sem).start()

        return own_entries(place_ref, base, slots, position, row, emit)

    lax.fori_loop(0, place_ref.shape[0], row_step, jnp.int32(0))
    pltpu.make_async_copy(got_ref, out_ref, sem).wait()


def route_pages(kernel, name, me, place, pages):
    capacity = pages.shape[0] // lax.axis_size("req")
    size = pages.size * pages.dtype.itemsize
    return pl.pallas_call(
        functools.partial(kernel, capacity),
        out_shape=jax.ShapeDtypeStruct(pages.shape, pages.dtype),
        grid_spec=pltpu.PrefetchScalarGridSpec(
            num_scalar_prefetch=2,
            grid=(1,),
            in_specs=[any_spec()],
            out_specs=any_spec(),
            scratch_shapes=[pltpu.SemaphoreType.DMA],
        ),
        cost_estimate=pl.CostEstimate(flops=0, bytes_accessed=2 * size, transcendentals=0),
        compiler_params=params(),
        name=name,
    )(me, place, pages)


def gather_used_kernel(counts, me_ref, choice_ref, place_ref, prefix_ref, pool_ref, *rest):
    outs, sem = rest[:-1], rest[-1]
    slots, page = pool_ref.shape[0], pool_ref.shape[2]
    base = me_ref[0] * slots
    columns = place_ref.shape[1]
    servers = place_ref.shape[0] // REQUESTS_PER_IDX
    for option, count in enumerate(counts):
        out_ref = outs[option]

        @pl.when(choice_ref[0] == option)
        def _(count=count, out_ref=out_ref):
            def server_step(server, carry):
                position = jnp.int32(0)
                for wanted in (True, False):

                    def row_step(offset, position, wanted=wanted):
                        row = server * REQUESTS_PER_IDX + offset
                        tokens = prefix_ref[row]
                        for j in range(columns):
                            slot = place_ref[row, j] - base
                            used = j * page < tokens
                            take = (slot >= 0) & (slot < slots) & (position < count)
                            take = take & (used if wanted else jnp.logical_not(used))

                            @pl.when(take)
                            def _(slot=slot, position=position):
                                pltpu.make_async_copy(
                                    pool_ref.at[slot], out_ref.at[server * count + position], sem
                                ).start()

                            position = position + jnp.where(take, 1, 0)
                        return position

                    position = lax.fori_loop(0, REQUESTS_PER_IDX, row_step, position)
                return carry

            lax.fori_loop(0, servers, server_step, jnp.int32(0))
            pltpu.make_async_copy(pool_ref.at[pl.ds(0, servers * count)], out_ref, sem).wait()


def gather_used(counts, me, choice, place, prefix, pages):
    servers = lax.axis_size("req")
    shapes = [
        jax.ShapeDtypeStruct((servers * count,) + pages.shape[1:], pages.dtype) for count in counts
    ]
    return pl.pallas_call(
        functools.partial(gather_used_kernel, counts),
        out_shape=shapes,
        grid_spec=pltpu.PrefetchScalarGridSpec(
            num_scalar_prefetch=4,
            grid=(1,),
            in_specs=[any_spec()],
            out_specs=[any_spec()] * len(counts),
            scratch_shapes=[pltpu.SemaphoreType.DMA],
        ),
        cost_estimate=pl.CostEstimate(
            flops=0, bytes_accessed=2 * pages.size * 2, transcendentals=0
        ),
        compiler_params=params(),
        name="gather_used_pages",
    )(me, choice, place, prefix, pages)


def conv_silu(buffer, cache_ref, values, weight_ref):
    length = values.shape[0]
    taps = weight_ref.shape[-2]
    buffer[0:8, :] = cache_ref[...]
    buffer[8:, :] = values.astype(jnp.float32)
    start = 8 - (taps - 1)
    summed = weight_ref[0:1, :] * buffer[start : start + length, :]
    for tap in range(1, taps):
        at = start + tap
        summed = summed + weight_ref[tap : tap + 1, :] * buffer[at : at + length, :]
    return jax.nn.silu(summed).astype(jnp.bfloat16)


def inner_kernel(
    heads,
    x_ref,
    x_cache_ref,
    x_weight_ref,
    maps_ref,
    maps_cache_ref,
    maps_weight_ref,
    decay_row_ref,
    decay_col_ref,
    delta_row_ref,
    tail_ref,
    skip_ref,
    partial_ref,
    update_ref,
    output_map_ref,
    x_buffer,
    maps_buffer,
    x_values,
    scaled,
):
    length, width = x_ref.shape
    head_dim = width // heads
    state = maps_ref.shape[1] // 2
    x_values[...] = conv_silu(x_buffer, x_cache_ref, x_ref[...], x_weight_ref)
    maps = conv_silu(maps_buffer, maps_cache_ref, maps_ref[...], maps_weight_ref)
    input_map, output_map = maps[:, :state], maps[:, state:]
    output_map_ref[...] = output_map
    intersection = lax.dot_general(
        output_map, input_map, HIDDEN, preferred_element_type=jnp.float32
    )
    rows = lax.broadcasted_iota(jnp.int32, (length, length), 0)
    columns = lax.broadcasted_iota(jnp.int32, (length, length), 1)
    causal = rows >= columns
    for h in range(heads):
        lanes = slice(h * head_dim, (h + 1) * head_dim)
        gap = decay_col_ref[:, h : h + 1] - decay_row_ref[h : h + 1, :]
        decays = jnp.where(causal, jnp.exp(jnp.where(causal, gap, 0.0)), 0.0)
        mixing = (intersection * decays * delta_row_ref[h : h + 1, :]).astype(jnp.bfloat16)
        x_head = x_values[:, lanes]
        x_wide = x_head.astype(jnp.float32)
        within = jnp.dot(mixing, x_head, preferred_element_type=jnp.float32)
        partial_ref[:, lanes] = within + skip_ref[:, lanes] * x_wide
        scaled[:, lanes] = (x_wide * tail_ref[:, h : h + 1]).astype(jnp.bfloat16)
    update_ref[...] = lax.dot_general(
        scaled[...], input_map, (((0,), (0,)), ((), ())), preferred_element_type=jnp.float32
    )


def state_kernel(
    me_ref,
    state_place_ref,
    store_place_ref,
    got_ref,
    update_ref,
    partial_ref,
    output_map_ref,
    growth_ref,
    decay_row_ref,
    out_ref,
    send_ref,
    pages,
    finals,
    prior,
    arrival,
    departure,
    counts,
    in_sems,
    out_sems,
):
    request, group = pl.program_id(0), pl.program_id(1)
    page_count, heads, page_rows, state = pages.shape
    entries = REQUESTS_PER_IDX * page_count
    slots = got_ref.shape[0]
    peers = counts.shape[0]
    capacity = entries // peers
    head_dim = page_count * page_rows

    @pl.when((request == 0) & (group == 0))
    def _():
        for place_ref, found in ((state_place_ref, arrival), (store_place_ref, departure)):
            for peer in range(peers):
                counts[peer] = 0

            def row_step(offset, carry, place_ref=place_ref, found=found):
                for j in range(page_count):
                    owner = place_ref[me_ref[0] * REQUESTS_PER_IDX + offset, j] // slots
                    rank = counts[owner]
                    counts[owner] = rank + 1
                    found[offset * page_count + j] = owner * capacity + rank
                return carry

            lax.fori_loop(0, REQUESTS_PER_IDX, row_step, jnp.int32(0))

    half = pl.ds(group * heads, heads)
    arrivals = [
        pltpu.make_async_copy(
            got_ref.at[arrival[request * page_count + j], half], pages.at[j], in_sems.at[j]
        )
        for j in range(page_count)
    ]
    for copy in arrivals:
        copy.start()
    departures = [
        pltpu.make_async_copy(
            finals.at[j], send_ref.at[departure[request * page_count + j], half], out_sems.at[j]
        )
        for j in range(page_count)
    ]
    last = decay_row_ref.shape[1] - 1
    for j in range(page_count):
        arrivals[j].wait()
        for h in range(heads):
            at = h * head_dim + j * page_rows
            old = pages[j, h].astype(jnp.float32)
            prior[at : at + page_rows, :] = old
            growth = jnp.exp(decay_row_ref[h : h + 1, last : last + 1])
            finals[j, h] = (growth * old + update_ref[at : at + page_rows, :]).astype(jnp.bfloat16)
        departures[j].start()
    carried = lax.dot_general(
        output_map_ref[...],
        prior[...].astype(jnp.bfloat16),
        HIDDEN,
        preferred_element_type=jnp.float32,
    )
    for h in range(heads):
        lanes = slice(h * head_dim, (h + 1) * head_dim)
        out_ref[:, lanes] = (
            partial_ref[:, lanes] + growth_ref[:, h : h + 1] * carried[:, lanes]
        ).astype(jnp.bfloat16)
    for copy in departures:
        copy.wait()


def attend_kernel(
    scale,
    count,
    me_ref,
    place_ref,
    prefix_ref,
    got_ref,
    query_ref,
    fresh_ref,
    out_ref,
    cached_kv,
    row_max,
    row_total,
    attended,
    arrival,
    counts,
    sems,
):
    request, kv_head = pl.program_id(0), pl.program_id(1)
    per_kv, length, head_dim = query_ref.shape
    page = got_ref.shape[2]
    page_count = place_ref.shape[1]
    slots = REQUESTS_PER_IDX * page_count
    peers = counts.shape[0]
    chunk = length
    first = me_ref[0] * REQUESTS_PER_IDX

    @pl.when((request == 0) & (kv_head == 0))
    def _():
        cached_kv[...] = jnp.zeros_like(cached_kv)
        for peer in range(peers):
            counts[peer] = 0

        def row_step(offset, carry):
            tokens = prefix_ref[first + offset]
            for j in range(page_count):
                owner = place_ref[first + offset, j] // slots
                rank = counts[owner]
                used = j * page < tokens
                counts[owner] = rank + jnp.where(used, 1, 0)
                arrival[offset * page_count + j] = owner * count + jnp.where(used, rank, 0)
            return carry

        lax.fori_loop(0, REQUESTS_PER_IDX, row_step, jnp.int32(0))

    tokens = prefix_ref[first + request]
    copies = [
        pltpu.make_async_copy(
            got_ref.at[arrival[request * page_count + j], kv_head],
            cached_kv.at[pl.ds(j * page, page)],
            sems.at[j],
        )
        for j in range(page_count)
    ]
    for j in range(page_count):

        @pl.when(j * page < tokens)
        def _(j=j):
            copies[j].start()

    rows = lax.broadcasted_iota(jnp.int32, (length, length), 0)
    columns = lax.broadcasted_iota(jnp.int32, (length, length), 1)
    fresh_keys = fresh_ref[:, :head_dim]
    fresh_values = fresh_ref[:, head_dim:]
    for k in range(per_kv):
        scores = (
            lax.dot_general(query_ref[k], fresh_keys, HIDDEN, preferred_element_type=jnp.float32)
            * scale
        )
        scores = jnp.where(columns <= rows, scores, -jnp.inf)
        top = jnp.max(scores, axis=-1, keepdims=True)
        exponent = jnp.exp(scores - top)
        row_max[k] = top
        row_total[k] = jnp.sum(exponent, axis=-1, keepdims=True)
        attended[k] = jnp.dot(
            exponent.astype(jnp.bfloat16), fresh_values, preferred_element_type=jnp.float32
        )
    for j in range(page_count):

        @pl.when(j * page < tokens)
        def _(j=j):
            copies[j].wait()

    def chunk_step(step, carry):
        start = pl.multiple_of(step * chunk, chunk)
        keys = cached_kv[pl.ds(start, chunk), :head_dim]
        values = cached_kv[pl.ds(start, chunk), head_dim:]
        for k in range(per_kv):
            scores = (
                lax.dot_general(query_ref[k], keys, HIDDEN, preferred_element_type=jnp.float32)
                * scale
            )
            scores = jnp.where(start + columns < tokens, scores, -jnp.inf)
            old = row_max[k]
            top = jnp.maximum(old, jnp.max(scores, axis=-1, keepdims=True))
            fade = jnp.exp(old - top)
            exponent = jnp.exp(scores - top)
            row_max[k] = top
            row_total[k] = row_total[k] * fade + jnp.sum(exponent, axis=-1, keepdims=True)
            attended[k] = attended[k] * fade + jnp.dot(
                exponent.astype(jnp.bfloat16), values, preferred_element_type=jnp.float32
            )
        return carry

    lax.fori_loop(0, (tokens + chunk - 1) // chunk, chunk_step, jnp.int32(0))
    for k in range(per_kv):
        out_ref[k] = (attended[k] / row_total[k]).astype(jnp.bfloat16)


def body(
    mixer_in,
    maps_in,
    delta_raw,
    conv_cache,
    maps_cache,
    conv_weight,
    maps_weight,
    decay_log,
    skip_gain,
    state_pool,
    queries,
    suffix_keyvals,
    page_pool,
    prefix_tokens,
    page_place,
    state_place,
    store_place,
):
    peers = lax.axis_size("req")
    me = lax.axis_index("req").astype(jnp.int32).reshape(1)
    requests, length = REQUESTS_PER_IDX, APPENDED_LENGTH
    groups = maps_in.shape[1]
    state = maps_in.shape[2] // 2
    heads = delta_raw.shape[1]
    per_group = heads // groups
    width = mixer_in.shape[1]
    group_width = width // groups
    head_dim = width // heads
    slots, _, page_rows, _ = state_pool.shape
    page_count = state_place.shape[1]
    kv_heads = page_pool.shape[2]
    attend_dim = queries.shape[2]
    per_kv = queries.shape[1] // kv_heads
    page = page_pool.shape[1]
    prefix_pages = page_place.shape[1]
    page_slots = page_pool.shape[0]
    pair_pages = requests * prefix_pages // peers
    taps = conv_weight.shape[0]

    def exchange(pages):
        return lax.all_to_all(pages, "req", split_axis=0, concat_axis=0, tiled=True)

    state_send = route_pages(gather_kernel, "gather_states", me, state_place, state_pool)
    state_got = exchange(state_send)

    counts = tuple(sorted({max(1, pair_pages * share // 16) for share in SHARES}))
    used = jnp.arange(prefix_pages)[None, :] * page < prefix_tokens[:, None]
    holders = page_place // page_slots
    pairs = used[:, :, None] & (holders[:, :, None] == jnp.arange(peers)[None, None, :])
    needed = jnp.max(
        jnp.sum(pairs.reshape(peers, -1, peers).astype(jnp.int32), axis=1)
    )
    choice = jnp.sum((needed > jnp.array(counts[:-1], jnp.int32)).astype(jnp.int32))
    page_sends = gather_used(
        counts,
        me,
        choice.reshape(1),
        page_place,
        prefix_tokens,
        page_pool.transpose(0, 2, 1, 3),
    )

    delta = jax.nn.softplus(delta_raw.T.astype(jnp.float32)).reshape(heads, requests, length)
    log_decay = jnp.cumsum(-delta * jnp.exp(decay_log)[:, None, None], axis=2)
    tail = jnp.exp(log_decay[:, :, -1:] - log_decay) * delta
    growth = jnp.exp(log_decay)

    def by_rows(values):
        return values.reshape(groups, per_group, requests, length).transpose(2, 0, 1, 3)

    def by_columns(values):
        return values.reshape(groups, per_group, requests, length).transpose(2, 0, 3, 1)

    decay_row = by_rows(log_decay)
    maps_split = maps_in.transpose(1, 0, 2)
    empty = 8 - (taps - 1)
    x_cache = jnp.pad(conv_cache.astype(jnp.float32), ((0, 0), (empty, 0), (0, 0)))
    maps_edge = jnp.pad(
        maps_cache.transpose(0, 2, 1, 3).astype(jnp.float32), ((0, 0), (0, 0), (empty, 0), (0, 0))
    )
    row_block = pl.BlockSpec((None, None, per_group, length), lambda r, g: (r, g, 0, 0))
    column_block = pl.BlockSpec((None, None, length, per_group), lambda r, g: (r, g, 0, 0))
    x_block = pl.BlockSpec((length, group_width), lambda r, g: (r, g))
    update_block = pl.BlockSpec((None, None, group_width, state), lambda r, g: (r, g, 0, 0))
    map_block = pl.BlockSpec((None, length, state), lambda r, g: (g, r, 0))
    partial, update, output_map = pl.pallas_call(
        functools.partial(inner_kernel, per_group),
        grid=(requests, groups),
        in_specs=[
            x_block,
            pl.BlockSpec((None, 8, group_width), lambda r, g: (r, 0, g)),
            pl.BlockSpec((taps, group_width), lambda r, g: (0, g)),
            pl.BlockSpec((None, length, 2 * state), lambda r, g: (g, r, 0)),
            pl.BlockSpec((None, None, 8, 2 * state), lambda r, g: (r, g, 0, 0)),
            pl.BlockSpec((None, taps, 2 * state), lambda r, g: (g, 0, 0)),
            row_block,
            column_block,
            row_block,
            column_block,
            pl.BlockSpec((1, group_width), lambda r, g: (0, g)),
        ],
        out_specs=[x_block, update_block, map_block],
        out_shape=[
            jax.ShapeDtypeStruct((requests * length, width), jnp.float32),
            jax.ShapeDtypeStruct((requests, groups, group_width, state), jnp.float32),
            jax.ShapeDtypeStruct((groups, requests * length, state), jnp.bfloat16),
        ],
        scratch_shapes=[
            pltpu.VMEM((8 + length, group_width), jnp.float32),
            pltpu.VMEM((8 + length, 2 * state), jnp.float32),
            pltpu.VMEM((length, group_width), jnp.bfloat16),
            pltpu.VMEM((length, group_width), jnp.bfloat16),
        ],
        cost_estimate=pl.CostEstimate(
            flops=3 * requests * length * width * state,
            bytes_accessed=32 * 2**20,
            transcendentals=requests * heads * length * length,
        ),
        compiler_params=params(),
        name="mix_new_tokens",
    )(
        mixer_in,
        x_cache,
        conv_weight.astype(jnp.float32),
        maps_split,
        maps_edge,
        maps_weight.transpose(1, 0, 2).astype(jnp.float32),
        decay_row,
        by_columns(log_decay),
        by_rows(delta),
        by_columns(tail),
        jnp.repeat(skip_gain, head_dim).reshape(1, width),
    )
    growth_col = by_columns(growth)
    grouped_queries = queries.reshape(requests, length, kv_heads, per_kv, attend_dim).transpose(
        0, 2, 3, 1, 4
    )
    fresh = suffix_keyvals.transpose(1, 0, 2)

    def remainder(option, state_got, page_sends, partial, update, output_map, small, attention_in):
        growth_col, decay_row = small
        grouped_queries, fresh = attention_in
        count = counts[option]
        page_got = exchange(page_sends[option])
        mixer_out, final_send = pl.pallas_call(
            state_kernel,
            grid_spec=pltpu.PrefetchScalarGridSpec(
                num_scalar_prefetch=3,
                grid=(requests, groups),
                in_specs=[
                    any_spec(),
                    pl.BlockSpec((None, None, group_width, state), lambda r, g, *_: (r, g, 0, 0)),
                    pl.BlockSpec((length, group_width), lambda r, g, *_: (r, g)),
                    pl.BlockSpec((None, length, state), lambda r, g, *_: (g, r, 0)),
                    pl.BlockSpec((None, None, length, per_group), lambda r, g, *_: (r, g, 0, 0)),
                    pl.BlockSpec((None, None, per_group, length), lambda r, g, *_: (r, g, 0, 0)),
                ],
                out_specs=[
                    pl.BlockSpec((length, group_width), lambda r, g, *_: (r, g)),
                    any_spec(),
                ],
                scratch_shapes=[
                    pltpu.VMEM((page_count, per_group, page_rows, state), jnp.bfloat16),
                    pltpu.VMEM((page_count, per_group, page_rows, state), jnp.bfloat16),
                    pltpu.VMEM((group_width, state), jnp.float32),
                    pltpu.SMEM((requests * page_count,), jnp.int32),
                    pltpu.SMEM((requests * page_count,), jnp.int32),
                    pltpu.SMEM((peers,), jnp.int32),
                    pltpu.SemaphoreType.DMA((page_count,)),
                    pltpu.SemaphoreType.DMA((page_count,)),
                ],
            ),
            out_shape=[
                jax.ShapeDtypeStruct((requests * length, width), jnp.bfloat16),
                jax.ShapeDtypeStruct(state_pool.shape, jnp.bfloat16),
            ],
            cost_estimate=pl.CostEstimate(
                flops=2 * requests * length * width * state,
                bytes_accessed=32 * 2**20,
                transcendentals=0,
            ),
            compiler_params=params(),
            name="advance_states",
        )(
            me,
            state_place,
            store_place,
            state_got,
            update,
            partial,
            output_map,
            growth_col,
            decay_row,
        )
        final_got = exchange(final_send)
        attended = pl.pallas_call(
            functools.partial(attend_kernel, attend_dim**-0.5, count),
            grid_spec=pltpu.PrefetchScalarGridSpec(
                num_scalar_prefetch=3,
                grid=(requests, kv_heads),
                in_specs=[
                    any_spec(),
                    pl.BlockSpec(
                        (None, None, per_kv, length, attend_dim), lambda r, e, *_: (r, e, 0, 0, 0)
                    ),
                    pl.BlockSpec((None, length, 2 * attend_dim), lambda r, e, *_: (e, r, 0)),
                ],
                out_specs=pl.BlockSpec(
                    (None, None, per_kv, length, attend_dim), lambda r, e, *_: (r, e, 0, 0, 0)
                ),
                scratch_shapes=[
                    pltpu.VMEM((prefix_pages * page, 2 * attend_dim), jnp.bfloat16),
                    pltpu.VMEM((per_kv, length, 1), jnp.float32),
                    pltpu.VMEM((per_kv, length, 1), jnp.float32),
                    pltpu.VMEM((per_kv, length, attend_dim), jnp.float32),
                    pltpu.SMEM((requests * prefix_pages,), jnp.int32),
                    pltpu.SMEM((peers,), jnp.int32),
                    pltpu.SemaphoreType.DMA((prefix_pages,)),
                ],
            ),
            out_shape=jax.ShapeDtypeStruct(grouped_queries.shape, jnp.bfloat16),
            cost_estimate=pl.CostEstimate(
                flops=4 * queries.size * (prefix_pages * page + length),
                bytes_accessed=16 * 2**20,
                transcendentals=queries.shape[0] * queries.shape[1] * (prefix_pages * page),
            ),
            compiler_params=params(),
            name="attend",
        )(me, page_place, prefix_tokens, page_got, grouped_queries, fresh)
        attention_out = attended.transpose(0, 3, 1, 2, 4).reshape(queries.shape)
        stored = route_pages(scatter_kernel, "scatter_states", me, store_place, final_got)
        return mixer_out, attention_out, stored

    return lax.switch(
        choice,
        [functools.partial(remainder, option) for option in range(len(counts))],
        state_got,
        page_sends,
        partial,
        update,
        output_map,
        (growth_col, decay_row),
        (grouped_queries, fresh),
    )


def solution(mesh):
    placed = (
        P(("parts", "req"), "tp"),
        P(("parts", "req"), "tp", None),
        P(("parts", "req"), "tp"),
        P(("parts", "req"), None, "tp"),
        P(("parts", "req"), None, "tp", None),
        P(None, "tp"),
        P(None, "tp", None),
        P("tp"),
        P("tp"),
        P(("parts", "req"), "tp", None, None),
        P(("parts", "req"), "tp", None),
        P(("parts", "req"), "tp", None),
        P(("parts", "req"), None, "tp", None),
        P("parts"),
        P("parts", None),
        P("parts", None),
        P("parts", None),
    )
    return jax.shard_map(
        body,
        mesh=mesh,
        in_specs=placed,
        out_specs=(
            P(("parts", "req"), "tp"),
            P(("parts", "req"), "tp", None),
            P(("parts", "req"), "tp", None, None),
        ),
        check_vma=False,
    )
```

```python
import functools

import jax
import jax.numpy as jnp
from jax import lax
from jax.experimental import pallas as pl
from jax.experimental.pallas import tpu as pltpu
from jax.sharding import PartitionSpec as P

APPENDED_LENGTH = 256
REQUESTS_PER_IDX = 4
VMEM_LIMIT = 48 * 1024 * 1024
SHARES = (8, 9, 10, 11, 12, 16)
PASSED = 8
HIDDEN = (((1,), (1,)), ((), ()))


def params():
    return pltpu.CompilerParams(vmem_limit_bytes=VMEM_LIMIT)


def any_spec():
    return pl.BlockSpec(memory_space=pl.ANY)


def hbm_spec():
    return pl.BlockSpec(memory_space=pltpu.HBM)


def own_entries(place_ref, base, slots, position, row, emit):
    for j in range(place_ref.shape[1]):
        slot = place_ref[row, j] - base
        mine = (slot >= 0) & (slot < slots)

        @pl.when(mine)
        def _(slot=slot, position=position, j=j):
            emit(position, slot)

        position = position + jnp.where(mine, 1, 0)
    return position


def gather_kernel(capacity, me_ref, place_ref, pool_ref, out_ref, sem):
    slots = pool_ref.shape[0]
    base = me_ref[0] * slots

    def row_step(row, position):
        position = jnp.where(row % REQUESTS_PER_IDX == 0, 0, position)
        first = (row // REQUESTS_PER_IDX) * capacity

        def emit(at, slot):
            pltpu.make_async_copy(pool_ref.at[slot], out_ref.at[first + at], sem).start()

        return own_entries(place_ref, base, slots, position, row, emit)

    lax.fori_loop(0, place_ref.shape[0], row_step, jnp.int32(0))
    pltpu.make_async_copy(pool_ref, out_ref, sem).wait()


def scatter_kernel(capacity, me_ref, place_ref, got_ref, out_ref, sem):
    slots = out_ref.shape[0]
    base = me_ref[0] * slots

    def row_step(row, position):
        position = jnp.where(row % REQUESTS_PER_IDX == 0, 0, position)
        first = (row // REQUESTS_PER_IDX) * capacity

        def emit(at, slot):
            pltpu.make_async_copy(got_ref.at[first + at], out_ref.at[slot], sem).start()

        return own_entries(place_ref, base, slots, position, row, emit)

    lax.fori_loop(0, place_ref.shape[0], row_step, jnp.int32(0))
    pltpu.make_async_copy(got_ref, out_ref, sem).wait()


def route_pages(kernel, name, me, place, pages):
    capacity = pages.shape[0] // lax.axis_size("req")
    size = pages.size * pages.dtype.itemsize
    return pl.pallas_call(
        functools.partial(kernel, capacity),
        out_shape=pltpu.HBM(pages.shape, pages.dtype),
        grid_spec=pltpu.PrefetchScalarGridSpec(
            num_scalar_prefetch=2,
            grid=(1,),
            in_specs=[hbm_spec()],
            out_specs=hbm_spec(),
            scratch_shapes=[pltpu.SemaphoreType.DMA],
        ),
        cost_estimate=pl.CostEstimate(flops=0, bytes_accessed=2 * size, transcendentals=0),
        compiler_params=params(),
        name=name,
    )(me, place, pltpu.with_memory_space_constraint(pages, pltpu.HBM))


def is_used(place_ref, prefix_ref, page, row, j, owner, slots):
    slot = place_ref[row, j] - owner * slots
    return slot, (slot >= 0) & (slot < slots) & (j * page < prefix_ref[row])


def send_kernel(counts, limits_ref, place_ref, prefix_ref, pool_ref, *rest):
    outs, (filled, needs, sems) = rest[: len(counts)], rest[len(counts) :]
    slots, page = pool_ref.shape[0], pool_ref.shape[2]
    me, limit, choice = limits_ref[0], limits_ref[1], limits_ref[2]
    columns = place_ref.shape[1]
    servers = place_ref.shape[0] // REQUESTS_PER_IDX
    first = counts[0]
    room = sems.shape[0] // servers
    used = functools.partial(is_used, place_ref, prefix_ref, page)

    def count_server(server, carry):
        def count_row(offset, total):
            for j in range(columns):
                _, wanted = used(server * REQUESTS_PER_IDX + offset, j, me, slots)
                total = total + jnp.where(wanted, 1, 0)
            return total

        needs[server] = lax.fori_loop(0, REQUESTS_PER_IDX, count_row, jnp.int32(0))
        return carry

    lax.fori_loop(0, servers, count_server, jnp.int32(0))

    def send(slot, peer, position):
        sem = sems.at[peer * room + position]

        @pl.when(position < first)
        def _():
            pltpu.make_async_copy(pool_ref.at[slot], outs[0].at[peer * first + position], sem).start()

        for option in range(1, len(counts)):
            more = counts[option] - first

            @pl.when((position >= first) & (choice == option))
            def _(option=option, more=more):
                pltpu.make_async_copy(
                    pool_ref.at[slot], outs[option].at[peer * more + position - first], sem
                ).start()

    def send_server(server, carry):
        partner = server + 1 - 2 * (server % 2)
        start = needs[partner] - limit

        def send_row(offset, rank):
            for j in range(columns):
                slot, wanted = used(server * REQUESTS_PER_IDX + offset, j, me, slots)

                @pl.when(wanted & (rank < limit))
                def _(slot=slot, rank=rank):
                    send(slot, server, rank)

                @pl.when(wanted & (rank >= limit) & (partner != me))
                def _(slot=slot, rank=rank):
                    send(slot, partner, start + rank)

                rank = rank + jnp.where(wanted, 1, 0)
            return rank

        lax.fori_loop(0, REQUESTS_PER_IDX, send_row, jnp.int32(0))
        own = jnp.minimum(needs[server], limit)
        passed = jnp.where(partner == me, 0, jnp.maximum(needs[partner] - limit, 0))
        filled[server] = jnp.where(server == me, 0, own + passed)
        return carry

    def others(server, carry):
        @pl.when(server != me)
        def _():
            send_server(server, carry)

        return carry

    filled[me] = 0
    lax.fori_loop(0, servers, others, jnp.int32(0))

    def wait_server(server, carry):
        for position in range(room):

            @pl.when(position < filled[server])
            def _(position=position):
                pltpu.make_async_copy(
                    pool_ref.at[0], outs[0].at[0], sems.at[server * room + position]
                ).wait()

        return carry

    lax.fori_loop(0, servers, wait_server, jnp.int32(0))


def send_used(counts, limits, place, prefix, pages):
    servers = lax.axis_size("req")
    sizes = [counts[0]] + [count - counts[0] for count in counts[1:]]
    shapes = [
        pltpu.HBM((servers * size,) + pages.shape[1:], pages.dtype) for size in sizes
    ]
    return pl.pallas_call(
        functools.partial(send_kernel, counts),
        out_shape=shapes,
        grid_spec=pltpu.PrefetchScalarGridSpec(
            num_scalar_prefetch=3,
            grid=(1,),
            in_specs=[hbm_spec()],
            out_specs=[hbm_spec()] * len(counts),
            scratch_shapes=[
                pltpu.SMEM((servers,), jnp.int32),
                pltpu.SMEM((servers,), jnp.int32),
                pltpu.SemaphoreType.DMA((servers * counts[-1],)),
            ],
        ),
        cost_estimate=pl.CostEstimate(
            flops=0, bytes_accessed=2 * pages.size * 2, transcendentals=0
        ),
        compiler_params=params(),
        name="send_used_pages",
    )(limits, place, prefix, pages)


def pass_kernel(counts, limits_ref, place_ref, prefix_ref, pool_ref, *rest):
    gots, out_ref, sems = rest[: len(counts)], rest[len(counts)], rest[len(counts) + 1]
    slots, page = pool_ref.shape[0], pool_ref.shape[2]
    me, limit, choice = limits_ref[0], limits_ref[1], limits_ref[2]
    columns = place_ref.shape[1]
    servers = place_ref.shape[0] // REQUESTS_PER_IDX
    first = counts[0]
    partner = me + 1 - 2 * (me % 2)
    used = functools.partial(is_used, place_ref, prefix_ref, page)

    def count_for(server, owner):
        def count_row(offset, total):
            for j in range(columns):
                _, wanted = used(server * REQUESTS_PER_IDX + offset, j, owner, slots)
                total = total + jnp.where(wanted, 1, 0)
            return total

        return lax.fori_loop(0, REQUESTS_PER_IDX, count_row, jnp.int32(0))

    def own_pages(at):
        def row_step(offset, carry):
            rank, at = carry
            for j in range(columns):
                slot, wanted = used(partner * REQUESTS_PER_IDX + offset, j, me, slots)
                take = wanted & (rank >= limit)

                @pl.when(take)
                def _(slot=slot, at=at):
                    pltpu.make_async_copy(pool_ref.at[slot], out_ref.at[at], sems.at[at]).start()

                rank = rank + jnp.where(wanted, 1, 0)
                at = at + jnp.where(take, 1, 0)
            return rank, at

        return lax.fori_loop(0, REQUESTS_PER_IDX, row_step, (jnp.int32(0), at))[1]

    def relayed_pages(owner, at):
        start = count_for(me, owner)
        more = jnp.maximum(count_for(partner, owner) - limit, 0)

        def page_step(step, carry):
            position = start + step
            target = at + step

            @pl.when(position < first)
            def _():
                pltpu.make_async_copy(
                    gots[0].at[owner * first + position], out_ref.at[target], sems.at[target]
                ).start()

            for option in range(1, len(counts)):
                size = counts[option] - first

                @pl.when((position >= first) & (choice == option))
                def _(option=option, size=size):
                    pltpu.make_async_copy(
                        gots[option].at[owner * size + position - first],
                        out_ref.at[target],
                        sems.at[target],
                    ).start()

            return carry

        lax.fori_loop(0, more, page_step, jnp.int32(0))
        return at + more

    def owner_step(owner, at):
        at = lax.cond(owner == me, own_pages, lambda at: at, at)
        outside = (owner != me) & (owner != partner)
        return lax.cond(outside, lambda at: relayed_pages(owner, at), lambda at: at, at)

    total = lax.fori_loop(0, servers, owner_step, jnp.int32(0))
    for position in range(sems.shape[0]):

        @pl.when(position < total)
        def _(position=position):
            pltpu.make_async_copy(
                pool_ref.at[0], out_ref.at[position], sems.at[position]
            ).wait()


def pass_on(counts, limits, place, prefix, pages, gots):
    shape = (PASSED,) + pages.shape[1:]
    collected = pl.pallas_call(
        functools.partial(pass_kernel, counts),
        out_shape=pltpu.HBM(shape, pages.dtype),
        grid_spec=pltpu.PrefetchScalarGridSpec(
            num_scalar_prefetch=3,
            grid=(1,),
            in_specs=[any_spec()] * (1 + len(gots)),
            out_specs=hbm_spec(),
            scratch_shapes=[pltpu.SemaphoreType.DMA((PASSED,))],
        ),
        cost_estimate=pl.CostEstimate(flops=0, bytes_accessed=2**20, transcendentals=0),
        compiler_params=params(),
        name="pass_pages_on",
    )(limits, place, prefix, pages, *gots)
    swaps = [(peer, peer ^ 1) for peer in range(lax.axis_size("req"))]
    return lax.ppermute(collected, "req", swaps)


def unwritten(shapes):
    return pl.pallas_call(
        lambda *refs: None,
        out_shape=shapes,
        out_specs=[hbm_spec()] * len(shapes),
        cost_estimate=pl.CostEstimate(flops=0, bytes_accessed=0, transcendentals=0),
        name="unwritten",
    )()


def conv_silu(buffer, cache_ref, values, weight_ref):
    length = values.shape[0]
    taps = weight_ref.shape[-2]
    buffer[0:8, :] = cache_ref[...]
    buffer[8:, :] = values.astype(jnp.float32)
    start = 8 - (taps - 1)
    summed = weight_ref[0:1, :] * buffer[start : start + length, :]
    for tap in range(1, taps):
        at = start + tap
        summed = summed + weight_ref[tap : tap + 1, :] * buffer[at : at + length, :]
    return jax.nn.silu(summed).astype(jnp.bfloat16)


def inner_kernel(
    heads,
    x_ref,
    x_cache_ref,
    x_weight_ref,
    maps_ref,
    maps_cache_ref,
    maps_weight_ref,
    decay_row_ref,
    decay_col_ref,
    delta_row_ref,
    tail_ref,
    skip_ref,
    partial_ref,
    update_ref,
    output_map_ref,
    x_buffer,
    maps_buffer,
    x_values,
    scaled,
):
    length, width = x_ref.shape
    head_dim = width // heads
    state = maps_ref.shape[1] // 2
    x_values[...] = conv_silu(x_buffer, x_cache_ref, x_ref[...], x_weight_ref)
    maps = conv_silu(maps_buffer, maps_cache_ref, maps_ref[...], maps_weight_ref)
    input_map, output_map = maps[:, :state], maps[:, state:]
    output_map_ref[...] = output_map
    intersection = lax.dot_general(
        output_map, input_map, HIDDEN, preferred_element_type=jnp.float32
    )
    rows = lax.broadcasted_iota(jnp.int32, (length, length), 0)
    columns = lax.broadcasted_iota(jnp.int32, (length, length), 1)
    causal = rows >= columns
    for h in range(heads):
        lanes = slice(h * head_dim, (h + 1) * head_dim)
        gap = decay_col_ref[:, h : h + 1] - decay_row_ref[h : h + 1, :]
        decays = jnp.where(causal, jnp.exp(jnp.where(causal, gap, 0.0)), 0.0)
        mixing = (intersection * decays * delta_row_ref[h : h + 1, :]).astype(jnp.bfloat16)
        x_head = x_values[:, lanes]
        x_wide = x_head.astype(jnp.float32)
        within = jnp.dot(mixing, x_head, preferred_element_type=jnp.float32)
        partial_ref[:, lanes] = within + skip_ref[:, lanes] * x_wide
        scaled[:, lanes] = (x_wide * tail_ref[:, h : h + 1]).astype(jnp.bfloat16)
    update_ref[...] = lax.dot_general(
        scaled[...], input_map, (((0,), (0,)), ((), ())), preferred_element_type=jnp.float32
    )


def state_kernel(
    me_ref,
    state_place_ref,
    store_place_ref,
    got_ref,
    update_ref,
    partial_ref,
    output_map_ref,
    growth_ref,
    decay_row_ref,
    out_ref,
    send_ref,
    pages,
    finals,
    prior,
    arrival,
    departure,
    counts,
    in_sems,
    out_sems,
):
    request, group = pl.program_id(0), pl.program_id(1)
    page_count, heads, page_rows, state = pages.shape
    entries = REQUESTS_PER_IDX * page_count
    slots = got_ref.shape[0]
    peers = counts.shape[0]
    capacity = entries // peers
    head_dim = page_count * page_rows

    @pl.when((request == 0) & (group == 0))
    def _():
        for place_ref, found in ((state_place_ref, arrival), (store_place_ref, departure)):
            for peer in range(peers):
                counts[peer] = 0

            def row_step(offset, carry, place_ref=place_ref, found=found):
                for j in range(page_count):
                    owner = place_ref[me_ref[0] * REQUESTS_PER_IDX + offset, j] // slots
                    rank = counts[owner]
                    counts[owner] = rank + 1
                    found[offset * page_count + j] = owner * capacity + rank
                return carry

            lax.fori_loop(0, REQUESTS_PER_IDX, row_step, jnp.int32(0))

    half = pl.ds(group * heads, heads)
    arrivals = [
        pltpu.make_async_copy(
            got_ref.at[arrival[request * page_count + j], half], pages.at[j], in_sems.at[j]
        )
        for j in range(page_count)
    ]
    for copy in arrivals:
        copy.start()
    departures = [
        pltpu.make_async_copy(
            finals.at[j], send_ref.at[departure[request * page_count + j], half], out_sems.at[j]
        )
        for j in range(page_count)
    ]
    last = decay_row_ref.shape[1] - 1
    for j in range(page_count):
        arrivals[j].wait()
        for h in range(heads):
            at = h * head_dim + j * page_rows
            old = pages[j, h].astype(jnp.float32)
            prior[at : at + page_rows, :] = old
            growth = jnp.exp(decay_row_ref[h : h + 1, last : last + 1])
            finals[j, h] = (growth * old + update_ref[at : at + page_rows, :]).astype(jnp.bfloat16)
        departures[j].start()
    carried = lax.dot_general(
        output_map_ref[...],
        prior[...].astype(jnp.bfloat16),
        HIDDEN,
        preferred_element_type=jnp.float32,
    )
    for h in range(heads):
        lanes = slice(h * head_dim, (h + 1) * head_dim)
        out_ref[:, lanes] = (
            partial_ref[:, lanes] + growth_ref[:, h : h + 1] * carried[:, lanes]
        ).astype(jnp.bfloat16)
    for copy in departures:
        copy.wait()


def attend_kernel(
    scale,
    counts,
    limits_ref,
    place_ref,
    prefix_ref,
    pool_ref,
    *rest,
):
    gots = rest[: len(counts) + 1]
    query_ref, fresh_ref, out_ref = rest[len(counts) + 1 : len(counts) + 4]
    cached_kv, row_max, row_total, attended, kinds, indices, ranks, sems = rest[len(counts) + 4 :]
    request, kv_head = pl.program_id(0), pl.program_id(1)
    per_kv, length, head_dim = query_ref.shape
    slots, page = pool_ref.shape[0], pool_ref.shape[2]
    page_count = place_ref.shape[1]
    peers = ranks.shape[0]
    me, limit, choice = limits_ref[0], limits_ref[1], limits_ref[2]
    first = counts[0]
    passed_kind = len(counts)
    chunk = length
    start_row = me * REQUESTS_PER_IDX

    @pl.when((request == 0) & (kv_head == 0))
    def _():
        cached_kv[...] = jnp.zeros_like(cached_kv)
        for peer in range(peers):
            ranks[peer] = 0

        def count_row(offset, carry):
            tokens = prefix_ref[start_row + offset]
            for j in range(page_count):
                owner = place_ref[start_row + offset, j] // slots
                ranks[owner] = ranks[owner] + jnp.where(j * page < tokens, 1, 0)
            return carry

        lax.fori_loop(0, REQUESTS_PER_IDX, count_row, jnp.int32(0))
        begin = jnp.int32(0)
        for peer in range(peers):
            extra = jnp.where(peer == me, 0, jnp.maximum(ranks[peer] - limit, 0))
            ranks[peer] = begin * 1024
            begin = begin + extra

        def place_row(offset, carry):
            tokens = prefix_ref[start_row + offset]
            for j in range(page_count):
                place = place_ref[start_row + offset, j]
                owner = place // slots
                state = ranks[owner]
                begin, rank = state // 1024, state % 1024
                ranks[owner] = state + jnp.where(j * page < tokens, 1, 0)
                more = jnp.int32(1)
                for option in range(1, len(counts)):
                    more = jnp.where(choice == option, counts[option] - first, more)
                kind = jnp.where(rank < first, 0, choice)
                index = jnp.where(
                    rank < first, owner * first + rank, owner * more + rank - first
                )
                index = jnp.where(rank < limit, index, begin + rank - limit)
                kind = jnp.where(rank < limit, kind, passed_kind)
                entry = offset * page_count + j
                kinds[entry] = jnp.where(owner == me, passed_kind + 1, kind)
                indices[entry] = jnp.where(owner == me, place - me * slots, index)
            return carry

        lax.fori_loop(0, REQUESTS_PER_IDX, place_row, jnp.int32(0))

    tokens = prefix_ref[start_row + request]
    used_pages = (tokens + page - 1) // page

    def target(j):
        return cached_kv.at[pl.ds(pl.multiple_of(j * page, page), page)]

    def start_copy(j, carry):
        entry = request * page_count + j
        for kind, source in enumerate(gots + (pool_ref,)):

            @pl.when(kinds[entry] == kind)
            def _(source=source):
                pltpu.make_async_copy(
                    source.at[indices[entry], kv_head], target(j), sems.at[j]
                ).start()

        return carry

    lax.fori_loop(0, used_pages, start_copy, jnp.int32(0))

    rows = per_kv * length
    query = query_ref[...].reshape(rows, head_dim)
    row = lax.broadcasted_iota(jnp.int32, (per_kv, length, length), 1).reshape(rows, length)
    column = lax.broadcasted_iota(jnp.int32, (rows, length), 1)
    scores = (
        lax.dot_general(query, fresh_ref[:, :head_dim], HIDDEN, preferred_element_type=jnp.float32)
        * scale
    )
    scores = jnp.where(column <= row, scores, -jnp.inf)
    top = jnp.max(scores, axis=-1, keepdims=True)
    exponent = jnp.exp(scores - top)
    row_max[...] = top
    row_total[...] = jnp.sum(exponent, axis=-1, keepdims=True)
    attended[...] = jnp.dot(
        exponent.astype(jnp.bfloat16), fresh_ref[:, head_dim:], preferred_element_type=jnp.float32
    )

    def wait_copy(j, carry):
        pltpu.make_async_copy(pool_ref.at[0, kv_head], target(j), sems.at[j]).wait()
        return carry

    lax.fori_loop(0, used_pages, wait_copy, jnp.int32(0))

    def chunk_step(step, carry):
        start = pl.multiple_of(step * chunk, chunk)
        keys = cached_kv[pl.ds(start, chunk), :head_dim]
        values = cached_kv[pl.ds(start, chunk), head_dim:]
        scores = (
            lax.dot_general(query, keys, HIDDEN, preferred_element_type=jnp.float32) * scale
        )
        scores = jnp.where(column < tokens - start, scores, -jnp.inf)
        old = row_max[...]
        top = jnp.maximum(old, jnp.max(scores, axis=-1, keepdims=True))
        fade = jnp.exp(old - top)
        exponent = jnp.exp(scores - top)
        row_max[...] = top
        row_total[...] = row_total[...] * fade + jnp.sum(exponent, axis=-1, keepdims=True)
        attended[...] = attended[...] * fade + jnp.dot(
            exponent.astype(jnp.bfloat16), values, preferred_element_type=jnp.float32
        )
        return carry

    lax.fori_loop(0, (tokens + chunk - 1) // chunk, chunk_step, jnp.int32(0))
    out_ref[...] = (
        (attended[...] / row_total[...]).astype(jnp.bfloat16).reshape(out_ref.shape)
    )


def body(
    mixer_in,
    maps_in,
    delta_raw,
    conv_cache,
    maps_cache,
    conv_weight,
    maps_weight,
    decay_log,
    skip_gain,
    state_pool,
    queries,
    suffix_keyvals,
    page_pool,
    prefix_tokens,
    page_place,
    state_place,
    store_place,
):
    peers = lax.axis_size("req")
    me = lax.axis_index("req").astype(jnp.int32).reshape(1)
    requests, length = REQUESTS_PER_IDX, APPENDED_LENGTH
    groups = maps_in.shape[1]
    state = maps_in.shape[2] // 2
    heads = delta_raw.shape[1]
    per_group = heads // groups
    width = mixer_in.shape[1]
    group_width = width // groups
    head_dim = width // heads
    slots, _, page_rows, _ = state_pool.shape
    page_count = state_place.shape[1]
    kv_heads = page_pool.shape[2]
    attend_dim = queries.shape[2]
    per_kv = queries.shape[1] // kv_heads
    page = page_pool.shape[1]
    prefix_pages = page_place.shape[1]
    page_slots = page_pool.shape[0]
    pair_pages = requests * prefix_pages // peers
    taps = conv_weight.shape[0]

    def exchange(pages):
        return lax.all_to_all(pages, "req", split_axis=0, concat_axis=0, tiled=True)

    state_send = route_pages(gather_kernel, "gather_states", me, state_place, state_pool)
    state_got = exchange(state_send)

    counts = tuple(sorted({max(1, pair_pages * share // 16) for share in SHARES}))
    used = jnp.arange(prefix_pages)[None, :] * page < prefix_tokens[:, None]
    holders = page_place // page_slots
    pairs = used[:, :, None] & (holders[:, :, None] == jnp.arange(peers)[None, None, :])
    needs = jnp.sum(pairs.reshape(peers, -1, peers).astype(jnp.int32), axis=1)
    places = jnp.arange(peers)
    both = needs + needs[places ^ 1]
    outside = (places[:, None] // 2 != places[None, :] // 2).astype(jnp.int32)
    elsewhere = (places[:, None] != places[None, :]).astype(jnp.int32)
    limit_table = jnp.array(counts, jnp.int32)
    crowded = jnp.max(both * outside) > 2 * limit_table
    rests = jnp.maximum(needs[None] - limit_table[:, None, None], 0) * elsewhere[None]
    crowded = crowded | (jnp.max(jnp.sum(rests, axis=2), axis=1) > PASSED)
    choice = jnp.sum(crowded.astype(jnp.int32))
    limits = jnp.stack([me[0], limit_table[choice], choice])
    pages_by_head = page_pool.transpose(0, 2, 1, 3)
    page_sends = send_used(counts, limits, page_place, prefix_tokens, pages_by_head)

    delta = jax.nn.softplus(delta_raw.T.astype(jnp.float32)).reshape(heads, requests, length)
    log_decay = jnp.cumsum(-delta * jnp.exp(decay_log)[:, None, None], axis=2)
    tail = jnp.exp(log_decay[:, :, -1:] - log_decay) * delta
    growth = jnp.exp(log_decay)

    def by_rows(values):
        return values.reshape(groups, per_group, requests, length).transpose(2, 0, 1, 3)

    def by_columns(values):
        return values.reshape(groups, per_group, requests, length).transpose(2, 0, 3, 1)

    decay_row = by_rows(log_decay)
    maps_split = maps_in.transpose(1, 0, 2)
    empty = 8 - (taps - 1)
    x_cache = jnp.pad(conv_cache.astype(jnp.float32), ((0, 0), (empty, 0), (0, 0)))
    maps_edge = jnp.pad(
        maps_cache.transpose(0, 2, 1, 3).astype(jnp.float32), ((0, 0), (0, 0), (empty, 0), (0, 0))
    )
    row_block = pl.BlockSpec((None, None, per_group, length), lambda r, g: (r, g, 0, 0))
    column_block = pl.BlockSpec((None, None, length, per_group), lambda r, g: (r, g, 0, 0))
    x_block = pl.BlockSpec((length, group_width), lambda r, g: (r, g))
    update_block = pl.BlockSpec((None, None, group_width, state), lambda r, g: (r, g, 0, 0))
    map_block = pl.BlockSpec((None, length, state), lambda r, g: (g, r, 0))
    partial, update, output_map = pl.pallas_call(
        functools.partial(inner_kernel, per_group),
        grid=(requests, groups),
        in_specs=[
            x_block,
            pl.BlockSpec((None, 8, group_width), lambda r, g: (r, 0, g)),
            pl.BlockSpec((taps, group_width), lambda r, g: (0, g)),
            pl.BlockSpec((None, length, 2 * state), lambda r, g: (g, r, 0)),
            pl.BlockSpec((None, None, 8, 2 * state), lambda r, g: (r, g, 0, 0)),
            pl.BlockSpec((None, taps, 2 * state), lambda r, g: (g, 0, 0)),
            row_block,
            column_block,
            row_block,
            column_block,
            pl.BlockSpec((1, group_width), lambda r, g: (0, g)),
        ],
        out_specs=[x_block, update_block, map_block],
        out_shape=[
            jax.ShapeDtypeStruct((requests * length, width), jnp.float32),
            jax.ShapeDtypeStruct((requests, groups, group_width, state), jnp.float32),
            jax.ShapeDtypeStruct((groups, requests * length, state), jnp.bfloat16),
        ],
        scratch_shapes=[
            pltpu.VMEM((8 + length, group_width), jnp.float32),
            pltpu.VMEM((8 + length, 2 * state), jnp.float32),
            pltpu.VMEM((length, group_width), jnp.bfloat16),
            pltpu.VMEM((length, group_width), jnp.bfloat16),
        ],
        cost_estimate=pl.CostEstimate(
            flops=3 * requests * length * width * state,
            bytes_accessed=32 * 2**20,
            transcendentals=requests * heads * length * length,
        ),
        compiler_params=params(),
        name="mix_new_tokens",
    )(
        mixer_in,
        x_cache,
        conv_weight.astype(jnp.float32),
        maps_split,
        maps_edge,
        maps_weight.transpose(1, 0, 2).astype(jnp.float32),
        decay_row,
        by_columns(log_decay),
        by_rows(delta),
        by_columns(tail),
        jnp.repeat(skip_gain, head_dim).reshape(1, width),
    )
    growth_col = by_columns(growth)
    grouped_queries = queries.reshape(requests, length, kv_heads, per_kv, attend_dim).transpose(
        0, 2, 3, 1, 4
    )
    fresh = suffix_keyvals.transpose(1, 0, 2)

    first_got = exchange(page_sends[0])
    more_sends = lax.optimization_barrier((first_got, page_sends[1:]))[1]
    more_shapes = [pltpu.HBM(sent.shape, sent.dtype) for sent in more_sends]

    def no_more(sends):
        return tuple(unwritten(more_shapes))

    def send_more(at, sends):
        gots = list(unwritten(more_shapes[:at] + more_shapes[at + 1 :]))
        return tuple(gots[:at] + [exchange(sends[at])] + gots[at:])

    more_gots = lax.switch(
        choice,
        [no_more] + [functools.partial(send_more, at) for at in range(len(more_shapes))],
        more_sends,
    )
    page_gots = (first_got,) + tuple(more_gots)
    mixer_out, final_send = pl.pallas_call(
        state_kernel,
        grid_spec=pltpu.PrefetchScalarGridSpec(
            num_scalar_prefetch=3,
            grid=(requests, groups),
            in_specs=[
                any_spec(),
                pl.BlockSpec((None, None, group_width, state), lambda r, g, *_: (r, g, 0, 0)),
                pl.BlockSpec((length, group_width), lambda r, g, *_: (r, g)),
                pl.BlockSpec((None, length, state), lambda r, g, *_: (g, r, 0)),
                pl.BlockSpec((None, None, length, per_group), lambda r, g, *_: (r, g, 0, 0)),
                pl.BlockSpec((None, None, per_group, length), lambda r, g, *_: (r, g, 0, 0)),
            ],
            out_specs=[
                pl.BlockSpec((length, group_width), lambda r, g, *_: (r, g)),
                hbm_spec(),
            ],
            scratch_shapes=[
                pltpu.VMEM((page_count, per_group, page_rows, state), jnp.bfloat16),
                pltpu.VMEM((page_count, per_group, page_rows, state), jnp.bfloat16),
                pltpu.VMEM((group_width, state), jnp.float32),
                pltpu.SMEM((requests * page_count,), jnp.int32),
                pltpu.SMEM((requests * page_count,), jnp.int32),
                pltpu.SMEM((peers,), jnp.int32),
                pltpu.SemaphoreType.DMA((page_count,)),
                pltpu.SemaphoreType.DMA((page_count,)),
            ],
        ),
        out_shape=[
            jax.ShapeDtypeStruct((requests * length, width), jnp.bfloat16),
            pltpu.HBM(state_pool.shape, jnp.bfloat16),
        ],
        cost_estimate=pl.CostEstimate(
            flops=2 * requests * length * width * state,
            bytes_accessed=32 * 2**20,
            transcendentals=0,
        ),
        compiler_params=params(),
        name="advance_states",
    )(
        me,
        state_place,
        store_place,
        state_got,
        update,
        partial,
        output_map,
        growth_col,
        decay_row,
    )
    final_got = exchange(final_send)
    passed = pass_on(counts, limits, page_place, prefix_tokens, pages_by_head, page_gots)
    head_block = pl.BlockSpec(
        (None, None, per_kv, length, attend_dim), lambda r, e, *_: (r, e, 0, 0, 0)
    )
    attended = pl.pallas_call(
        functools.partial(attend_kernel, attend_dim**-0.5, counts),
        grid_spec=pltpu.PrefetchScalarGridSpec(
            num_scalar_prefetch=3,
            grid=(requests, kv_heads),
            in_specs=[any_spec()] * (len(page_gots) + 2)
            + [
                head_block,
                pl.BlockSpec((None, length, 2 * attend_dim), lambda r, e, *_: (e, r, 0)),
            ],
            out_specs=head_block,
            scratch_shapes=[
                pltpu.VMEM((prefix_pages * page, 2 * attend_dim), jnp.bfloat16),
                pltpu.VMEM((per_kv * length, 1), jnp.float32),
                pltpu.VMEM((per_kv * length, 1), jnp.float32),
                pltpu.VMEM((per_kv * length, attend_dim), jnp.float32),
                pltpu.SMEM((requests * prefix_pages,), jnp.int32),
                pltpu.SMEM((requests * prefix_pages,), jnp.int32),
                pltpu.SMEM((peers,), jnp.int32),
                pltpu.SemaphoreType.DMA((prefix_pages,)),
            ],
        ),
        out_shape=jax.ShapeDtypeStruct(grouped_queries.shape, jnp.bfloat16),
        cost_estimate=pl.CostEstimate(
            flops=4 * queries.size * (prefix_pages * page + length),
            bytes_accessed=16 * 2**20,
            transcendentals=queries.shape[0] * queries.shape[1] * (prefix_pages * page),
        ),
        compiler_params=params(),
        name="attend",
    )(
        limits,
        page_place,
        prefix_tokens,
        pages_by_head,
        *page_gots,
        passed,
        grouped_queries,
        fresh,
    )
    attention_out = attended.transpose(0, 3, 1, 2, 4).reshape(queries.shape)
    stored = route_pages(scatter_kernel, "scatter_states", me, store_place, final_got)
    return mixer_out, attention_out, stored


def solution(mesh):
    placed = (
        P(("parts", "req"), "tp"),
        P(("parts", "req"), "tp", None),
        P(("parts", "req"), "tp"),
        P(("parts", "req"), None, "tp"),
        P(("parts", "req"), None, "tp", None),
        P(None, "tp"),
        P(None, "tp", None),
        P("tp"),
        P("tp"),
        P(("parts", "req"), "tp", None, None),
        P(("parts", "req"), "tp", None),
        P(("parts", "req"), "tp", None),
        P(("parts", "req"), None, "tp", None),
        P("parts"),
        P("parts", None),
        P("parts", None),
        P("parts", None),
    )
    return jax.shard_map(
        body,
        mesh=mesh,
        in_specs=placed,
        out_specs=(
            P(("parts", "req"), "tp"),
            P(("parts", "req"), "tp", None),
            P(("parts", "req"), "tp", None, None),
        ),
        check_vma=False,
    )
```

```python
import functools

import jax
import jax.numpy as jnp
from jax import lax
from jax.experimental import pallas as pl
from jax.experimental.pallas import tpu as pltpu
from jax.sharding import PartitionSpec as P

APPENDED_LENGTH = 256
REQUESTS_PER_IDX = 4
VMEM_LIMIT = 48 * 1024 * 1024
SHARES = (9, 10, 11, 12, 13, 16)
HIDDEN = (((1,), (1,)), ((), ()))


def params():
    return pltpu.CompilerParams(vmem_limit_bytes=VMEM_LIMIT)


def any_spec():
    return pl.BlockSpec(memory_space=pl.ANY)


def hbm_spec():
    return pl.BlockSpec(memory_space=pltpu.HBM)


def own_entries(place_ref, base, slots, position, row, emit):
    for j in range(place_ref.shape[1]):
        slot = place_ref[row, j] - base
        mine = (slot >= 0) & (slot < slots)

        @pl.when(mine)
        def _(slot=slot, position=position, j=j):
            emit(position, slot)

        position = position + jnp.where(mine, 1, 0)
    return position


def gather_kernel(capacity, me_ref, place_ref, pool_ref, out_ref, staged, in_sems, out_sems):
    slots = pool_ref.shape[0]
    base = me_ref[0] * slots
    servers = place_ref.shape[0] // REQUESTS_PER_IDX

    def server_step(server, carry):
        def row_step(offset, position):
            def emit(at, slot):
                pltpu.make_async_copy(
                    pool_ref.at[slot], staged.at[server * capacity + at], in_sems.at[server]
                ).start()

            row = server * REQUESTS_PER_IDX + offset
            return own_entries(place_ref, base, slots, position, row, emit)

        lax.fori_loop(0, REQUESTS_PER_IDX, row_step, jnp.int32(0))
        return carry

    lax.fori_loop(0, servers, server_step, jnp.int32(0))

    def part(server):
        return pl.ds(pl.multiple_of(server * capacity, capacity), capacity)

    def forward(server, carry):
        pltpu.make_async_copy(
            pool_ref.at[part(0)], staged.at[part(server)], in_sems.at[server]
        ).wait()
        pltpu.make_async_copy(
            staged.at[part(server)], out_ref.at[part(server)], out_sems.at[server]
        ).start()
        return carry

    lax.fori_loop(0, servers, forward, jnp.int32(0))

    def finish(server, carry):
        pltpu.make_async_copy(
            staged.at[part(server)], out_ref.at[part(server)], out_sems.at[server]
        ).wait()
        return carry

    lax.fori_loop(0, servers, finish, jnp.int32(0))


def scatter_kernel(capacity, me_ref, place_ref, got_ref, out_ref, staged, in_sems, out_sems):
    slots = out_ref.shape[0]
    base = me_ref[0] * slots
    servers = place_ref.shape[0] // REQUESTS_PER_IDX

    def fetch(server):
        part = pl.ds(pl.multiple_of(server * capacity, capacity), capacity)
        return pltpu.make_async_copy(got_ref.at[part], staged.at[part], in_sems.at[server])

    def start_fetch(server, carry):
        fetch(server).start()
        return carry

    lax.fori_loop(0, servers, start_fetch, jnp.int32(0))

    def server_step(server, carry):
        fetch(server).wait()

        def row_step(offset, position):
            def emit(at, slot):
                pltpu.make_async_copy(
                    staged.at[server * capacity + at], out_ref.at[slot], out_sems.at[0]
                ).start()

            row = server * REQUESTS_PER_IDX + offset
            return own_entries(place_ref, base, slots, position, row, emit)

        lax.fori_loop(0, REQUESTS_PER_IDX, row_step, jnp.int32(0))
        return carry

    lax.fori_loop(0, servers, server_step, jnp.int32(0))
    pltpu.make_async_copy(staged, out_ref, out_sems.at[0]).wait()


def route_pages(kernel, name, me, place, pages):
    servers = lax.axis_size("req")
    capacity = pages.shape[0] // servers
    size = pages.size * pages.dtype.itemsize
    return pl.pallas_call(
        functools.partial(kernel, capacity),
        out_shape=pltpu.HBM(pages.shape, pages.dtype),
        grid_spec=pltpu.PrefetchScalarGridSpec(
            num_scalar_prefetch=2,
            grid=(1,),
            in_specs=[hbm_spec()],
            out_specs=hbm_spec(),
            scratch_shapes=[
                pltpu.VMEM(pages.shape, pages.dtype),
                pltpu.SemaphoreType.DMA((servers,)),
                pltpu.SemaphoreType.DMA((servers,)),
            ],
        ),
        cost_estimate=pl.CostEstimate(flops=0, bytes_accessed=2 * size, transcendentals=0),
        compiler_params=params(),
        name=name,
    )(me, place, pltpu.with_memory_space_constraint(pages, pltpu.HBM))


def send_kernel(counts, limits_ref, place_ref, prefix_ref, pool_ref, *rest):
    outs, (staged, filled, in_sems, out_sems) = rest[: len(counts)], rest[len(counts) :]
    slots, page = pool_ref.shape[0], pool_ref.shape[2]
    me, choice = limits_ref[0], limits_ref[1]
    columns = place_ref.shape[1]
    servers, room = staged.shape[:2]
    first = counts[0]

    def fetch(slot, server, position):
        return pltpu.make_async_copy(
            pool_ref.at[slot], staged.at[server, position], in_sems.at[server, position]
        )

    def fetch_server(server, carry):
        def fetch_row(offset, position):
            row = server * REQUESTS_PER_IDX + offset
            for j in range(columns):
                slot = place_ref[row, j] - me * slots
                wanted = (slot >= 0) & (slot < slots) & (j * page < prefix_ref[row])
                wanted = wanted & (server != me)

                @pl.when(wanted)
                def _(slot=slot, position=position):
                    fetch(slot, server, position).start()

                position = position + jnp.where(wanted, 1, 0)
            return position

        filled[server] = lax.fori_loop(0, REQUESTS_PER_IDX, fetch_row, jnp.int32(0))
        return carry

    lax.fori_loop(0, servers, fetch_server, jnp.int32(0))

    def forward(server, option):
        size = first if option == 0 else counts[option] - first
        begin = 0 if option == 0 else first
        return pltpu.make_async_copy(
            staged.at[server, pl.ds(begin, size)],
            outs[option].at[pl.ds(server * size, size)],
            out_sems.at[server, min(option, 1)],
        )

    def forward_server(server, carry):
        for position in range(room):

            @pl.when(position < filled[server])
            def _(position=position):
                fetch(0, server, position).wait()

        forward(server, 0).start()
        for option in range(1, len(counts)):

            @pl.when(choice == option)
            def _(option=option):
                forward(server, option).start()

        return carry

    lax.fori_loop(0, servers, forward_server, jnp.int32(0))

    def finish_server(server, carry):
        forward(server, 0).wait()
        for option in range(1, len(counts)):

            @pl.when(choice == option)
            def _(option=option):
                forward(server, option).wait()

        return carry

    lax.fori_loop(0, servers, finish_server, jnp.int32(0))


def send_used(counts, limits, place, prefix, pages):
    servers = lax.axis_size("req")
    sizes = [counts[0]] + [count - counts[0] for count in counts[1:]]
    shapes = [
        pltpu.HBM((servers * size,) + pages.shape[1:], pages.dtype) for size in sizes
    ]
    return pl.pallas_call(
        functools.partial(send_kernel, counts),
        out_shape=shapes,
        grid_spec=pltpu.PrefetchScalarGridSpec(
            num_scalar_prefetch=3,
            grid=(1,),
            in_specs=[any_spec()],
            out_specs=[hbm_spec()] * len(counts),
            scratch_shapes=[
                pltpu.VMEM((servers, counts[-1]) + pages.shape[1:], pages.dtype),
                pltpu.SMEM((servers,), jnp.int32),
                pltpu.SemaphoreType.DMA((servers, counts[-1])),
                pltpu.SemaphoreType.DMA((servers, 2)),
            ],
        ),
        cost_estimate=pl.CostEstimate(
            flops=0, bytes_accessed=2 * pages.size * 2, transcendentals=0
        ),
        compiler_params=params(),
        name="send_used_pages",
    )(limits, place, prefix, pages)


def unwritten(shapes):
    return pl.pallas_call(
        lambda *refs: None,
        out_shape=shapes,
        out_specs=[hbm_spec()] * len(shapes),
        cost_estimate=pl.CostEstimate(flops=0, bytes_accessed=0, transcendentals=0),
        name="unwritten",
    )()


def conv_silu(buffer, cache_ref, values, weight_ref):
    length = values.shape[0]
    taps = weight_ref.shape[-2]
    buffer[0:8, :] = cache_ref[...]
    buffer[8:, :] = values.astype(jnp.float32)
    start = 8 - (taps - 1)
    summed = weight_ref[0:1, :] * buffer[start : start + length, :]
    for tap in range(1, taps):
        at = start + tap
        summed = summed + weight_ref[tap : tap + 1, :] * buffer[at : at + length, :]
    return jax.nn.silu(summed).astype(jnp.bfloat16)


def inner_kernel(
    heads,
    x_ref,
    x_cache_ref,
    x_weight_ref,
    maps_ref,
    maps_cache_ref,
    maps_weight_ref,
    decay_row_ref,
    decay_col_ref,
    delta_row_ref,
    tail_ref,
    skip_ref,
    partial_ref,
    update_ref,
    output_map_ref,
    x_buffer,
    maps_buffer,
    x_values,
    scaled,
):
    length, width = x_ref.shape
    head_dim = width // heads
    state = maps_ref.shape[1] // 2
    x_values[...] = conv_silu(x_buffer, x_cache_ref, x_ref[...], x_weight_ref)
    maps = conv_silu(maps_buffer, maps_cache_ref, maps_ref[...], maps_weight_ref)
    input_map, output_map = maps[:, :state], maps[:, state:]
    output_map_ref[...] = output_map
    intersection = lax.dot_general(
        output_map, input_map, HIDDEN, preferred_element_type=jnp.float32
    )
    rows = lax.broadcasted_iota(jnp.int32, (length, length), 0)
    columns = lax.broadcasted_iota(jnp.int32, (length, length), 1)
    causal = rows >= columns
    for h in range(heads):
        lanes = slice(h * head_dim, (h + 1) * head_dim)
        gap = decay_col_ref[:, h : h + 1] - decay_row_ref[h : h + 1, :]
        decays = jnp.where(causal, jnp.exp(jnp.where(causal, gap, 0.0)), 0.0)
        mixing = (intersection * decays * delta_row_ref[h : h + 1, :]).astype(jnp.bfloat16)
        x_head = x_values[:, lanes]
        x_wide = x_head.astype(jnp.float32)
        within = jnp.dot(mixing, x_head, preferred_element_type=jnp.float32)
        partial_ref[:, lanes] = within + skip_ref[:, lanes] * x_wide
        scaled[:, lanes] = (x_wide * tail_ref[:, h : h + 1]).astype(jnp.bfloat16)
    update_ref[...] = lax.dot_general(
        scaled[...], input_map, (((0,), (0,)), ((), ())), preferred_element_type=jnp.float32
    )


def state_kernel(
    me_ref,
    state_place_ref,
    store_place_ref,
    got_ref,
    update_ref,
    partial_ref,
    output_map_ref,
    growth_ref,
    decay_row_ref,
    out_ref,
    send_ref,
    pages,
    finals,
    prior,
    arrival,
    departure,
    counts,
    in_sems,
    out_sems,
):
    request, group = pl.program_id(0), pl.program_id(1)
    page_count, heads, page_rows, state = pages.shape
    entries = REQUESTS_PER_IDX * page_count
    slots = got_ref.shape[0]
    peers = counts.shape[0]
    capacity = entries // peers
    head_dim = page_count * page_rows

    @pl.when((request == 0) & (group == 0))
    def _():
        for place_ref, found in ((state_place_ref, arrival), (store_place_ref, departure)):
            for peer in range(peers):
                counts[peer] = 0

            def row_step(offset, carry, place_ref=place_ref, found=found):
                for j in range(page_count):
                    owner = place_ref[me_ref[0] * REQUESTS_PER_IDX + offset, j] // slots
                    rank = counts[owner]
                    counts[owner] = rank + 1
                    found[offset * page_count + j] = owner * capacity + rank
                return carry

            lax.fori_loop(0, REQUESTS_PER_IDX, row_step, jnp.int32(0))

    half = pl.ds(group * heads, heads)
    arrivals = [
        pltpu.make_async_copy(
            got_ref.at[arrival[request * page_count + j], half], pages.at[j], in_sems.at[j]
        )
        for j in range(page_count)
    ]
    for copy in arrivals:
        copy.start()
    departures = [
        pltpu.make_async_copy(
            finals.at[j], send_ref.at[departure[request * page_count + j], half], out_sems.at[j]
        )
        for j in range(page_count)
    ]
    last = decay_row_ref.shape[1] - 1
    for j in range(page_count):
        arrivals[j].wait()
        for h in range(heads):
            at = h * head_dim + j * page_rows
            old = pages[j, h].astype(jnp.float32)
            prior[at : at + page_rows, :] = old
            growth = jnp.exp(decay_row_ref[h : h + 1, last : last + 1])
            finals[j, h] = (growth * old + update_ref[at : at + page_rows, :]).astype(jnp.bfloat16)
        departures[j].start()
    carried = lax.dot_general(
        output_map_ref[...],
        prior[...].astype(jnp.bfloat16),
        HIDDEN,
        preferred_element_type=jnp.float32,
    )
    for h in range(heads):
        lanes = slice(h * head_dim, (h + 1) * head_dim)
        out_ref[:, lanes] = (
            partial_ref[:, lanes] + growth_ref[:, h : h + 1] * carried[:, lanes]
        ).astype(jnp.bfloat16)
    for copy in departures:
        copy.wait()


def attend_kernel(
    scale,
    counts,
    limits_ref,
    place_ref,
    prefix_ref,
    pool_ref,
    *rest,
):
    gots = rest[: len(counts)]
    query_ref, fresh_ref, out_ref = rest[len(counts) : len(counts) + 3]
    cached_kv, top_ref, total_ref, attended, kinds, indices, ranks, sems = rest[len(counts) + 3 :]
    request, kv_head = pl.program_id(0), pl.program_id(1)
    per_kv, length, head_dim = query_ref.shape
    slots, page = pool_ref.shape[0], pool_ref.shape[2]
    page_count = place_ref.shape[1]
    peers = ranks.shape[0]
    me, choice = limits_ref[0], limits_ref[1]
    first = counts[0]
    chunk = length
    start_row = me * REQUESTS_PER_IDX

    @pl.when((request == 0) & (kv_head == 0))
    def _():
        cached_kv[...] = jnp.zeros_like(cached_kv)
        for peer in range(peers):
            ranks[peer] = 0
        more = jnp.int32(1)
        for option in range(1, len(counts)):
            more = jnp.where(choice == option, counts[option] - first, more)

        def place_row(offset, carry):
            tokens = prefix_ref[start_row + offset]
            for j in range(page_count):
                place = place_ref[start_row + offset, j]
                owner = place // slots
                rank = ranks[owner]
                ranks[owner] = rank + jnp.where(j * page < tokens, 1, 0)
                here = owner == me
                early = rank < first
                index = jnp.where(early, owner * first + rank, owner * more + rank - first)
                entry = offset * page_count + j
                kinds[entry] = jnp.where(here, len(counts), jnp.where(early, 0, choice))
                indices[entry] = jnp.where(here, place - me * slots, index)
            return carry

        lax.fori_loop(0, REQUESTS_PER_IDX, place_row, jnp.int32(0))

    tokens = prefix_ref[start_row + request]
    used_pages = (tokens + page - 1) // page

    def target(j):
        return cached_kv.at[pl.ds(pl.multiple_of(j * page, page), page)]

    def start_copy(j, carry):
        entry = request * page_count + j
        for kind, source in enumerate(gots + (pool_ref,)):

            @pl.when(kinds[entry] == kind)
            def _(source=source):
                pltpu.make_async_copy(
                    source.at[indices[entry], kv_head], target(j), sems.at[j]
                ).start()

        return carry

    lax.fori_loop(0, used_pages, start_copy, jnp.int32(0))

    query = query_ref[...].reshape(per_kv * length, head_dim)
    keys_at = lax.broadcasted_iota(jnp.int32, (length, per_kv * length), 0)

    def score(keys):
        return lax.dot_general(keys, query, HIDDEN, preferred_element_type=jnp.float32) * scale

    def weigh(values, exponent):
        return lax.dot_general(
            values,
            exponent.astype(jnp.bfloat16),
            (((0,), (0,)), ((), ())),
            preferred_element_type=jnp.float32,
        )

    queries_at = lax.broadcasted_iota(jnp.int32, (length, per_kv * length), 1) % length
    scores = jnp.where(keys_at <= queries_at, score(fresh_ref[:, :head_dim]), -jnp.inf)
    top = jnp.max(scores, axis=0, keepdims=True)
    exponent = jnp.exp(scores - top)
    top_ref[...] = top
    total_ref[...] = jnp.sum(exponent, axis=0, keepdims=True)
    attended[...] = weigh(fresh_ref[:, head_dim:], exponent)

    def wait_copy(j, carry):
        pltpu.make_async_copy(pool_ref.at[0, kv_head], target(j), sems.at[j]).wait()
        return carry

    lax.fori_loop(0, used_pages, wait_copy, jnp.int32(0))

    def chunk_step(step, carry):
        start = pl.multiple_of(step * chunk, chunk)
        scores = score(cached_kv[pl.ds(start, chunk), :head_dim])
        scores = jnp.where(keys_at < tokens - start, scores, -jnp.inf)
        old = top_ref[...]
        top = jnp.maximum(old, jnp.max(scores, axis=0, keepdims=True))
        fade = jnp.exp(old - top)
        exponent = jnp.exp(scores - top)
        top_ref[...] = top
        total_ref[...] = total_ref[...] * fade + jnp.sum(exponent, axis=0, keepdims=True)
        attended[...] = attended[...] * fade + weigh(
            cached_kv[pl.ds(start, chunk), head_dim:], exponent
        )
        return carry

    lax.fori_loop(0, (tokens + chunk - 1) // chunk, chunk_step, jnp.int32(0))
    out_ref[...] = (
        (attended[...] / total_ref[...]).T.astype(jnp.bfloat16).reshape(out_ref.shape)
    )


def body(
    mixer_in,
    maps_in,
    delta_raw,
    conv_cache,
    maps_cache,
    conv_weight,
    maps_weight,
    decay_log,
    skip_gain,
    state_pool,
    queries,
    suffix_keyvals,
    page_pool,
    prefix_tokens,
    page_place,
    state_place,
    store_place,
):
    peers = lax.axis_size("req")
    me = lax.axis_index("req").astype(jnp.int32).reshape(1)
    requests, length = REQUESTS_PER_IDX, APPENDED_LENGTH
    groups = maps_in.shape[1]
    state = maps_in.shape[2] // 2
    heads = delta_raw.shape[1]
    per_group = heads // groups
    width = mixer_in.shape[1]
    group_width = width // groups
    head_dim = width // heads
    slots, _, page_rows, _ = state_pool.shape
    page_count = state_place.shape[1]
    kv_heads = page_pool.shape[2]
    attend_dim = queries.shape[2]
    per_kv = queries.shape[1] // kv_heads
    page = page_pool.shape[1]
    prefix_pages = page_place.shape[1]
    page_slots = page_pool.shape[0]
    pair_pages = requests * prefix_pages // peers
    taps = conv_weight.shape[0]

    def exchange(pages):
        return lax.all_to_all(pages, "req", split_axis=0, concat_axis=0, tiled=True)

    state_send = route_pages(gather_kernel, "gather_states", me, state_place, state_pool)
    state_got = exchange(state_send)

    counts = tuple(sorted({max(1, pair_pages * share // 16) for share in SHARES}))
    used = jnp.arange(prefix_pages)[None, :] * page < prefix_tokens[:, None]
    holders = page_place // page_slots
    pairs = used[:, :, None] & (holders[:, :, None] == jnp.arange(peers)[None, None, :])
    needs = jnp.sum(pairs.reshape(peers, -1, peers).astype(jnp.int32), axis=1)
    elsewhere = jnp.arange(peers)[:, None] != jnp.arange(peers)[None, :]
    needed = jnp.max(jnp.where(elsewhere, needs, 0))
    choice = jnp.sum((needed > jnp.array(counts[:-1], jnp.int32)).astype(jnp.int32))
    limits = jnp.stack([me[0], choice])
    pages_by_head = page_pool.transpose(0, 2, 1, 3)
    page_sends = send_used(counts, limits, page_place, prefix_tokens, pages_by_head)

    delta = jax.nn.softplus(delta_raw.T.astype(jnp.float32)).reshape(heads, requests, length)
    log_decay = jnp.cumsum(-delta * jnp.exp(decay_log)[:, None, None], axis=2)
    tail = jnp.exp(log_decay[:, :, -1:] - log_decay) * delta
    growth = jnp.exp(log_decay)

    def by_rows(values):
        return values.reshape(groups, per_group, requests, length).transpose(2, 0, 1, 3)

    def by_columns(values):
        return values.reshape(groups, per_group, requests, length).transpose(2, 0, 3, 1)

    decay_row = by_rows(log_decay)
    maps_split = maps_in.transpose(1, 0, 2)
    empty = 8 - (taps - 1)
    x_cache = jnp.pad(conv_cache.astype(jnp.float32), ((0, 0), (empty, 0), (0, 0)))
    maps_edge = jnp.pad(
        maps_cache.transpose(0, 2, 1, 3).astype(jnp.float32), ((0, 0), (0, 0), (empty, 0), (0, 0))
    )
    row_block = pl.BlockSpec((None, None, per_group, length), lambda r, g: (r, g, 0, 0))
    column_block = pl.BlockSpec((None, None, length, per_group), lambda r, g: (r, g, 0, 0))
    x_block = pl.BlockSpec((length, group_width), lambda r, g: (r, g))
    update_block = pl.BlockSpec((None, None, group_width, state), lambda r, g: (r, g, 0, 0))
    map_block = pl.BlockSpec((None, length, state), lambda r, g: (g, r, 0))
    partial, update, output_map = pl.pallas_call(
        functools.partial(inner_kernel, per_group),
        grid=(requests, groups),
        in_specs=[
            x_block,
            pl.BlockSpec((None, 8, group_width), lambda r, g: (r, 0, g)),
            pl.BlockSpec((taps, group_width), lambda r, g: (0, g)),
            pl.BlockSpec((None, length, 2 * state), lambda r, g: (g, r, 0)),
            pl.BlockSpec((None, None, 8, 2 * state), lambda r, g: (r, g, 0, 0)),
            pl.BlockSpec((None, taps, 2 * state), lambda r, g: (g, 0, 0)),
            row_block,
            column_block,
            row_block,
            column_block,
            pl.BlockSpec((1, group_width), lambda r, g: (0, g)),
        ],
        out_specs=[x_block, update_block, map_block],
        out_shape=[
            jax.ShapeDtypeStruct((requests * length, width), jnp.float32),
            jax.ShapeDtypeStruct((requests, groups, group_width, state), jnp.float32),
            jax.ShapeDtypeStruct((groups, requests * length, state), jnp.bfloat16),
        ],
        scratch_shapes=[
            pltpu.VMEM((8 + length, group_width), jnp.float32),
            pltpu.VMEM((8 + length, 2 * state), jnp.float32),
            pltpu.VMEM((length, group_width), jnp.bfloat16),
            pltpu.VMEM((length, group_width), jnp.bfloat16),
        ],
        cost_estimate=pl.CostEstimate(
            flops=3 * requests * length * width * state,
            bytes_accessed=32 * 2**20,
            transcendentals=requests * heads * length * length,
        ),
        compiler_params=params(),
        name="mix_new_tokens",
    )(
        mixer_in,
        x_cache,
        conv_weight.astype(jnp.float32),
        maps_split,
        maps_edge,
        maps_weight.transpose(1, 0, 2).astype(jnp.float32),
        decay_row,
        by_columns(log_decay),
        by_rows(delta),
        by_columns(tail),
        jnp.repeat(skip_gain, head_dim).reshape(1, width),
    )
    growth_col = by_columns(growth)
    grouped_queries = queries.reshape(requests, length, kv_heads, per_kv, attend_dim).transpose(
        0, 2, 3, 1, 4
    )
    fresh = suffix_keyvals.transpose(1, 0, 2)

    first_send = lax.optimization_barrier((page_sends[0], state_got))[0]
    first_got = exchange(first_send)
    more_sends = lax.optimization_barrier((first_got, page_sends[1:]))[1]
    more_shapes = [pltpu.HBM(sent.shape, sent.dtype) for sent in more_sends]

    def no_more(sends):
        return tuple(unwritten(more_shapes))

    def send_more(at, sends):
        gots = list(unwritten(more_shapes[:at] + more_shapes[at + 1 :]))
        return tuple(gots[:at] + [exchange(sends[at])] + gots[at:])

    more_gots = lax.switch(
        choice,
        [no_more] + [functools.partial(send_more, at) for at in range(len(more_shapes))],
        more_sends,
    )
    page_gots = (first_got,) + tuple(more_gots)
    mixer_out, final_send = pl.pallas_call(
        state_kernel,
        grid_spec=pltpu.PrefetchScalarGridSpec(
            num_scalar_prefetch=3,
            grid=(requests, groups),
            in_specs=[
                any_spec(),
                pl.BlockSpec((None, None, group_width, state), lambda r, g, *_: (r, g, 0, 0)),
                pl.BlockSpec((length, group_width), lambda r, g, *_: (r, g)),
                pl.BlockSpec((None, length, state), lambda r, g, *_: (g, r, 0)),
                pl.BlockSpec((None, None, length, per_group), lambda r, g, *_: (r, g, 0, 0)),
                pl.BlockSpec((None, None, per_group, length), lambda r, g, *_: (r, g, 0, 0)),
            ],
            out_specs=[
                pl.BlockSpec((length, group_width), lambda r, g, *_: (r, g)),
                hbm_spec(),
            ],
            scratch_shapes=[
                pltpu.VMEM((page_count, per_group, page_rows, state), jnp.bfloat16),
                pltpu.VMEM((page_count, per_group, page_rows, state), jnp.bfloat16),
                pltpu.VMEM((group_width, state), jnp.float32),
                pltpu.SMEM((requests * page_count,), jnp.int32),
                pltpu.SMEM((requests * page_count,), jnp.int32),
                pltpu.SMEM((peers,), jnp.int32),
                pltpu.SemaphoreType.DMA((page_count,)),
                pltpu.SemaphoreType.DMA((page_count,)),
            ],
        ),
        out_shape=[
            jax.ShapeDtypeStruct((requests * length, width), jnp.bfloat16),
            pltpu.HBM(state_pool.shape, jnp.bfloat16),
        ],
        cost_estimate=pl.CostEstimate(
            flops=2 * requests * length * width * state,
            bytes_accessed=32 * 2**20,
            transcendentals=0,
        ),
        compiler_params=params(),
        name="advance_states",
    )(
        me,
        state_place,
        store_place,
        state_got,
        update,
        partial,
        output_map,
        growth_col,
        decay_row,
    )
    final_send, page_gots = lax.optimization_barrier((final_send, page_gots))
    final_got = exchange(final_send)
    head_block = pl.BlockSpec(
        (None, None, per_kv, length, attend_dim), lambda r, e, *_: (r, e, 0, 0, 0)
    )
    attended = pl.pallas_call(
        functools.partial(attend_kernel, attend_dim**-0.5, counts),
        grid_spec=pltpu.PrefetchScalarGridSpec(
            num_scalar_prefetch=3,
            grid=(requests, kv_heads),
            in_specs=[any_spec()] * (len(page_gots) + 1)
            + [
                head_block,
                pl.BlockSpec((None, length, 2 * attend_dim), lambda r, e, *_: (e, r, 0)),
            ],
            out_specs=head_block,
            scratch_shapes=[
                pltpu.VMEM((prefix_pages * page, 2 * attend_dim), jnp.bfloat16),
                pltpu.VMEM((1, per_kv * length), jnp.float32),
                pltpu.VMEM((1, per_kv * length), jnp.float32),
                pltpu.VMEM((attend_dim, per_kv * length), jnp.float32),
                pltpu.SMEM((requests * prefix_pages,), jnp.int32),
                pltpu.SMEM((requests * prefix_pages,), jnp.int32),
                pltpu.SMEM((peers,), jnp.int32),
                pltpu.SemaphoreType.DMA((prefix_pages,)),
            ],
        ),
        out_shape=jax.ShapeDtypeStruct(grouped_queries.shape, jnp.bfloat16),
        cost_estimate=pl.CostEstimate(
            flops=4 * queries.size * (prefix_pages * page + length),
            bytes_accessed=16 * 2**20,
            transcendentals=queries.shape[0] * queries.shape[1] * (prefix_pages * page),
        ),
        compiler_params=params(),
        name="attend",
    )(
        limits,
        page_place,
        prefix_tokens,
        pages_by_head,
        *page_gots,
        grouped_queries,
        fresh,
    )
    attention_out = attended.transpose(0, 3, 1, 2, 4).reshape(queries.shape)
    stored = route_pages(scatter_kernel, "scatter_states", me, store_place, final_got)
    return mixer_out, attention_out, stored


def solution(mesh):
    placed = (
        P(("parts", "req"), "tp"),
        P(("parts", "req"), "tp", None),
        P(("parts", "req"), "tp"),
        P(("parts", "req"), None, "tp"),
        P(("parts", "req"), None, "tp", None),
        P(None, "tp"),
        P(None, "tp", None),
        P("tp"),
        P("tp"),
        P(("parts", "req"), "tp", None, None),
        P(("parts", "req"), "tp", None),
        P(("parts", "req"), "tp", None),
        P(("parts", "req"), None, "tp", None),
        P("parts"),
        P("parts", None),
        P("parts", None),
        P("parts", None),
    )
    return jax.shard_map(
        body,
        mesh=mesh,
        in_specs=placed,
        out_specs=(
            P(("parts", "req"), "tp"),
            P(("parts", "req"), "tp", None),
            P(("parts", "req"), "tp", None, None),
        ),
        check_vma=False,
    )
```

```python
import functools

import jax
import jax.numpy as jnp
from jax import lax
from jax.experimental import pallas as pl
from jax.experimental.pallas import tpu as pltpu
from jax.sharding import PartitionSpec as P

APPENDED_LENGTH = 256
REQUESTS_PER_IDX = 4
VMEM_LIMIT = 48 * 1024 * 1024
SHARES = (9, 10, 11, 12, 13, 16)
HIDDEN = (((1,), (1,)), ((), ()))


def params():
    return pltpu.CompilerParams(vmem_limit_bytes=VMEM_LIMIT)


def any_spec():
    return pl.BlockSpec(memory_space=pl.ANY)


def hbm_spec():
    return pl.BlockSpec(memory_space=pltpu.HBM)


def own_entries(place_ref, base, slots, position, row, emit):
    for j in range(place_ref.shape[1]):
        slot = place_ref[row, j] - base
        mine = (slot >= 0) & (slot < slots)

        @pl.when(mine)
        def _(slot=slot, position=position, j=j):
            emit(position, slot)

        position = position + jnp.where(mine, 1, 0)
    return position


def gather_kernel(capacity, me_ref, place_ref, pool_ref, out_ref, staged, in_sems, out_sems):
    slots = pool_ref.shape[0]
    base = me_ref[0] * slots
    servers = place_ref.shape[0] // REQUESTS_PER_IDX

    def server_step(server, carry):
        def row_step(offset, position):
            def emit(at, slot):
                pltpu.make_async_copy(
                    pool_ref.at[slot], staged.at[server * capacity + at], in_sems.at[server]
                ).start()

            row = server * REQUESTS_PER_IDX + offset
            return own_entries(place_ref, base, slots, position, row, emit)

        lax.fori_loop(0, REQUESTS_PER_IDX, row_step, jnp.int32(0))
        return carry

    lax.fori_loop(0, servers, server_step, jnp.int32(0))

    def part(server):
        return pl.ds(pl.multiple_of(server * capacity, capacity), capacity)

    def forward(server, carry):
        pltpu.make_async_copy(
            pool_ref.at[part(0)], staged.at[part(server)], in_sems.at[server]
        ).wait()
        pltpu.make_async_copy(
            staged.at[part(server)], out_ref.at[part(server)], out_sems.at[server]
        ).start()
        return carry

    lax.fori_loop(0, servers, forward, jnp.int32(0))

    def finish(server, carry):
        pltpu.make_async_copy(
            staged.at[part(server)], out_ref.at[part(server)], out_sems.at[server]
        ).wait()
        return carry

    lax.fori_loop(0, servers, finish, jnp.int32(0))


def scatter_kernel(capacity, me_ref, place_ref, got_ref, out_ref, staged, in_sems, out_sems):
    slots = out_ref.shape[0]
    base = me_ref[0] * slots
    servers = place_ref.shape[0] // REQUESTS_PER_IDX

    def fetch(server):
        part = pl.ds(pl.multiple_of(server * capacity, capacity), capacity)
        return pltpu.make_async_copy(got_ref.at[part], staged.at[part], in_sems.at[server])

    def start_fetch(server, carry):
        fetch(server).start()
        return carry

    lax.fori_loop(0, servers, start_fetch, jnp.int32(0))

    def server_step(server, carry):
        fetch(server).wait()

        def row_step(offset, position):
            def emit(at, slot):
                pltpu.make_async_copy(
                    staged.at[server * capacity + at], out_ref.at[slot], out_sems.at[0]
                ).start()

            row = server * REQUESTS_PER_IDX + offset
            return own_entries(place_ref, base, slots, position, row, emit)

        lax.fori_loop(0, REQUESTS_PER_IDX, row_step, jnp.int32(0))
        return carry

    lax.fori_loop(0, servers, server_step, jnp.int32(0))
    pltpu.make_async_copy(staged, out_ref, out_sems.at[0]).wait()


def route_pages(kernel, name, me, place, pages):
    servers = lax.axis_size("req")
    capacity = pages.shape[0] // servers
    size = pages.size * pages.dtype.itemsize
    return pl.pallas_call(
        functools.partial(kernel, capacity),
        out_shape=pltpu.HBM(pages.shape, pages.dtype),
        grid_spec=pltpu.PrefetchScalarGridSpec(
            num_scalar_prefetch=2,
            grid=(1,),
            in_specs=[hbm_spec()],
            out_specs=hbm_spec(),
            scratch_shapes=[
                pltpu.VMEM(pages.shape, pages.dtype),
                pltpu.SemaphoreType.DMA((servers,)),
                pltpu.SemaphoreType.DMA((servers,)),
            ],
        ),
        cost_estimate=pl.CostEstimate(flops=0, bytes_accessed=2 * size, transcendentals=0),
        compiler_params=params(),
        name=name,
    )(me, place, pltpu.with_memory_space_constraint(pages, pltpu.HBM))


def send_kernel(counts, limits_ref, place_ref, prefix_ref, pool_ref, *rest):
    outs, (staged, filled, in_sems, out_sems) = rest[: len(counts)], rest[len(counts) :]
    slots, page = pool_ref.shape[0], pool_ref.shape[2]
    me, choice = limits_ref[0], limits_ref[1]
    columns = place_ref.shape[1]
    servers, room = staged.shape[:2]
    first = counts[0]

    def fetch(slot, server, position):
        return pltpu.make_async_copy(
            pool_ref.at[slot], staged.at[server, position], in_sems.at[server, position]
        )

    def fetch_server(server, carry):
        def fetch_row(offset, position):
            row = server * REQUESTS_PER_IDX + offset
            for j in range(columns):
                slot = place_ref[row, j] - me * slots
                wanted = (slot >= 0) & (slot < slots) & (j * page < prefix_ref[row])
                wanted = wanted & (server != me)

                @pl.when(wanted)
                def _(slot=slot, position=position):
                    fetch(slot, server, position).start()

                position = position + jnp.where(wanted, 1, 0)
            return position

        filled[server] = lax.fori_loop(0, REQUESTS_PER_IDX, fetch_row, jnp.int32(0))
        return carry

    lax.fori_loop(0, servers, fetch_server, jnp.int32(0))

    def forward(server, option):
        size = first if option == 0 else counts[option] - first
        begin = 0 if option == 0 else first
        return pltpu.make_async_copy(
            staged.at[server, pl.ds(begin, size)],
            outs[option].at[pl.ds(server * size, size)],
            out_sems.at[server, min(option, 1)],
        )

    def forward_server(server, carry):
        for position in range(room):

            @pl.when(position < filled[server])
            def _(position=position):
                fetch(0, server, position).wait()

        forward(server, 0).start()
        for option in range(1, len(counts)):

            @pl.when(choice == option)
            def _(option=option):
                forward(server, option).start()

        return carry

    lax.fori_loop(0, servers, forward_server, jnp.int32(0))

    def finish_server(server, carry):
        forward(server, 0).wait()
        for option in range(1, len(counts)):

            @pl.when(choice == option)
            def _(option=option):
                forward(server, option).wait()

        return carry

    lax.fori_loop(0, servers, finish_server, jnp.int32(0))


def send_used(counts, limits, place, prefix, pages):
    servers = lax.axis_size("req")
    sizes = [counts[0]] + [count - counts[0] for count in counts[1:]]
    shapes = [
        pltpu.HBM((servers * size,) + pages.shape[1:], pages.dtype) for size in sizes
    ]
    return pl.pallas_call(
        functools.partial(send_kernel, counts),
        out_shape=shapes,
        grid_spec=pltpu.PrefetchScalarGridSpec(
            num_scalar_prefetch=3,
            grid=(1,),
            in_specs=[any_spec()],
            out_specs=[hbm_spec()] * len(counts),
            scratch_shapes=[
                pltpu.VMEM((servers, counts[-1]) + pages.shape[1:], pages.dtype),
                pltpu.SMEM((servers,), jnp.int32),
                pltpu.SemaphoreType.DMA((servers, counts[-1])),
                pltpu.SemaphoreType.DMA((servers, 2)),
            ],
        ),
        cost_estimate=pl.CostEstimate(
            flops=0, bytes_accessed=2 * pages.size * 2, transcendentals=0
        ),
        compiler_params=params(),
        name="send_used_pages",
    )(limits, place, prefix, pages)


def unwritten(shapes):
    return pl.pallas_call(
        lambda *refs: None,
        out_shape=shapes,
        out_specs=[hbm_spec()] * len(shapes),
        cost_estimate=pl.CostEstimate(flops=0, bytes_accessed=0, transcendentals=0),
        name="unwritten",
    )()


def conv_silu(buffer, cache_ref, values, weight_ref):
    length = values.shape[0]
    taps = weight_ref.shape[-2]
    buffer[0:8, :] = cache_ref[...]
    buffer[8:, :] = values.astype(jnp.float32)
    start = 8 - (taps - 1)
    summed = weight_ref[0:1, :] * buffer[start : start + length, :]
    for tap in range(1, taps):
        at = start + tap
        summed = summed + weight_ref[tap : tap + 1, :] * buffer[at : at + length, :]
    return jax.nn.silu(summed).astype(jnp.bfloat16)


def inner_kernel(
    heads,
    x_ref,
    x_cache_ref,
    x_weight_ref,
    maps_ref,
    maps_cache_ref,
    maps_weight_ref,
    decay_row_ref,
    decay_col_ref,
    delta_row_ref,
    tail_ref,
    skip_ref,
    partial_ref,
    update_ref,
    output_map_ref,
    x_buffer,
    maps_buffer,
    x_values,
    scaled,
):
    length, width = x_ref.shape
    head_dim = width // heads
    state = maps_ref.shape[1] // 2
    x_values[...] = conv_silu(x_buffer, x_cache_ref, x_ref[...], x_weight_ref)
    maps = conv_silu(maps_buffer, maps_cache_ref, maps_ref[...], maps_weight_ref)
    input_map, output_map = maps[:, :state], maps[:, state:]
    output_map_ref[...] = output_map
    intersection = lax.dot_general(
        output_map, input_map, HIDDEN, preferred_element_type=jnp.float32
    )
    rows = lax.broadcasted_iota(jnp.int32, (length, length), 0)
    columns = lax.broadcasted_iota(jnp.int32, (length, length), 1)
    causal = rows >= columns
    for h in range(heads):
        lanes = slice(h * head_dim, (h + 1) * head_dim)
        gap = decay_col_ref[:, h : h + 1] - decay_row_ref[h : h + 1, :]
        decays = jnp.where(causal, jnp.exp(jnp.where(causal, gap, 0.0)), 0.0)
        mixing = (intersection * decays * delta_row_ref[h : h + 1, :]).astype(jnp.bfloat16)
        x_head = x_values[:, lanes]
        x_wide = x_head.astype(jnp.float32)
        within = jnp.dot(mixing, x_head, preferred_element_type=jnp.float32)
        partial_ref[:, lanes] = within + skip_ref[:, lanes] * x_wide
        scaled[:, lanes] = (x_wide * tail_ref[:, h : h + 1]).astype(jnp.bfloat16)
    update_ref[...] = lax.dot_general(
        scaled[...], input_map, (((0,), (0,)), ((), ())), preferred_element_type=jnp.float32
    )


def state_kernel(
    me_ref,
    state_place_ref,
    store_place_ref,
    got_ref,
    update_ref,
    partial_ref,
    output_map_ref,
    growth_ref,
    decay_row_ref,
    out_ref,
    send_ref,
    pages,
    finals,
    prior,
    arrival,
    departure,
    counts,
    in_sems,
    out_sems,
):
    request, group = pl.program_id(0), pl.program_id(1)
    page_count, heads, page_rows, state = pages.shape
    entries = REQUESTS_PER_IDX * page_count
    slots = got_ref.shape[0]
    peers = counts.shape[0]
    capacity = entries // peers
    head_dim = page_count * page_rows

    @pl.when((request == 0) & (group == 0))
    def _():
        for place_ref, found in ((state_place_ref, arrival), (store_place_ref, departure)):
            for peer in range(peers):
                counts[peer] = 0

            def row_step(offset, carry, place_ref=place_ref, found=found):
                for j in range(page_count):
                    owner = place_ref[me_ref[0] * REQUESTS_PER_IDX + offset, j] // slots
                    rank = counts[owner]
                    counts[owner] = rank + 1
                    found[offset * page_count + j] = owner * capacity + rank
                return carry

            lax.fori_loop(0, REQUESTS_PER_IDX, row_step, jnp.int32(0))

    half = pl.ds(group * heads, heads)
    arrivals = [
        pltpu.make_async_copy(
            got_ref.at[arrival[request * page_count + j], half], pages.at[j], in_sems.at[j]
        )
        for j in range(page_count)
    ]
    for copy in arrivals:
        copy.start()
    departures = [
        pltpu.make_async_copy(
            finals.at[j], send_ref.at[departure[request * page_count + j], half], out_sems.at[j]
        )
        for j in range(page_count)
    ]
    last = decay_row_ref.shape[1] - 1
    for j in range(page_count):
        arrivals[j].wait()
        for h in range(heads):
            at = h * head_dim + j * page_rows
            old = pages[j, h].astype(jnp.float32)
            prior[at : at + page_rows, :] = old
            growth = jnp.exp(decay_row_ref[h : h + 1, last : last + 1])
            finals[j, h] = (growth * old + update_ref[at : at + page_rows, :]).astype(jnp.bfloat16)
        departures[j].start()
    carried = lax.dot_general(
        output_map_ref[...],
        prior[...].astype(jnp.bfloat16),
        HIDDEN,
        preferred_element_type=jnp.float32,
    )
    for h in range(heads):
        lanes = slice(h * head_dim, (h + 1) * head_dim)
        out_ref[:, lanes] = (
            partial_ref[:, lanes] + growth_ref[:, h : h + 1] * carried[:, lanes]
        ).astype(jnp.bfloat16)
    for copy in departures:
        copy.wait()


def attend_kernel(
    scale,
    counts,
    limits_ref,
    place_ref,
    prefix_ref,
    pool_ref,
    *rest,
):
    gots = rest[: len(counts)]
    query_ref, fresh_ref, out_ref = rest[len(counts) : len(counts) + 3]
    cached_kv, top_ref, total_ref, attended, kinds, indices, ranks, sems = rest[len(counts) + 3 :]
    request, kv_head = pl.program_id(0), pl.program_id(1)
    per_kv, length, head_dim = query_ref.shape
    slots, page = pool_ref.shape[0], pool_ref.shape[2]
    page_count = place_ref.shape[1]
    peers = ranks.shape[0]
    me, choice = limits_ref[0], limits_ref[1]
    first = counts[0]
    chunk = length
    start_row = me * REQUESTS_PER_IDX

    @pl.when((request == 0) & (kv_head == 0))
    def _():
        cached_kv[...] = jnp.zeros_like(cached_kv)
        for peer in range(peers):
            ranks[peer] = 0
        more = jnp.int32(1)
        for option in range(1, len(counts)):
            more = jnp.where(choice == option, counts[option] - first, more)

        def place_row(offset, carry):
            tokens = prefix_ref[start_row + offset]
            for j in range(page_count):
                place = place_ref[start_row + offset, j]
                owner = place // slots
                rank = ranks[owner]
                ranks[owner] = rank + jnp.where(j * page < tokens, 1, 0)
                here = owner == me
                early = rank < first
                index = jnp.where(early, owner * first + rank, owner * more + rank - first)
                entry = offset * page_count + j
                kinds[entry] = jnp.where(here, len(counts), jnp.where(early, 0, choice))
                indices[entry] = jnp.where(here, place - me * slots, index)
            return carry

        lax.fori_loop(0, REQUESTS_PER_IDX, place_row, jnp.int32(0))

    tokens = prefix_ref[start_row + request]
    used_pages = (tokens + page - 1) // page

    def target(j):
        return cached_kv.at[pl.ds(pl.multiple_of(j * page, page), page)]

    def start_copy(j, carry):
        entry = request * page_count + j
        for kind, source in enumerate(gots + (pool_ref,)):

            @pl.when(kinds[entry] == kind)
            def _(source=source):
                pltpu.make_async_copy(
                    source.at[indices[entry], kv_head], target(j), sems.at[j]
                ).start()

        return carry

    lax.fori_loop(0, used_pages, start_copy, jnp.int32(0))

    query = query_ref[...].reshape(per_kv * length, head_dim)
    keys_at = lax.broadcasted_iota(jnp.int32, (length, per_kv * length), 0)

    def score(keys):
        return lax.dot_general(keys, query, HIDDEN, preferred_element_type=jnp.float32) * scale

    def weigh(values, exponent):
        return lax.dot_general(
            values,
            exponent.astype(jnp.bfloat16),
            (((0,), (0,)), ((), ())),
            preferred_element_type=jnp.float32,
        )

    queries_at = lax.broadcasted_iota(jnp.int32, (length, per_kv * length), 1) % length
    scores = jnp.where(keys_at <= queries_at, score(fresh_ref[:, :head_dim]), -jnp.inf)
    top = jnp.max(scores, axis=0, keepdims=True)
    exponent = jnp.exp(scores - top)
    top_ref[...] = top
    total_ref[...] = jnp.sum(exponent, axis=0, keepdims=True)
    attended[...] = weigh(fresh_ref[:, head_dim:], exponent)

    def wait_copy(j, carry):
        pltpu.make_async_copy(pool_ref.at[0, kv_head], target(j), sems.at[j]).wait()
        return carry

    lax.fori_loop(0, used_pages, wait_copy, jnp.int32(0))

    def chunk_step(step, carry):
        start = pl.multiple_of(step * chunk, chunk)
        scores = score(cached_kv[pl.ds(start, chunk), :head_dim])
        scores = jnp.where(keys_at < tokens - start, scores, -jnp.inf)
        old = top_ref[...]
        top = jnp.maximum(old, jnp.max(scores, axis=0, keepdims=True))
        fade = jnp.exp(old - top)
        exponent = jnp.exp(scores - top)
        top_ref[...] = top
        total_ref[...] = total_ref[...] * fade + jnp.sum(exponent, axis=0, keepdims=True)
        attended[...] = attended[...] * fade + weigh(
            cached_kv[pl.ds(start, chunk), head_dim:], exponent
        )
        return carry

    lax.fori_loop(0, (tokens + chunk - 1) // chunk, chunk_step, jnp.int32(0))
    out_ref[...] = (
        (attended[...] / total_ref[...]).T.astype(jnp.bfloat16).reshape(out_ref.shape)
    )


def body(
    mixer_in,
    maps_in,
    delta_raw,
    conv_cache,
    maps_cache,
    conv_weight,
    maps_weight,
    decay_log,
    skip_gain,
    state_pool,
    queries,
    suffix_keyvals,
    page_pool,
    prefix_tokens,
    page_place,
    state_place,
    store_place,
):
    peers = lax.axis_size("req")
    me = lax.axis_index("req").astype(jnp.int32).reshape(1)
    requests, length = REQUESTS_PER_IDX, APPENDED_LENGTH
    groups = maps_in.shape[1]
    state = maps_in.shape[2] // 2
    heads = delta_raw.shape[1]
    per_group = heads // groups
    width = mixer_in.shape[1]
    group_width = width // groups
    head_dim = width // heads
    slots, _, page_rows, _ = state_pool.shape
    page_count = state_place.shape[1]
    kv_heads = page_pool.shape[2]
    attend_dim = queries.shape[2]
    per_kv = queries.shape[1] // kv_heads
    page = page_pool.shape[1]
    prefix_pages = page_place.shape[1]
    page_slots = page_pool.shape[0]
    pair_pages = requests * prefix_pages // peers
    taps = conv_weight.shape[0]

    def exchange(pages):
        return lax.all_to_all(pages, "req", split_axis=0, concat_axis=0, tiled=True)

    state_send = route_pages(gather_kernel, "gather_states", me, state_place, state_pool)
    state_got = exchange(state_send)

    counts = tuple(sorted({max(1, pair_pages * share // 16) for share in SHARES}))
    used = jnp.arange(prefix_pages)[None, :] * page < prefix_tokens[:, None]
    holders = page_place // page_slots
    pairs = used[:, :, None] & (holders[:, :, None] == jnp.arange(peers)[None, None, :])
    needs = jnp.sum(pairs.reshape(peers, -1, peers).astype(jnp.int32), axis=1)
    elsewhere = jnp.arange(peers)[:, None] != jnp.arange(peers)[None, :]
    needed = jnp.max(jnp.where(elsewhere, needs, 0))
    choice = jnp.sum((needed > jnp.array(counts[:-1], jnp.int32)).astype(jnp.int32))
    limits = jnp.stack([me[0], choice])
    pages_by_head = page_pool.transpose(0, 2, 1, 3)
    page_sends = send_used(counts, limits, page_place, prefix_tokens, pages_by_head)

    delta = jax.nn.softplus(delta_raw.T.astype(jnp.float32)).reshape(heads, requests, length)
    log_decay = jnp.cumsum(-delta * jnp.exp(decay_log)[:, None, None], axis=2)
    tail = jnp.exp(log_decay[:, :, -1:] - log_decay) * delta
    growth = jnp.exp(log_decay)

    def by_rows(values):
        return values.reshape(groups, per_group, requests, length).transpose(2, 0, 1, 3)

    def by_columns(values):
        return values.reshape(groups, per_group, requests, length).transpose(2, 0, 3, 1)

    decay_row = by_rows(log_decay)
    maps_split = maps_in.transpose(1, 0, 2)
    empty = 8 - (taps - 1)
    x_cache = jnp.pad(conv_cache.astype(jnp.float32), ((0, 0), (empty, 0), (0, 0)))
    maps_edge = jnp.pad(
        maps_cache.transpose(0, 2, 1, 3).astype(jnp.float32), ((0, 0), (0, 0), (empty, 0), (0, 0))
    )
    row_block = pl.BlockSpec((None, None, per_group, length), lambda r, g: (r, g, 0, 0))
    column_block = pl.BlockSpec((None, None, length, per_group), lambda r, g: (r, g, 0, 0))
    x_block = pl.BlockSpec((length, group_width), lambda r, g: (r, g))
    update_block = pl.BlockSpec((None, None, group_width, state), lambda r, g: (r, g, 0, 0))
    map_block = pl.BlockSpec((None, length, state), lambda r, g: (g, r, 0))
    partial, update, output_map = pl.pallas_call(
        functools.partial(inner_kernel, per_group),
        grid=(requests, groups),
        in_specs=[
            x_block,
            pl.BlockSpec((None, 8, group_width), lambda r, g: (r, 0, g)),
            pl.BlockSpec((taps, group_width), lambda r, g: (0, g)),
            pl.BlockSpec((None, length, 2 * state), lambda r, g: (g, r, 0)),
            pl.BlockSpec((None, None, 8, 2 * state), lambda r, g: (r, g, 0, 0)),
            pl.BlockSpec((None, taps, 2 * state), lambda r, g: (g, 0, 0)),
            row_block,
            column_block,
            row_block,
            column_block,
            pl.BlockSpec((1, group_width), lambda r, g: (0, g)),
        ],
        out_specs=[x_block, update_block, map_block],
        out_shape=[
            jax.ShapeDtypeStruct((requests * length, width), jnp.float32),
            jax.ShapeDtypeStruct((requests, groups, group_width, state), jnp.float32),
            jax.ShapeDtypeStruct((groups, requests * length, state), jnp.bfloat16),
        ],
        scratch_shapes=[
            pltpu.VMEM((8 + length, group_width), jnp.float32),
            pltpu.VMEM((8 + length, 2 * state), jnp.float32),
            pltpu.VMEM((length, group_width), jnp.bfloat16),
            pltpu.VMEM((length, group_width), jnp.bfloat16),
        ],
        cost_estimate=pl.CostEstimate(
            flops=3 * requests * length * width * state,
            bytes_accessed=32 * 2**20,
            transcendentals=requests * heads * length * length,
        ),
        compiler_params=params(),
        name="mix_new_tokens",
    )(
        mixer_in,
        x_cache,
        conv_weight.astype(jnp.float32),
        maps_split,
        maps_edge,
        maps_weight.transpose(1, 0, 2).astype(jnp.float32),
        decay_row,
        by_columns(log_decay),
        by_rows(delta),
        by_columns(tail),
        jnp.repeat(skip_gain, head_dim).reshape(1, width),
    )
    growth_col = by_columns(growth)
    grouped_queries = queries.reshape(requests, length, kv_heads, per_kv, attend_dim).transpose(
        0, 2, 3, 1, 4
    )
    fresh = suffix_keyvals.transpose(1, 0, 2)

    first_send, state_got, partial, update, output_map, growth_col, decay_row = (
        lax.optimization_barrier(
            (page_sends[0], state_got, partial, update, output_map, growth_col, decay_row)
        )
    )
    first_got = exchange(first_send)
    more_sends = lax.optimization_barrier((first_got, page_sends[1:]))[1]
    more_shapes = [pltpu.HBM(sent.shape, sent.dtype) for sent in more_sends]

    def no_more(sends):
        return tuple(unwritten(more_shapes))

    def send_more(at, sends):
        gots = list(unwritten(more_shapes[:at] + more_shapes[at + 1 :]))
        return tuple(gots[:at] + [exchange(sends[at])] + gots[at:])

    more_gots = lax.switch(
        choice,
        [no_more] + [functools.partial(send_more, at) for at in range(len(more_shapes))],
        more_sends,
    )
    page_gots = (first_got,) + tuple(more_gots)
    mixer_out, final_send = pl.pallas_call(
        state_kernel,
        grid_spec=pltpu.PrefetchScalarGridSpec(
            num_scalar_prefetch=3,
            grid=(requests, groups),
            in_specs=[
                any_spec(),
                pl.BlockSpec((None, None, group_width, state), lambda r, g, *_: (r, g, 0, 0)),
                pl.BlockSpec((length, group_width), lambda r, g, *_: (r, g)),
                pl.BlockSpec((None, length, state), lambda r, g, *_: (g, r, 0)),
                pl.BlockSpec((None, None, length, per_group), lambda r, g, *_: (r, g, 0, 0)),
                pl.BlockSpec((None, None, per_group, length), lambda r, g, *_: (r, g, 0, 0)),
            ],
            out_specs=[
                pl.BlockSpec((length, group_width), lambda r, g, *_: (r, g)),
                hbm_spec(),
            ],
            scratch_shapes=[
                pltpu.VMEM((page_count, per_group, page_rows, state), jnp.bfloat16),
                pltpu.VMEM((page_count, per_group, page_rows, state), jnp.bfloat16),
                pltpu.VMEM((group_width, state), jnp.float32),
                pltpu.SMEM((requests * page_count,), jnp.int32),
                pltpu.SMEM((requests * page_count,), jnp.int32),
                pltpu.SMEM((peers,), jnp.int32),
                pltpu.SemaphoreType.DMA((page_count,)),
                pltpu.SemaphoreType.DMA((page_count,)),
            ],
        ),
        out_shape=[
            jax.ShapeDtypeStruct((requests * length, width), jnp.bfloat16),
            pltpu.HBM(state_pool.shape, jnp.bfloat16),
        ],
        cost_estimate=pl.CostEstimate(
            flops=2 * requests * length * width * state,
            bytes_accessed=32 * 2**20,
            transcendentals=0,
        ),
        compiler_params=params(),
        name="advance_states",
    )(
        me,
        state_place,
        store_place,
        state_got,
        update,
        partial,
        output_map,
        growth_col,
        decay_row,
    )
    final_send, page_gots = lax.optimization_barrier((final_send, page_gots))
    final_got = exchange(final_send)
    head_block = pl.BlockSpec(
        (None, None, per_kv, length, attend_dim), lambda r, e, *_: (r, e, 0, 0, 0)
    )
    attended = pl.pallas_call(
        functools.partial(attend_kernel, attend_dim**-0.5, counts),
        grid_spec=pltpu.PrefetchScalarGridSpec(
            num_scalar_prefetch=3,
            grid=(requests, kv_heads),
            in_specs=[any_spec()] * (len(page_gots) + 1)
            + [
                head_block,
                pl.BlockSpec((None, length, 2 * attend_dim), lambda r, e, *_: (e, r, 0)),
            ],
            out_specs=head_block,
            scratch_shapes=[
                pltpu.VMEM((prefix_pages * page, 2 * attend_dim), jnp.bfloat16),
                pltpu.VMEM((1, per_kv * length), jnp.float32),
                pltpu.VMEM((1, per_kv * length), jnp.float32),
                pltpu.VMEM((attend_dim, per_kv * length), jnp.float32),
                pltpu.SMEM((requests * prefix_pages,), jnp.int32),
                pltpu.SMEM((requests * prefix_pages,), jnp.int32),
                pltpu.SMEM((peers,), jnp.int32),
                pltpu.SemaphoreType.DMA((prefix_pages,)),
            ],
        ),
        out_shape=jax.ShapeDtypeStruct(grouped_queries.shape, jnp.bfloat16),
        cost_estimate=pl.CostEstimate(
            flops=4 * queries.size * (prefix_pages * page + length),
            bytes_accessed=16 * 2**20,
            transcendentals=queries.shape[0] * queries.shape[1] * (prefix_pages * page),
        ),
        compiler_params=params(),
        name="attend",
    )(
        limits,
        page_place,
        prefix_tokens,
        pages_by_head,
        *page_gots,
        grouped_queries,
        fresh,
    )
    attention_out = attended.transpose(0, 3, 1, 2, 4).reshape(queries.shape)
    stored = route_pages(scatter_kernel, "scatter_states", me, store_place, final_got)
    return mixer_out, attention_out, stored


def solution(mesh):
    placed = (
        P(("parts", "req"), "tp"),
        P(("parts", "req"), "tp", None),
        P(("parts", "req"), "tp"),
        P(("parts", "req"), None, "tp"),
        P(("parts", "req"), None, "tp", None),
        P(None, "tp"),
        P(None, "tp", None),
        P("tp"),
        P("tp"),
        P(("parts", "req"), "tp", None, None),
        P(("parts", "req"), "tp", None),
        P(("parts", "req"), "tp", None),
        P(("parts", "req"), None, "tp", None),
        P("parts"),
        P("parts", None),
        P("parts", None),
        P("parts", None),
    )
    return jax.shard_map(
        body,
        mesh=mesh,
        in_specs=placed,
        out_specs=(
            P(("parts", "req"), "tp"),
            P(("parts", "req"), "tp", None),
            P(("parts", "req"), "tp", None, None),
        ),
        check_vma=False,
    )
```

```python
import functools

import jax
import jax.numpy as jnp
from jax import lax
from jax.experimental import pallas as pl
from jax.experimental.pallas import tpu as pltpu
from jax.sharding import PartitionSpec as P

APPENDED_LENGTH = 256
REQUESTS_PER_IDX = 4
VMEM_LIMIT = 48 * 1024 * 1024
SHARES = (8, 9, 10, 11, 12, 16)
PASSED = 8
HIDDEN = (((1,), (1,)), ((), ()))


def params():
    return pltpu.CompilerParams(vmem_limit_bytes=VMEM_LIMIT)


def any_spec():
    return pl.BlockSpec(memory_space=pl.ANY)


def hbm_spec():
    return pl.BlockSpec(memory_space=pltpu.HBM)


def own_entries(place_ref, base, slots, position, row, emit):
    for j in range(place_ref.shape[1]):
        slot = place_ref[row, j] - base
        mine = (slot >= 0) & (slot < slots)

        @pl.when(mine)
        def _(slot=slot, position=position, j=j):
            emit(position, slot)

        position = position + jnp.where(mine, 1, 0)
    return position


def gather_kernel(capacity, me_ref, place_ref, pool_ref, out_ref, staged, in_sems, out_sems):
    slots = pool_ref.shape[0]
    base = me_ref[0] * slots
    servers = place_ref.shape[0] // REQUESTS_PER_IDX

    def server_step(server, carry):
        def row_step(offset, position):
            def emit(at, slot):
                pltpu.make_async_copy(
                    pool_ref.at[slot], staged.at[server * capacity + at], in_sems.at[server]
                ).start()

            row = server * REQUESTS_PER_IDX + offset
            return own_entries(place_ref, base, slots, position, row, emit)

        lax.fori_loop(0, REQUESTS_PER_IDX, row_step, jnp.int32(0))
        return carry

    lax.fori_loop(0, servers, server_step, jnp.int32(0))

    def part(server):
        return pl.ds(pl.multiple_of(server * capacity, capacity), capacity)

    def forward(server, carry):
        pltpu.make_async_copy(
            pool_ref.at[part(0)], staged.at[part(server)], in_sems.at[server]
        ).wait()
        pltpu.make_async_copy(
            staged.at[part(server)], out_ref.at[part(server)], out_sems.at[server]
        ).start()
        return carry

    lax.fori_loop(0, servers, forward, jnp.int32(0))

    def finish(server, carry):
        pltpu.make_async_copy(
            staged.at[part(server)], out_ref.at[part(server)], out_sems.at[server]
        ).wait()
        return carry

    lax.fori_loop(0, servers, finish, jnp.int32(0))


def scatter_kernel(capacity, me_ref, place_ref, got_ref, out_ref, staged, in_sems, out_sems):
    slots = out_ref.shape[0]
    base = me_ref[0] * slots
    servers = place_ref.shape[0] // REQUESTS_PER_IDX

    def fetch(server):
        part = pl.ds(pl.multiple_of(server * capacity, capacity), capacity)
        return pltpu.make_async_copy(got_ref.at[part], staged.at[part], in_sems.at[server])

    def start_fetch(server, carry):
        fetch(server).start()
        return carry

    lax.fori_loop(0, servers, start_fetch, jnp.int32(0))

    def server_step(server, carry):
        fetch(server).wait()

        def row_step(offset, position):
            def emit(at, slot):
                pltpu.make_async_copy(
                    staged.at[server * capacity + at], out_ref.at[slot], out_sems.at[0]
                ).start()

            row = server * REQUESTS_PER_IDX + offset
            return own_entries(place_ref, base, slots, position, row, emit)

        lax.fori_loop(0, REQUESTS_PER_IDX, row_step, jnp.int32(0))
        return carry

    lax.fori_loop(0, servers, server_step, jnp.int32(0))
    pltpu.make_async_copy(staged, out_ref, out_sems.at[0]).wait()


def route_pages(kernel, name, me, place, pages):
    servers = lax.axis_size("req")
    capacity = pages.shape[0] // servers
    size = pages.size * pages.dtype.itemsize
    return pl.pallas_call(
        functools.partial(kernel, capacity),
        out_shape=pltpu.HBM(pages.shape, pages.dtype),
        grid_spec=pltpu.PrefetchScalarGridSpec(
            num_scalar_prefetch=2,
            grid=(1,),
            in_specs=[hbm_spec()],
            out_specs=hbm_spec(),
            scratch_shapes=[
                pltpu.VMEM(pages.shape, pages.dtype),
                pltpu.SemaphoreType.DMA((servers,)),
                pltpu.SemaphoreType.DMA((servers,)),
            ],
        ),
        cost_estimate=pl.CostEstimate(flops=0, bytes_accessed=2 * size, transcendentals=0),
        compiler_params=params(),
        name=name,
    )(me, place, pltpu.with_memory_space_constraint(pages, pltpu.HBM))


def used_entry(place_ref, prefix_ref, page, slots, owner, row, j):
    slot = place_ref[row, j] - owner * slots
    return slot, (slot >= 0) & (slot < slots) & (j * page < prefix_ref[row])


def count_used(place_ref, entry, owner, server):
    def count_row(offset, total):
        for j in range(place_ref.shape[1]):
            _, wanted = entry(owner, server * REQUESTS_PER_IDX + offset, j)
            total = total + jnp.where(wanted, 1, 0)
        return total

    return lax.fori_loop(0, REQUESTS_PER_IDX, count_row, jnp.int32(0))


def partner_of(device):
    return device + 1 - 2 * (device % 2)


def send_kernel(counts, limits_ref, place_ref, prefix_ref, pool_ref, *rest):
    outs, (staged, needs, filled, in_sems, out_sems) = rest[: len(counts)], rest[len(counts) :]
    slots, page = pool_ref.shape[0], pool_ref.shape[2]
    me, limit, choice = limits_ref[0], limits_ref[1], limits_ref[2]
    columns = place_ref.shape[1]
    servers, room = staged.shape[:2]
    first = counts[0]
    entry = functools.partial(used_entry, place_ref, prefix_ref, page, slots)

    def count_server(server, carry):
        needs[server] = count_used(place_ref, entry, me, server)
        return carry

    lax.fori_loop(0, servers, count_server, jnp.int32(0))

    def fetch(slot, server, position):
        return pltpu.make_async_copy(
            pool_ref.at[slot], staged.at[server, position], in_sems.at[server, position]
        )

    def fetch_server(server, carry):
        partner = partner_of(server)
        start = needs[partner] - limit

        def fetch_row(offset, rank):
            for j in range(columns):
                slot, wanted = entry(me, server * REQUESTS_PER_IDX + offset, j)
                wanted = wanted & (server != me)
                direct = rank < limit

                @pl.when(wanted & (direct | (partner != me)))
                def _(slot=slot, rank=rank, direct=direct):
                    fetch(
                        slot,
                        jnp.where(direct, server, partner),
                        jnp.where(direct, rank, start + rank),
                    ).start()

                rank = rank + jnp.where(wanted, 1, 0)
            return rank

        lax.fori_loop(0, REQUESTS_PER_IDX, fetch_row, jnp.int32(0))
        passed = jnp.where(partner == me, 0, jnp.maximum(needs[partner] - limit, 0))
        own = jnp.minimum(needs[server], limit)
        filled[server] = jnp.where(server == me, 0, own + passed)
        return carry

    lax.fori_loop(0, servers, fetch_server, jnp.int32(0))

    def forward(server, option):
        size = first if option == 0 else counts[option] - first
        begin = 0 if option == 0 else first
        return pltpu.make_async_copy(
            staged.at[server, pl.ds(begin, size)],
            outs[option].at[pl.ds(server * size, size)],
            out_sems.at[server, min(option, 1)],
        )

    def forward_server(server, carry):
        for position in range(room):

            @pl.when(position < filled[server])
            def _(position=position):
                fetch(0, server, position).wait()

        forward(server, 0).start()
        for option in range(1, len(counts)):

            @pl.when(choice == option)
            def _(option=option):
                forward(server, option).start()

        return carry

    lax.fori_loop(0, servers, forward_server, jnp.int32(0))

    def finish_server(server, carry):
        forward(server, 0).wait()
        for option in range(1, len(counts)):

            @pl.when(choice == option)
            def _(option=option):
                forward(server, option).wait()

        return carry

    lax.fori_loop(0, servers, finish_server, jnp.int32(0))


def send_used(counts, limits, place, prefix, pages):
    servers = lax.axis_size("req")
    sizes = [counts[0]] + [count - counts[0] for count in counts[1:]]
    shapes = [
        pltpu.HBM((servers * size,) + pages.shape[1:], pages.dtype) for size in sizes
    ]
    return pl.pallas_call(
        functools.partial(send_kernel, counts),
        out_shape=shapes,
        grid_spec=pltpu.PrefetchScalarGridSpec(
            num_scalar_prefetch=3,
            grid=(1,),
            in_specs=[any_spec()],
            out_specs=[hbm_spec()] * len(counts),
            scratch_shapes=[
                pltpu.VMEM((servers, counts[-1]) + pages.shape[1:], pages.dtype),
                pltpu.SMEM((servers,), jnp.int32),
                pltpu.SMEM((servers,), jnp.int32),
                pltpu.SemaphoreType.DMA((servers, counts[-1])),
                pltpu.SemaphoreType.DMA((servers, 2)),
            ],
        ),
        cost_estimate=pl.CostEstimate(
            flops=0, bytes_accessed=2 * pages.size * 2, transcendentals=0
        ),
        compiler_params=params(),
        name="send_used_pages",
    )(limits, place, prefix, pages)


def pass_kernel(counts, limits_ref, place_ref, prefix_ref, pool_ref, *rest):
    gots, (out_ref, staged, in_sems, out_sem) = rest[: len(counts)], rest[len(counts) :]
    slots, page = pool_ref.shape[0], pool_ref.shape[2]
    me, limit, choice = limits_ref[0], limits_ref[1], limits_ref[2]
    columns = place_ref.shape[1]
    servers = place_ref.shape[0] // REQUESTS_PER_IDX
    first = counts[0]
    partner = partner_of(me)
    entry = functools.partial(used_entry, place_ref, prefix_ref, page, slots)

    def fetch(source, index, at):
        return pltpu.make_async_copy(source.at[index], staged.at[at], in_sems.at[at])

    def own_pages(at):
        def row_step(offset, carry):
            rank, at = carry
            for j in range(columns):
                slot, wanted = entry(me, partner * REQUESTS_PER_IDX + offset, j)
                take = wanted & (rank >= limit)

                @pl.when(take)
                def _(slot=slot, at=at):
                    fetch(pool_ref, slot, at).start()

                rank = rank + jnp.where(wanted, 1, 0)
                at = at + jnp.where(take, 1, 0)
            return rank, at

        return lax.fori_loop(0, REQUESTS_PER_IDX, row_step, (jnp.int32(0), at))[1]

    def relayed_pages(owner, at):
        start = count_used(place_ref, entry, owner, me)
        more = jnp.maximum(count_used(place_ref, entry, owner, partner) - limit, 0)

        def page_step(step, carry):
            position = start + step

            @pl.when(position < first)
            def _():
                fetch(gots[0], owner * first + position, at + step).start()

            for option in range(1, len(counts)):
                size = counts[option] - first

                @pl.when((position >= first) & (choice == option))
                def _(option=option, size=size):
                    fetch(gots[option], owner * size + position - first, at + step).start()

            return carry

        lax.fori_loop(0, more, page_step, jnp.int32(0))
        return at + more

    def owner_step(owner, at):
        at = lax.cond(owner == me, own_pages, lambda at: at, at)
        outside = (owner != me) & (owner != partner)
        return lax.cond(outside, lambda at: relayed_pages(owner, at), lambda at: at, at)

    total = lax.fori_loop(0, servers, owner_step, jnp.int32(0))
    for position in range(staged.shape[0]):

        @pl.when(position < total)
        def _(position=position):
            fetch(pool_ref, 0, position).wait()

    forward = pltpu.make_async_copy(staged, out_ref, out_sem)
    forward.start()
    forward.wait()


def pass_on(counts, limits, place, prefix, pages, gots):
    shape = (PASSED,) + pages.shape[1:]
    collected = pl.pallas_call(
        functools.partial(pass_kernel, counts),
        out_shape=pltpu.HBM(shape, pages.dtype),
        grid_spec=pltpu.PrefetchScalarGridSpec(
            num_scalar_prefetch=3,
            grid=(1,),
            in_specs=[any_spec()] * (1 + len(gots)),
            out_specs=hbm_spec(),
            scratch_shapes=[
                pltpu.VMEM(shape, pages.dtype),
                pltpu.SemaphoreType.DMA((PASSED,)),
                pltpu.SemaphoreType.DMA,
            ],
        ),
        cost_estimate=pl.CostEstimate(flops=0, bytes_accessed=2**20, transcendentals=0),
        compiler_params=params(),
        name="pass_pages_on",
    )(limits, place, prefix, pages, *gots)
    swaps = [(peer, peer ^ 1) for peer in range(lax.axis_size("req"))]
    return lax.ppermute(collected, "req", swaps)


def unwritten(shapes):
    return pl.pallas_call(
        lambda *refs: None,
        out_shape=shapes,
        out_specs=[hbm_spec()] * len(shapes),
        cost_estimate=pl.CostEstimate(flops=0, bytes_accessed=0, transcendentals=0),
        name="unwritten",
    )()


def conv_silu(buffer, cache_ref, values, weight_ref):
    length = values.shape[0]
    taps = weight_ref.shape[-2]
    buffer[0:8, :] = cache_ref[...]
    buffer[8:, :] = values.astype(jnp.float32)
    start = 8 - (taps - 1)
    summed = weight_ref[0:1, :] * buffer[start : start + length, :]
    for tap in range(1, taps):
        at = start + tap
        summed = summed + weight_ref[tap : tap + 1, :] * buffer[at : at + length, :]
    return jax.nn.silu(summed).astype(jnp.bfloat16)


def inner_kernel(
    heads,
    x_ref,
    x_cache_ref,
    x_weight_ref,
    maps_ref,
    maps_cache_ref,
    maps_weight_ref,
    decay_row_ref,
    decay_col_ref,
    delta_row_ref,
    tail_ref,
    skip_ref,
    partial_ref,
    update_ref,
    output_map_ref,
    x_buffer,
    maps_buffer,
    x_values,
    scaled,
):
    length, width = x_ref.shape
    head_dim = width // heads
    state = maps_ref.shape[1] // 2
    x_values[...] = conv_silu(x_buffer, x_cache_ref, x_ref[...], x_weight_ref)
    maps = conv_silu(maps_buffer, maps_cache_ref, maps_ref[...], maps_weight_ref)
    input_map, output_map = maps[:, :state], maps[:, state:]
    output_map_ref[...] = output_map
    intersection = lax.dot_general(
        output_map, input_map, HIDDEN, preferred_element_type=jnp.float32
    )
    rows = lax.broadcasted_iota(jnp.int32, (length, length), 0)
    columns = lax.broadcasted_iota(jnp.int32, (length, length), 1)
    causal = rows >= columns
    for h in range(heads):
        lanes = slice(h * head_dim, (h + 1) * head_dim)
        gap = decay_col_ref[:, h : h + 1] - decay_row_ref[h : h + 1, :]
        decays = jnp.where(causal, jnp.exp(jnp.where(causal, gap, 0.0)), 0.0)
        mixing = (intersection * decays * delta_row_ref[h : h + 1, :]).astype(jnp.bfloat16)
        x_head = x_values[:, lanes]
        x_wide = x_head.astype(jnp.float32)
        within = jnp.dot(mixing, x_head, preferred_element_type=jnp.float32)
        partial_ref[:, lanes] = within + skip_ref[:, lanes] * x_wide
        scaled[:, lanes] = (x_wide * tail_ref[:, h : h + 1]).astype(jnp.bfloat16)
    update_ref[...] = lax.dot_general(
        scaled[...], input_map, (((0,), (0,)), ((), ())), preferred_element_type=jnp.float32
    )


def state_kernel(
    me_ref,
    state_place_ref,
    store_place_ref,
    got_ref,
    update_ref,
    partial_ref,
    output_map_ref,
    growth_ref,
    decay_row_ref,
    out_ref,
    send_ref,
    pages,
    finals,
    prior,
    arrival,
    departure,
    counts,
    in_sems,
    out_sems,
):
    request, group = pl.program_id(0), pl.program_id(1)
    page_count, heads, page_rows, state = pages.shape
    entries = REQUESTS_PER_IDX * page_count
    slots = got_ref.shape[0]
    peers = counts.shape[0]
    capacity = entries // peers
    head_dim = page_count * page_rows

    @pl.when((request == 0) & (group == 0))
    def _():
        for place_ref, found in ((state_place_ref, arrival), (store_place_ref, departure)):
            for peer in range(peers):
                counts[peer] = 0

            def row_step(offset, carry, place_ref=place_ref, found=found):
                for j in range(page_count):
                    owner = place_ref[me_ref[0] * REQUESTS_PER_IDX + offset, j] // slots
                    rank = counts[owner]
                    counts[owner] = rank + 1
                    found[offset * page_count + j] = owner * capacity + rank
                return carry

            lax.fori_loop(0, REQUESTS_PER_IDX, row_step, jnp.int32(0))

    half = pl.ds(group * heads, heads)
    arrivals = [
        pltpu.make_async_copy(
            got_ref.at[arrival[request * page_count + j], half], pages.at[j], in_sems.at[j]
        )
        for j in range(page_count)
    ]
    for copy in arrivals:
        copy.start()
    departures = [
        pltpu.make_async_copy(
            finals.at[j], send_ref.at[departure[request * page_count + j], half], out_sems.at[j]
        )
        for j in range(page_count)
    ]
    last = decay_row_ref.shape[1] - 1
    for j in range(page_count):
        arrivals[j].wait()
        for h in range(heads):
            at = h * head_dim + j * page_rows
            old = pages[j, h].astype(jnp.float32)
            prior[at : at + page_rows, :] = old
            growth = jnp.exp(decay_row_ref[h : h + 1, last : last + 1])
            finals[j, h] = (growth * old + update_ref[at : at + page_rows, :]).astype(jnp.bfloat16)
        departures[j].start()
    carried = lax.dot_general(
        output_map_ref[...],
        prior[...].astype(jnp.bfloat16),
        HIDDEN,
        preferred_element_type=jnp.float32,
    )
    for h in range(heads):
        lanes = slice(h * head_dim, (h + 1) * head_dim)
        out_ref[:, lanes] = (
            partial_ref[:, lanes] + growth_ref[:, h : h + 1] * carried[:, lanes]
        ).astype(jnp.bfloat16)
    for copy in departures:
        copy.wait()


def list_pages(
    counts, passed, limits_ref, place_ref, prefix_ref, slots, page, kinds, indices, amounts, sizes, ranks
):
    me, limit, choice = limits_ref[0], limits_ref[1], limits_ref[2]
    page_count = place_ref.shape[1]
    peers = ranks.shape[1]
    start_row = me * REQUESTS_PER_IDX
    first = counts[0]
    for peer in range(peers):
        ranks[0, peer] = 0
    if passed:

        def count_row(offset, carry):
            tokens = prefix_ref[start_row + offset]
            for j in range(page_count):
                owner = place_ref[start_row + offset, j] // slots
                ranks[0, owner] = ranks[0, owner] + jnp.where(j * page < tokens, 1, 0)
            return carry

        lax.fori_loop(0, REQUESTS_PER_IDX, count_row, jnp.int32(0))
        begin = jnp.int32(0)
        for peer in range(peers):
            ranks[1, peer] = begin
            begin = begin + jnp.where(peer == me, 0, jnp.maximum(ranks[0, peer] - limit, 0))
            ranks[0, peer] = 0
    more = jnp.int32(1)
    for option in range(1, len(counts)):
        more = jnp.where(choice == option, counts[option] - first, more)

    def place_row(offset, carry):
        tokens = prefix_ref[start_row + offset]
        at, size = jnp.int32(0), jnp.int32(0)
        for j in range(page_count):
            place = place_ref[start_row + offset, j]
            owner = place // slots
            rank = ranks[0, owner]
            used = j * page < tokens
            ranks[0, owner] = rank + jnp.where(used, 1, 0)
            here = owner == me
            late = (rank >= limit) & jnp.logical_not(here)
            if passed:
                take = used & late
                kind = jnp.int32(0)
                index = ranks[1, owner] + rank - limit
            else:
                take = used & jnp.logical_not(late)
                early = rank < first
                kind = jnp.where(here, len(counts), jnp.where(early, 0, choice))
                index = jnp.where(early, owner * first + rank, owner * more + rank - first)
                index = jnp.where(here, place - me * slots, index)

            @pl.when(take)
            def _(at=at, kind=kind, index=index):
                kinds[offset * page_count + at] = kind
                indices[offset * page_count + at] = index

            at = at + jnp.where(take, 1, 0)
            size = size + jnp.where(take, jnp.minimum(page, tokens - j * page), 0)
        amounts[offset] = at
        sizes[offset] = size
        return carry

    lax.fori_loop(0, REQUESTS_PER_IDX, place_row, jnp.int32(0))


def score(scale, keys, query):
    return lax.dot_general(keys, query, HIDDEN, preferred_element_type=jnp.float32) * scale


def weigh(values, exponent):
    return lax.dot_general(
        values,
        exponent.astype(jnp.bfloat16),
        (((0,), (0,)), ((), ())),
        preferred_element_type=jnp.float32,
    )


def add_pages(scale, query, size, chunk, cached_kv, stats_ref, sums_ref):
    head_dim = query.shape[1]
    keys_at = lax.broadcasted_iota(jnp.int32, (chunk, query.shape[0]), 0)

    def chunk_step(step, carry):
        start = pl.multiple_of(step * chunk, chunk)
        scores = score(scale, cached_kv[pl.ds(start, chunk), :head_dim], query)
        scores = jnp.where(keys_at < size - start, scores, -jnp.inf)
        old = stats_ref[0:1, :]
        top = jnp.maximum(old, jnp.max(scores, axis=0, keepdims=True))
        fade = jnp.exp(old - top)
        exponent = jnp.exp(scores - top)
        stats_ref[0:1, :] = top
        stats_ref[1:2, :] = stats_ref[1:2, :] * fade + jnp.sum(exponent, axis=0, keepdims=True)
        sums_ref[...] = sums_ref[...] * fade + weigh(
            cached_kv[pl.ds(start, chunk), head_dim:], exponent
        )
        return carry

    lax.fori_loop(0, (size + chunk - 1) // chunk, chunk_step, jnp.int32(0))


def attend_kernel(scale, counts, limits_ref, place_ref, prefix_ref, pool_ref, *rest):
    gots = rest[: len(counts)]
    query_ref, fresh_ref, sums_ref, stats_ref = rest[len(counts) : len(counts) + 4]
    cached_kv, kinds, indices, amounts, sizes, ranks, sems = rest[len(counts) + 4 :]
    request, kv_head = pl.program_id(0), pl.program_id(1)
    per_kv, length, head_dim = query_ref.shape
    slots, page = pool_ref.shape[0], pool_ref.shape[2]
    page_count = place_ref.shape[1]

    @pl.when((request == 0) & (kv_head == 0))
    def _():
        cached_kv[...] = jnp.zeros_like(cached_kv)
        list_pages(
            counts, False, limits_ref, place_ref, prefix_ref, slots, page,
            kinds, indices, amounts, sizes, ranks,
        )

    amount = amounts[request]

    def target(j):
        return cached_kv.at[pl.ds(pl.multiple_of(j * page, page), page)]

    def start_copy(j, carry):
        entry = request * page_count + j
        for kind, source in enumerate(gots + (pool_ref,)):

            @pl.when(kinds[entry] == kind)
            def _(source=source):
                pltpu.make_async_copy(
                    source.at[indices[entry], kv_head], target(j), sems.at[j]
                ).start()

        return carry

    lax.fori_loop(0, amount, start_copy, jnp.int32(0))
    query = query_ref[...].reshape(per_kv * length, head_dim)
    keys_at = lax.broadcasted_iota(jnp.int32, (length, per_kv * length), 0)
    queries_at = lax.broadcasted_iota(jnp.int32, (length, per_kv * length), 1) % length
    scores = score(scale, fresh_ref[:, :head_dim], query)
    scores = jnp.where(keys_at <= queries_at, scores, -jnp.inf)
    top = jnp.max(scores, axis=0, keepdims=True)
    exponent = jnp.exp(scores - top)
    stats_ref[0:1, :] = top
    stats_ref[1:2, :] = jnp.sum(exponent, axis=0, keepdims=True)
    sums_ref[...] = weigh(fresh_ref[:, head_dim:], exponent)

    def wait_copy(j, carry):
        pltpu.make_async_copy(pool_ref.at[0, kv_head], target(j), sems.at[j]).wait()
        return carry

    lax.fori_loop(0, amount, wait_copy, jnp.int32(0))
    add_pages(scale, query, sizes[request], length, cached_kv, stats_ref, sums_ref)


def attend_passed_kernel(
    scale,
    counts,
    slots,
    limits_ref,
    place_ref,
    prefix_ref,
    passed_ref,
    query_ref,
    sums_in_ref,
    stats_in_ref,
    out_ref,
    cached_kv,
    sums_ref,
    stats_ref,
    kinds,
    indices,
    amounts,
    sizes,
    ranks,
    sems,
):
    request, kv_head = pl.program_id(0), pl.program_id(1)
    per_kv, length, head_dim = query_ref.shape
    page = passed_ref.shape[2]
    page_count = place_ref.shape[1]

    @pl.when((request == 0) & (kv_head == 0))
    def _():
        cached_kv[...] = jnp.zeros_like(cached_kv)
        list_pages(
            counts, True, limits_ref, place_ref, prefix_ref, slots, page,
            kinds, indices, amounts, sizes, ranks,
        )

    amount = amounts[request]

    def fetch(j, index):
        target = cached_kv.at[pl.ds(pl.multiple_of(j * page, page), page)]
        return pltpu.make_async_copy(passed_ref.at[index, kv_head], target, sems.at[j])

    def start_copy(j, carry):
        fetch(j, indices[request * page_count + j]).start()
        return carry

    def wait_copy(j, carry):
        fetch(j, 0).wait()
        return carry

    @pl.when(amount == 0)
    def _():
        out_ref[...] = (
            (sums_in_ref[...] / stats_in_ref[1:2, :]).T.astype(jnp.bfloat16).reshape(out_ref.shape)
        )

    @pl.when(amount > 0)
    def _():
        lax.fori_loop(0, amount, start_copy, jnp.int32(0))
        sums_ref[...] = sums_in_ref[...]
        stats_ref[...] = stats_in_ref[...]
        lax.fori_loop(0, amount, wait_copy, jnp.int32(0))
        query = query_ref[...].reshape(per_kv * length, head_dim)
        add_pages(scale, query, sizes[request], length, cached_kv, stats_ref, sums_ref)
        out_ref[...] = (
            (sums_ref[...] / stats_ref[1:2, :]).T.astype(jnp.bfloat16).reshape(out_ref.shape)
        )


def body(
    mixer_in,
    maps_in,
    delta_raw,
    conv_cache,
    maps_cache,
    conv_weight,
    maps_weight,
    decay_log,
    skip_gain,
    state_pool,
    queries,
    suffix_keyvals,
    page_pool,
    prefix_tokens,
    page_place,
    state_place,
    store_place,
):
    peers = lax.axis_size("req")
    me = lax.axis_index("req").astype(jnp.int32).reshape(1)
    requests, length = REQUESTS_PER_IDX, APPENDED_LENGTH
    groups = maps_in.shape[1]
    state = maps_in.shape[2] // 2
    heads = delta_raw.shape[1]
    per_group = heads // groups
    width = mixer_in.shape[1]
    group_width = width // groups
    head_dim = width // heads
    slots, _, page_rows, _ = state_pool.shape
    page_count = state_place.shape[1]
    kv_heads = page_pool.shape[2]
    attend_dim = queries.shape[2]
    per_kv = queries.shape[1] // kv_heads
    page = page_pool.shape[1]
    prefix_pages = page_place.shape[1]
    page_slots = page_pool.shape[0]
    pair_pages = requests * prefix_pages // peers
    taps = conv_weight.shape[0]

    def exchange(pages):
        return lax.all_to_all(pages, "req", split_axis=0, concat_axis=0, tiled=True)

    state_send = route_pages(gather_kernel, "gather_states", me, state_place, state_pool)
    state_got = exchange(state_send)

    counts = tuple(sorted({max(1, pair_pages * share // 16) for share in SHARES}))
    used = jnp.arange(prefix_pages)[None, :] * page < prefix_tokens[:, None]
    holders = page_place // page_slots
    pairs = used[:, :, None] & (holders[:, :, None] == jnp.arange(peers)[None, None, :])
    needs = jnp.sum(pairs.reshape(peers, -1, peers).astype(jnp.int32), axis=1)
    places = jnp.arange(peers)
    both = jnp.sum(needs.reshape(peers // 2, 2, peers), axis=1)
    outside = jnp.arange(peers // 2)[:, None] != places[None, :] // 2
    limit_table = jnp.array(counts, jnp.int32)
    crowded = jnp.max(jnp.where(outside, both, 0)) > 2 * limit_table
    rests = jnp.maximum(needs[None] - limit_table[:, None, None], 0)
    rests = jnp.where(places[:, None] != places[None, :], rests, 0)
    crowded = crowded | (jnp.max(jnp.sum(rests, axis=2), axis=1) > PASSED)
    choice = jnp.sum(crowded.astype(jnp.int32))
    limit = jnp.sum(jnp.where(jnp.arange(len(counts)) == choice, limit_table, 0))
    limits = jnp.stack([me[0], limit, choice])
    pages_by_head = page_pool.transpose(0, 2, 1, 3)
    page_sends = send_used(counts, limits, page_place, prefix_tokens, pages_by_head)

    delta = jax.nn.softplus(delta_raw.T.astype(jnp.float32)).reshape(heads, requests, length)
    log_decay = jnp.cumsum(-delta * jnp.exp(decay_log)[:, None, None], axis=2)
    tail = jnp.exp(log_decay[:, :, -1:] - log_decay) * delta
    growth = jnp.exp(log_decay)

    def by_rows(values):
        return values.reshape(groups, per_group, requests, length).transpose(2, 0, 1, 3)

    def by_columns(values):
        return values.reshape(groups, per_group, requests, length).transpose(2, 0, 3, 1)

    decay_row = by_rows(log_decay)
    maps_split = maps_in.transpose(1, 0, 2)
    empty = 8 - (taps - 1)
    x_cache = jnp.pad(conv_cache.astype(jnp.float32), ((0, 0), (empty, 0), (0, 0)))
    maps_edge = jnp.pad(
        maps_cache.transpose(0, 2, 1, 3).astype(jnp.float32), ((0, 0), (0, 0), (empty, 0), (0, 0))
    )
    row_block = pl.BlockSpec((None, None, per_group, length), lambda r, g: (r, g, 0, 0))
    column_block = pl.BlockSpec((None, None, length, per_group), lambda r, g: (r, g, 0, 0))
    x_block = pl.BlockSpec((length, group_width), lambda r, g: (r, g))
    update_block = pl.BlockSpec((None, None, group_width, state), lambda r, g: (r, g, 0, 0))
    map_block = pl.BlockSpec((None, length, state), lambda r, g: (g, r, 0))
    partial, update, output_map = pl.pallas_call(
        functools.partial(inner_kernel, per_group),
        grid=(requests, groups),
        in_specs=[
            x_block,
            pl.BlockSpec((None, 8, group_width), lambda r, g: (r, 0, g)),
            pl.BlockSpec((taps, group_width), lambda r, g: (0, g)),
            pl.BlockSpec((None, length, 2 * state), lambda r, g: (g, r, 0)),
            pl.BlockSpec((None, None, 8, 2 * state), lambda r, g: (r, g, 0, 0)),
            pl.BlockSpec((None, taps, 2 * state), lambda r, g: (g, 0, 0)),
            row_block,
            column_block,
            row_block,
            column_block,
            pl.BlockSpec((1, group_width), lambda r, g: (0, g)),
        ],
        out_specs=[x_block, update_block, map_block],
        out_shape=[
            jax.ShapeDtypeStruct((requests * length, width), jnp.float32),
            jax.ShapeDtypeStruct((requests, groups, group_width, state), jnp.float32),
            jax.ShapeDtypeStruct((groups, requests * length, state), jnp.bfloat16),
        ],
        scratch_shapes=[
            pltpu.VMEM((8 + length, group_width), jnp.float32),
            pltpu.VMEM((8 + length, 2 * state), jnp.float32),
            pltpu.VMEM((length, group_width), jnp.bfloat16),
            pltpu.VMEM((length, group_width), jnp.bfloat16),
        ],
        cost_estimate=pl.CostEstimate(
            flops=3 * requests * length * width * state,
            bytes_accessed=32 * 2**20,
            transcendentals=requests * heads * length * length,
        ),
        compiler_params=params(),
        name="mix_new_tokens",
    )(
        mixer_in,
        x_cache,
        conv_weight.astype(jnp.float32),
        maps_split,
        maps_edge,
        maps_weight.transpose(1, 0, 2).astype(jnp.float32),
        decay_row,
        by_columns(log_decay),
        by_rows(delta),
        by_columns(tail),
        jnp.repeat(skip_gain, head_dim).reshape(1, width),
    )
    growth_col = by_columns(growth)
    grouped_queries = queries.reshape(requests, length, kv_heads, per_kv, attend_dim).transpose(
        0, 2, 3, 1, 4
    )
    fresh = suffix_keyvals.transpose(1, 0, 2)

    first_send, state_got, partial, update, output_map, growth_col, decay_row = (
        lax.optimization_barrier(
            (page_sends[0], state_got, partial, update, output_map, growth_col, decay_row)
        )
    )
    first_got = exchange(first_send)
    more_sends = lax.optimization_barrier((first_got, page_sends[1:]))[1]
    more_shapes = [pltpu.HBM(sent.shape, sent.dtype) for sent in more_sends]

    def no_more(sends):
        return tuple(unwritten(more_shapes))

    def send_more(at, sends):
        gots = list(unwritten(more_shapes[:at] + more_shapes[at + 1 :]))
        return tuple(gots[:at] + [exchange(sends[at])] + gots[at:])

    more_gots = lax.switch(
        choice,
        [no_more] + [functools.partial(send_more, at) for at in range(len(more_shapes))],
        more_sends,
    )
    page_gots = (first_got,) + tuple(more_gots)
    mixer_out, final_send = pl.pallas_call(
        state_kernel,
        grid_spec=pltpu.PrefetchScalarGridSpec(
            num_scalar_prefetch=3,
            grid=(requests, groups),
            in_specs=[
                any_spec(),
                pl.BlockSpec((None, None, group_width, state), lambda r, g, *_: (r, g, 0, 0)),
                pl.BlockSpec((length, group_width), lambda r, g, *_: (r, g)),
                pl.BlockSpec((None, length, state), lambda r, g, *_: (g, r, 0)),
                pl.BlockSpec((None, None, length, per_group), lambda r, g, *_: (r, g, 0, 0)),
                pl.BlockSpec((None, None, per_group, length), lambda r, g, *_: (r, g, 0, 0)),
            ],
            out_specs=[
                pl.BlockSpec((length, group_width), lambda r, g, *_: (r, g)),
                hbm_spec(),
            ],
            scratch_shapes=[
                pltpu.VMEM((page_count, per_group, page_rows, state), jnp.bfloat16),
                pltpu.VMEM((page_count, per_group, page_rows, state), jnp.bfloat16),
                pltpu.VMEM((group_width, state), jnp.float32),
                pltpu.SMEM((requests * page_count,), jnp.int32),
                pltpu.SMEM((requests * page_count,), jnp.int32),
                pltpu.SMEM((peers,), jnp.int32),
                pltpu.SemaphoreType.DMA((page_count,)),
                pltpu.SemaphoreType.DMA((page_count,)),
            ],
        ),
        out_shape=[
            jax.ShapeDtypeStruct((requests * length, width), jnp.bfloat16),
            pltpu.HBM(state_pool.shape, jnp.bfloat16),
        ],
        cost_estimate=pl.CostEstimate(
            flops=2 * requests * length * width * state,
            bytes_accessed=32 * 2**20,
            transcendentals=0,
        ),
        compiler_params=params(),
        name="advance_states",
    )(
        me,
        state_place,
        store_place,
        state_got,
        update,
        partial,
        output_map,
        growth_col,
        decay_row,
    )
    final_send, page_gots = lax.optimization_barrier((final_send, page_gots))
    final_got = exchange(final_send)
    passed = pass_on(counts, limits, page_place, prefix_tokens, pages_by_head, page_gots)
    rows = per_kv * length
    head_block = pl.BlockSpec(
        (None, None, per_kv, length, attend_dim), lambda r, e, *_: (r, e, 0, 0, 0)
    )
    sums_block = pl.BlockSpec((None, None, attend_dim, rows), lambda r, e, *_: (r, e, 0, 0))
    stats_block = pl.BlockSpec((None, None, 2, rows), lambda r, e, *_: (r, e, 0, 0))
    lists = [
        pltpu.SMEM((requests * prefix_pages,), jnp.int32),
        pltpu.SMEM((requests * prefix_pages,), jnp.int32),
        pltpu.SMEM((requests,), jnp.int32),
        pltpu.SMEM((requests,), jnp.int32),
        pltpu.SMEM((2, peers), jnp.int32),
    ]
    sums, stats = pl.pallas_call(
        functools.partial(attend_kernel, attend_dim**-0.5, counts),
        grid_spec=pltpu.PrefetchScalarGridSpec(
            num_scalar_prefetch=3,
            grid=(requests, kv_heads),
            in_specs=[any_spec()] * (len(page_gots) + 1)
            + [
                head_block,
                pl.BlockSpec((None, length, 2 * attend_dim), lambda r, e, *_: (e, r, 0)),
            ],
            out_specs=[sums_block, stats_block],
            scratch_shapes=[
                pltpu.VMEM((prefix_pages * page, 2 * attend_dim), jnp.bfloat16),
                *lists,
                pltpu.SemaphoreType.DMA((prefix_pages,)),
            ],
        ),
        out_shape=[
            jax.ShapeDtypeStruct((requests, kv_heads, attend_dim, rows), jnp.float32),
            jax.ShapeDtypeStruct((requests, kv_heads, 2, rows), jnp.float32),
        ],
        cost_estimate=pl.CostEstimate(
            flops=4 * queries.size * (prefix_pages * page + length),
            bytes_accessed=16 * 2**20,
            transcendentals=queries.shape[0] * queries.shape[1] * (prefix_pages * page),
        ),
        compiler_params=params(),
        name="attend",
    )(
        limits,
        page_place,
        prefix_tokens,
        pages_by_head,
        *page_gots,
        grouped_queries,
        fresh,
    )
    attended = pl.pallas_call(
        functools.partial(attend_passed_kernel, attend_dim**-0.5, counts, page_slots),
        grid_spec=pltpu.PrefetchScalarGridSpec(
            num_scalar_prefetch=3,
            grid=(requests, kv_heads),
            in_specs=[any_spec(), head_block, sums_block, stats_block],
            out_specs=head_block,
            scratch_shapes=[
                pltpu.VMEM((-(-PASSED * page // length) * length, 2 * attend_dim), jnp.bfloat16),
                pltpu.VMEM((attend_dim, rows), jnp.float32),
                pltpu.VMEM((2, rows), jnp.float32),
                *lists,
                pltpu.SemaphoreType.DMA((PASSED,)),
            ],
        ),
        out_shape=jax.ShapeDtypeStruct(grouped_queries.shape, jnp.bfloat16),
        cost_estimate=pl.CostEstimate(
            flops=queries.size * PASSED * page,
            bytes_accessed=8 * 2**20,
            transcendentals=queries.shape[0] * queries.shape[1] * PASSED * page // 4,
        ),
        compiler_params=params(),
        name="attend_passed",
    )(limits, page_place, prefix_tokens, passed, grouped_queries, sums, stats)
    attention_out = attended.transpose(0, 3, 1, 2, 4).reshape(queries.shape)
    stored = route_pages(scatter_kernel, "scatter_states", me, store_place, final_got)
    return mixer_out, attention_out, stored


def solution(mesh):
    placed = (
        P(("parts", "req"), "tp"),
        P(("parts", "req"), "tp", None),
        P(("parts", "req"), "tp"),
        P(("parts", "req"), None, "tp"),
        P(("parts", "req"), None, "tp", None),
        P(None, "tp"),
        P(None, "tp", None),
        P("tp"),
        P("tp"),
        P(("parts", "req"), "tp", None, None),
        P(("parts", "req"), "tp", None),
        P(("parts", "req"), "tp", None),
        P(("parts", "req"), None, "tp", None),
        P("parts"),
        P("parts", None),
        P("parts", None),
        P("parts", None),
    )
    return jax.shard_map(
        body,
        mesh=mesh,
        in_specs=placed,
        out_specs=(
            P(("parts", "req"), "tp"),
            P(("parts", "req"), "tp", None),
            P(("parts", "req"), "tp", None, None),
        ),
        check_vma=False,
    )
```

```python
import functools

import jax
import jax.numpy as jnp
from jax import lax
from jax.experimental import pallas as pl
from jax.experimental.pallas import tpu as pltpu
from jax.sharding import PartitionSpec as P

APPENDED_LENGTH = 256
REQUESTS_PER_IDX = 4
VMEM_LIMIT = 48 * 1024 * 1024
SHARES = (6, 7, 8, 9, 10, 11, 16)
PASSED = 8
HIDDEN = (((1,), (1,)), ((), ()))


def params():
    return pltpu.CompilerParams(vmem_limit_bytes=VMEM_LIMIT)


def any_spec():
    return pl.BlockSpec(memory_space=pl.ANY)


def hbm_spec():
    return pl.BlockSpec(memory_space=pltpu.HBM)


def own_entries(place_ref, base, slots, position, row, emit):
    for j in range(place_ref.shape[1]):
        slot = place_ref[row, j] - base
        mine = (slot >= 0) & (slot < slots)

        @pl.when(mine)
        def _(slot=slot, position=position, j=j):
            emit(position, slot)

        position = position + jnp.where(mine, 1, 0)
    return position


def gather_kernel(capacity, me_ref, place_ref, pool_ref, out_ref, staged, in_sems, out_sems):
    slots = pool_ref.shape[0]
    base = me_ref[0] * slots
    servers = place_ref.shape[0] // REQUESTS_PER_IDX

    def server_step(server, carry):
        def row_step(offset, position):
            def emit(at, slot):
                pltpu.make_async_copy(
                    pool_ref.at[slot], staged.at[server * capacity + at], in_sems.at[server]
                ).start()

            row = server * REQUESTS_PER_IDX + offset
            return own_entries(place_ref, base, slots, position, row, emit)

        lax.fori_loop(0, REQUESTS_PER_IDX, row_step, jnp.int32(0))
        return carry

    lax.fori_loop(0, servers, server_step, jnp.int32(0))

    def part(server):
        return pl.ds(pl.multiple_of(server * capacity, capacity), capacity)

    def forward(server, carry):
        pltpu.make_async_copy(
            pool_ref.at[part(0)], staged.at[part(server)], in_sems.at[server]
        ).wait()
        pltpu.make_async_copy(
            staged.at[part(server)], out_ref.at[part(server)], out_sems.at[server]
        ).start()
        return carry

    lax.fori_loop(0, servers, forward, jnp.int32(0))

    def finish(server, carry):
        pltpu.make_async_copy(
            staged.at[part(server)], out_ref.at[part(server)], out_sems.at[server]
        ).wait()
        return carry

    lax.fori_loop(0, servers, finish, jnp.int32(0))


def scatter_kernel(capacity, me_ref, place_ref, got_ref, out_ref, staged, in_sems, out_sems):
    slots = out_ref.shape[0]
    base = me_ref[0] * slots
    servers = place_ref.shape[0] // REQUESTS_PER_IDX

    def fetch(server):
        part = pl.ds(pl.multiple_of(server * capacity, capacity), capacity)
        return pltpu.make_async_copy(got_ref.at[part], staged.at[part], in_sems.at[server])

    def start_fetch(server, carry):
        fetch(server).start()
        return carry

    lax.fori_loop(0, servers, start_fetch, jnp.int32(0))

    def server_step(server, carry):
        fetch(server).wait()

        def row_step(offset, position):
            def emit(at, slot):
                pltpu.make_async_copy(
                    staged.at[server * capacity + at], out_ref.at[slot], out_sems.at[0]
                ).start()

            row = server * REQUESTS_PER_IDX + offset
            return own_entries(place_ref, base, slots, position, row, emit)

        lax.fori_loop(0, REQUESTS_PER_IDX, row_step, jnp.int32(0))
        return carry

    lax.fori_loop(0, servers, server_step, jnp.int32(0))
    pltpu.make_async_copy(staged, out_ref, out_sems.at[0]).wait()


def route_pages(kernel, name, me, place, pages):
    servers = lax.axis_size("req")
    capacity = pages.shape[0] // servers
    size = pages.size * pages.dtype.itemsize
    return pl.pallas_call(
        functools.partial(kernel, capacity),
        out_shape=pltpu.HBM(pages.shape, pages.dtype),
        grid_spec=pltpu.PrefetchScalarGridSpec(
            num_scalar_prefetch=2,
            grid=(1,),
            in_specs=[hbm_spec()],
            out_specs=hbm_spec(),
            scratch_shapes=[
                pltpu.VMEM(pages.shape, pages.dtype),
                pltpu.SemaphoreType.DMA((servers,)),
                pltpu.SemaphoreType.DMA((servers,)),
            ],
        ),
        cost_estimate=pl.CostEstimate(flops=0, bytes_accessed=2 * size, transcendentals=0),
        compiler_params=params(),
        name=name,
    )(me, place, pltpu.with_memory_space_constraint(pages, pltpu.HBM))


def used_entry(place_ref, prefix_ref, page, slots, owner, row, j):
    slot = place_ref[row, j] - owner * slots
    return slot, (slot >= 0) & (slot < slots) & (j * page < prefix_ref[row])


def count_used(place_ref, entry, owner, server):
    def count_row(offset, total):
        for j in range(place_ref.shape[1]):
            _, wanted = entry(owner, server * REQUESTS_PER_IDX + offset, j)
            total = total + jnp.where(wanted, 1, 0)
        return total

    return lax.fori_loop(0, REQUESTS_PER_IDX, count_row, jnp.int32(0))


def partner_of(device):
    return device + 1 - 2 * (device % 2)


def send_kernel(counts, limits_ref, place_ref, prefix_ref, pool_ref, *rest):
    outs, (staged, needs, filled, in_sems, out_sems) = rest[: len(counts)], rest[len(counts) :]
    slots, page = pool_ref.shape[0], pool_ref.shape[2]
    me, limit, choice = limits_ref[0], limits_ref[1], limits_ref[2]
    columns = place_ref.shape[1]
    servers, room = staged.shape[:2]
    entry = functools.partial(used_entry, place_ref, prefix_ref, page, slots)

    def count_server(server, carry):
        needs[server] = count_used(place_ref, entry, me, server)
        return carry

    lax.fori_loop(0, servers, count_server, jnp.int32(0))

    def fetch(slot, server, position):
        return pltpu.make_async_copy(
            pool_ref.at[slot], staged.at[server, position], in_sems.at[server, position]
        )

    def fetch_server(server, carry):
        partner = partner_of(server)
        start = needs[partner] - limit

        def fetch_row(offset, rank):
            for j in range(columns):
                slot, wanted = entry(me, server * REQUESTS_PER_IDX + offset, j)
                wanted = wanted & (server != me)
                direct = rank < limit

                @pl.when(wanted & (direct | (partner != me)))
                def _(slot=slot, rank=rank, direct=direct):
                    fetch(
                        slot,
                        jnp.where(direct, server, partner),
                        jnp.where(direct, rank, start + rank),
                    ).start()

                rank = rank + jnp.where(wanted, 1, 0)
            return rank

        lax.fori_loop(0, REQUESTS_PER_IDX, fetch_row, jnp.int32(0))
        passed = jnp.where(partner == me, 0, jnp.maximum(needs[partner] - limit, 0))
        own = jnp.minimum(needs[server], limit)
        filled[server] = jnp.where(server == me, 0, own + passed)
        return carry

    lax.fori_loop(0, servers, fetch_server, jnp.int32(0))

    def forward(server, option):
        count = counts[option]
        return pltpu.make_async_copy(
            staged.at[server, pl.ds(0, count)],
            outs[option].at[pl.ds(server * count, count)],
            out_sems.at[server],
        )

    def forward_server(server, carry):
        for position in range(room):

            @pl.when(position < filled[server])
            def _(position=position):
                fetch(0, server, position).wait()

        for option in range(len(counts)):

            @pl.when(choice == option)
            def _(option=option):
                forward(server, option).start()

        return carry

    lax.fori_loop(0, servers, forward_server, jnp.int32(0))

    def finish_server(server, carry):
        for option in range(len(counts)):

            @pl.when(choice == option)
            def _(option=option):
                forward(server, option).wait()

        return carry

    lax.fori_loop(0, servers, finish_server, jnp.int32(0))


def send_used(counts, limits, place, prefix, pages):
    servers = lax.axis_size("req")
    shapes = [
        pltpu.HBM((servers * count,) + pages.shape[1:], pages.dtype) for count in counts
    ]
    return pl.pallas_call(
        functools.partial(send_kernel, counts),
        out_shape=shapes,
        grid_spec=pltpu.PrefetchScalarGridSpec(
            num_scalar_prefetch=3,
            grid=(1,),
            in_specs=[any_spec()],
            out_specs=[hbm_spec()] * len(counts),
            scratch_shapes=[
                pltpu.VMEM((servers, counts[-1]) + pages.shape[1:], pages.dtype),
                pltpu.SMEM((servers,), jnp.int32),
                pltpu.SMEM((servers,), jnp.int32),
                pltpu.SemaphoreType.DMA((servers, counts[-1])),
                pltpu.SemaphoreType.DMA((servers,)),
            ],
        ),
        cost_estimate=pl.CostEstimate(
            flops=0, bytes_accessed=2 * pages.size * 2, transcendentals=0
        ),
        compiler_params=params(),
        name="send_used_pages",
    )(limits, place, prefix, pages)


def pass_kernel(counts, limits_ref, place_ref, prefix_ref, pool_ref, *rest):
    gots, (out_ref, staged, in_sems, out_sem) = rest[: len(counts)], rest[len(counts) :]
    slots, page = pool_ref.shape[0], pool_ref.shape[2]
    me, limit, choice = limits_ref[0], limits_ref[1], limits_ref[2]
    columns = place_ref.shape[1]
    servers = place_ref.shape[0] // REQUESTS_PER_IDX
    partner = partner_of(me)
    entry = functools.partial(used_entry, place_ref, prefix_ref, page, slots)

    def fetch(source, index, at):
        return pltpu.make_async_copy(source.at[index], staged.at[at], in_sems.at[at])

    def own_pages(at):
        def row_step(offset, carry):
            rank, at = carry
            for j in range(columns):
                slot, wanted = entry(me, partner * REQUESTS_PER_IDX + offset, j)
                take = wanted & (rank >= limit)

                @pl.when(take)
                def _(slot=slot, at=at):
                    fetch(pool_ref, slot, at).start()

                rank = rank + jnp.where(wanted, 1, 0)
                at = at + jnp.where(take, 1, 0)
            return rank, at

        return lax.fori_loop(0, REQUESTS_PER_IDX, row_step, (jnp.int32(0), at))[1]

    def relayed_pages(owner, at):
        start = count_used(place_ref, entry, owner, me)
        more = jnp.maximum(count_used(place_ref, entry, owner, partner) - limit, 0)

        def page_step(step, carry):
            index = owner * limit + start + step
            for option in range(len(counts)):

                @pl.when(choice == option)
                def _(option=option):
                    fetch(gots[option], index, at + step).start()

            return carry

        lax.fori_loop(0, more, page_step, jnp.int32(0))
        return at + more

    def owner_step(owner, at):
        at = lax.cond(owner == me, own_pages, lambda at: at, at)
        outside = (owner != me) & (owner != partner)
        return lax.cond(outside, lambda at: relayed_pages(owner, at), lambda at: at, at)

    total = lax.fori_loop(0, servers, owner_step, jnp.int32(0))
    for position in range(staged.shape[0]):

        @pl.when(position < total)
        def _(position=position):
            fetch(pool_ref, 0, position).wait()

    forward = pltpu.make_async_copy(staged, out_ref, out_sem)
    forward.start()
    forward.wait()


def pass_on(counts, limits, place, prefix, pages, gots):
    shape = (PASSED,) + pages.shape[1:]
    collected = pl.pallas_call(
        functools.partial(pass_kernel, counts),
        out_shape=pltpu.HBM(shape, pages.dtype),
        grid_spec=pltpu.PrefetchScalarGridSpec(
            num_scalar_prefetch=3,
            grid=(1,),
            in_specs=[any_spec()] * (1 + len(gots)),
            out_specs=hbm_spec(),
            scratch_shapes=[
                pltpu.VMEM(shape, pages.dtype),
                pltpu.SemaphoreType.DMA((PASSED,)),
                pltpu.SemaphoreType.DMA,
            ],
        ),
        cost_estimate=pl.CostEstimate(flops=0, bytes_accessed=2**20, transcendentals=0),
        compiler_params=params(),
        name="pass_pages_on",
    )(limits, place, prefix, pages, *gots)
    swaps = [(peer, peer ^ 1) for peer in range(lax.axis_size("req"))]
    return lax.ppermute(collected, "req", swaps)


def unwritten(shapes):
    return pl.pallas_call(
        lambda *refs: None,
        out_shape=shapes,
        out_specs=[hbm_spec()] * len(shapes),
        cost_estimate=pl.CostEstimate(flops=0, bytes_accessed=0, transcendentals=0),
        name="unwritten",
    )()


def conv_silu(buffer, cache_ref, values, weight_ref):
    length = values.shape[0]
    taps = weight_ref.shape[-2]
    buffer[0:8, :] = cache_ref[...]
    buffer[8:, :] = values.astype(jnp.float32)
    start = 8 - (taps - 1)
    summed = weight_ref[0:1, :] * buffer[start : start + length, :]
    for tap in range(1, taps):
        at = start + tap
        summed = summed + weight_ref[tap : tap + 1, :] * buffer[at : at + length, :]
    return jax.nn.silu(summed).astype(jnp.bfloat16)


def inner_kernel(
    heads,
    x_ref,
    x_cache_ref,
    x_weight_ref,
    maps_ref,
    maps_cache_ref,
    maps_weight_ref,
    decay_row_ref,
    decay_col_ref,
    delta_row_ref,
    tail_ref,
    skip_ref,
    partial_ref,
    update_ref,
    output_map_ref,
    x_buffer,
    maps_buffer,
    x_values,
    scaled,
):
    length, width = x_ref.shape
    head_dim = width // heads
    state = maps_ref.shape[1] // 2
    x_values[...] = conv_silu(x_buffer, x_cache_ref, x_ref[...], x_weight_ref)
    maps = conv_silu(maps_buffer, maps_cache_ref, maps_ref[...], maps_weight_ref)
    input_map, output_map = maps[:, :state], maps[:, state:]
    output_map_ref[...] = output_map
    intersection = lax.dot_general(
        output_map, input_map, HIDDEN, preferred_element_type=jnp.float32
    )
    rows = lax.broadcasted_iota(jnp.int32, (length, length), 0)
    columns = lax.broadcasted_iota(jnp.int32, (length, length), 1)
    causal = rows >= columns
    for h in range(heads):
        lanes = slice(h * head_dim, (h + 1) * head_dim)
        gap = decay_col_ref[:, h : h + 1] - decay_row_ref[h : h + 1, :]
        decays = jnp.where(causal, jnp.exp(jnp.where(causal, gap, 0.0)), 0.0)
        mixing = (intersection * decays * delta_row_ref[h : h + 1, :]).astype(jnp.bfloat16)
        x_head = x_values[:, lanes]
        x_wide = x_head.astype(jnp.float32)
        within = jnp.dot(mixing, x_head, preferred_element_type=jnp.float32)
        partial_ref[:, lanes] = within + skip_ref[:, lanes] * x_wide
        scaled[:, lanes] = (x_wide * tail_ref[:, h : h + 1]).astype(jnp.bfloat16)
    update_ref[...] = lax.dot_general(
        scaled[...], input_map, (((0,), (0,)), ((), ())), preferred_element_type=jnp.float32
    )


def state_kernel(
    me_ref,
    state_place_ref,
    store_place_ref,
    got_ref,
    update_ref,
    decay_row_ref,
    prior_ref,
    send_ref,
    pages,
    finals,
    arrival,
    departure,
    counts,
    in_sems,
    out_sems,
):
    request, group = pl.program_id(0), pl.program_id(1)
    page_count, heads, page_rows, state = pages.shape
    entries = REQUESTS_PER_IDX * page_count
    slots = got_ref.shape[0]
    peers = counts.shape[0]
    capacity = entries // peers
    head_dim = page_count * page_rows
    joint = 16 // page_rows

    @pl.when((request == 0) & (group == 0))
    def _():
        for place_ref, found in ((state_place_ref, arrival), (store_place_ref, departure)):
            for peer in range(peers):
                counts[peer] = 0

            def row_step(offset, carry, place_ref=place_ref, found=found):
                for j in range(page_count):
                    owner = place_ref[me_ref[0] * REQUESTS_PER_IDX + offset, j] // slots
                    rank = counts[owner]
                    counts[owner] = rank + 1
                    found[offset * page_count + j] = owner * capacity + rank
                return carry

            lax.fori_loop(0, REQUESTS_PER_IDX, row_step, jnp.int32(0))

    half = pl.ds(group * heads, heads)

    def arrive(j):
        return pltpu.make_async_copy(
            got_ref.at[arrival[request * page_count + j], half], pages.at[j], in_sems.at[j]
        )

    def depart(j):
        return pltpu.make_async_copy(
            finals.at[j], send_ref.at[departure[request * page_count + j], half], out_sems.at[j]
        )

    def each(start, end, act):
        def step(j, carry):
            act(j)
            return carry

        lax.fori_loop(start, end, step, jnp.int32(0))

    each(0, page_count, lambda j: arrive(j).start())
    last = decay_row_ref.shape[1] - 1
    growths = [jnp.exp(decay_row_ref[h : h + 1, last : last + 1]) for h in range(heads)]

    def joint_step(step, carry):
        first = step * joint
        each(first, first + joint, lambda j: arrive(j).wait())
        for h in range(heads):
            rows = pl.ds(pl.multiple_of(h * head_dim + step * 16, 16), 16)
            old = jnp.concatenate(
                [pages[first + i, h].astype(jnp.float32) for i in range(joint)], axis=0
            )
            prior_ref[rows, :] = old.astype(jnp.bfloat16)
            new = growths[h] * old + update_ref[rows, :]
            for i in range(joint):
                finals[first + i, h] = new[i * page_rows : (i + 1) * page_rows].astype(
                    jnp.bfloat16
                )
        each(first, first + joint, lambda j: depart(j).start())
        return carry

    lax.fori_loop(0, page_count // joint, joint_step, jnp.int32(0))
    each(0, page_count, lambda j: depart(j).wait())


def output_kernel(heads, partial_ref, output_map_ref, growth_ref, prior_ref, out_ref):
    head_dim = out_ref.shape[1] // heads
    carried = lax.dot_general(
        output_map_ref[...], prior_ref[...], HIDDEN, preferred_element_type=jnp.float32
    )
    for h in range(heads):
        lanes = slice(h * head_dim, (h + 1) * head_dim)
        out_ref[:, lanes] = (
            partial_ref[:, lanes] + growth_ref[:, h : h + 1] * carried[:, lanes]
        ).astype(jnp.bfloat16)


def list_pages(
    counts, passed, limits_ref, place_ref, prefix_ref, slots, page, kinds, indices, amounts, sizes, ranks
):
    me, limit, choice = limits_ref[0], limits_ref[1], limits_ref[2]
    page_count = place_ref.shape[1]
    peers = ranks.shape[1]
    start_row = me * REQUESTS_PER_IDX
    for peer in range(peers):
        ranks[0, peer] = 0
    if passed:

        def count_row(offset, carry):
            tokens = prefix_ref[start_row + offset]
            for j in range(page_count):
                owner = place_ref[start_row + offset, j] // slots
                ranks[0, owner] = ranks[0, owner] + jnp.where(j * page < tokens, 1, 0)
            return carry

        lax.fori_loop(0, REQUESTS_PER_IDX, count_row, jnp.int32(0))
        begin = jnp.int32(0)
        for peer in range(peers):
            ranks[1, peer] = begin
            begin = begin + jnp.where(peer == me, 0, jnp.maximum(ranks[0, peer] - limit, 0))
            ranks[0, peer] = 0
    def place_row(offset, carry):
        tokens = prefix_ref[start_row + offset]
        at, size = jnp.int32(0), jnp.int32(0)
        for j in range(page_count):
            place = place_ref[start_row + offset, j]
            owner = place // slots
            rank = ranks[0, owner]
            used = j * page < tokens
            ranks[0, owner] = rank + jnp.where(used, 1, 0)
            here = owner == me
            late = (rank >= limit) & jnp.logical_not(here)
            if passed:
                take = used & late
                kind = jnp.int32(0)
                index = ranks[1, owner] + rank - limit
            else:
                take = used & jnp.logical_not(late)
                kind = jnp.where(here, len(counts), choice)
                index = jnp.where(here, place - me * slots, owner * limit + rank)

            @pl.when(take)
            def _(at=at, kind=kind, index=index):
                kinds[offset * page_count + at] = kind
                indices[offset * page_count + at] = index

            at = at + jnp.where(take, 1, 0)
            size = size + jnp.where(take, jnp.minimum(page, tokens - j * page), 0)
        amounts[offset] = at
        sizes[offset] = size
        return carry

    lax.fori_loop(0, REQUESTS_PER_IDX, place_row, jnp.int32(0))


def score(scale, keys, query):
    return lax.dot_general(keys, query, HIDDEN, preferred_element_type=jnp.float32) * scale


def weigh(values, exponent):
    return lax.dot_general(
        values,
        exponent.astype(jnp.bfloat16),
        (((0,), (0,)), ((), ())),
        preferred_element_type=jnp.float32,
    )


def add_pages(scale, query, size, chunk, cached_kv, stats_ref, sums_ref):
    head_dim = query.shape[1]
    keys_at = lax.broadcasted_iota(jnp.int32, (chunk, query.shape[0]), 0)

    def chunk_step(step, carry):
        start = pl.multiple_of(step * chunk, chunk)
        scores = score(scale, cached_kv[pl.ds(start, chunk), :head_dim], query)
        scores = jnp.where(keys_at < size - start, scores, -jnp.inf)
        old = stats_ref[0:1, :]
        top = jnp.maximum(old, jnp.max(scores, axis=0, keepdims=True))
        fade = jnp.exp(old - top)
        exponent = jnp.exp(scores - top)
        stats_ref[0:1, :] = top
        stats_ref[1:2, :] = stats_ref[1:2, :] * fade + jnp.sum(exponent, axis=0, keepdims=True)
        sums_ref[...] = sums_ref[...] * fade + weigh(
            cached_kv[pl.ds(start, chunk), head_dim:], exponent
        )
        return carry

    lax.fori_loop(0, (size + chunk - 1) // chunk, chunk_step, jnp.int32(0))


def attend_kernel(scale, counts, limits_ref, place_ref, prefix_ref, pool_ref, *rest):
    gots = rest[: len(counts)]
    query_ref, fresh_ref, sums_ref, stats_ref = rest[len(counts) : len(counts) + 4]
    cached_kv, kinds, indices, amounts, sizes, ranks, sems = rest[len(counts) + 4 :]
    request, kv_head = pl.program_id(0), pl.program_id(1)
    per_kv, length, head_dim = query_ref.shape
    slots, page = pool_ref.shape[0], pool_ref.shape[2]
    page_count = place_ref.shape[1]

    @pl.when((request == 0) & (kv_head == 0))
    def _():
        cached_kv[...] = jnp.zeros_like(cached_kv)
        list_pages(
            counts, False, limits_ref, place_ref, prefix_ref, slots, page,
            kinds, indices, amounts, sizes, ranks,
        )

    amount = amounts[request]

    def target(j):
        return cached_kv.at[pl.ds(pl.multiple_of(j * page, page), page)]

    def start_copy(j, carry):
        entry = request * page_count + j
        for kind, source in enumerate(gots + (pool_ref,)):

            @pl.when(kinds[entry] == kind)
            def _(source=source):
                pltpu.make_async_copy(
                    source.at[indices[entry], kv_head], target(j), sems.at[j]
                ).start()

        return carry

    lax.fori_loop(0, amount, start_copy, jnp.int32(0))
    query = query_ref[...].reshape(per_kv * length, head_dim)
    keys_at = lax.broadcasted_iota(jnp.int32, (length, per_kv * length), 0)
    queries_at = lax.broadcasted_iota(jnp.int32, (length, per_kv * length), 1) % length
    scores = score(scale, fresh_ref[:, :head_dim], query)
    scores = jnp.where(keys_at <= queries_at, scores, -jnp.inf)
    top = jnp.max(scores, axis=0, keepdims=True)
    exponent = jnp.exp(scores - top)
    stats_ref[0:1, :] = top
    stats_ref[1:2, :] = jnp.sum(exponent, axis=0, keepdims=True)
    sums_ref[...] = weigh(fresh_ref[:, head_dim:], exponent)

    def wait_copy(j, carry):
        pltpu.make_async_copy(pool_ref.at[0, kv_head], target(j), sems.at[j]).wait()
        return carry

    lax.fori_loop(0, amount, wait_copy, jnp.int32(0))
    add_pages(scale, query, sizes[request], length, cached_kv, stats_ref, sums_ref)


def attend_passed_kernel(
    scale,
    counts,
    slots,
    limits_ref,
    place_ref,
    prefix_ref,
    passed_ref,
    query_ref,
    sums_in_ref,
    stats_in_ref,
    out_ref,
    cached_kv,
    sums_ref,
    stats_ref,
    kinds,
    indices,
    amounts,
    sizes,
    ranks,
    sems,
):
    request, kv_head = pl.program_id(0), pl.program_id(1)
    per_kv, length, head_dim = query_ref.shape
    page = passed_ref.shape[2]
    page_count = place_ref.shape[1]

    @pl.when((request == 0) & (kv_head == 0))
    def _():
        cached_kv[...] = jnp.zeros_like(cached_kv)
        list_pages(
            counts, True, limits_ref, place_ref, prefix_ref, slots, page,
            kinds, indices, amounts, sizes, ranks,
        )

    amount = amounts[request]

    def fetch(j, index):
        target = cached_kv.at[pl.ds(pl.multiple_of(j * page, page), page)]
        return pltpu.make_async_copy(passed_ref.at[index, kv_head], target, sems.at[j])

    def start_copy(j, carry):
        fetch(j, indices[request * page_count + j]).start()
        return carry

    def wait_copy(j, carry):
        fetch(j, 0).wait()
        return carry

    @pl.when(amount == 0)
    def _():
        out_ref[...] = (
            (sums_in_ref[...] / stats_in_ref[1:2, :]).T.astype(jnp.bfloat16).reshape(out_ref.shape)
        )

    @pl.when(amount > 0)
    def _():
        lax.fori_loop(0, amount, start_copy, jnp.int32(0))
        sums_ref[...] = sums_in_ref[...]
        stats_ref[...] = stats_in_ref[...]
        lax.fori_loop(0, amount, wait_copy, jnp.int32(0))
        query = query_ref[...].reshape(per_kv * length, head_dim)
        add_pages(scale, query, sizes[request], length, cached_kv, stats_ref, sums_ref)
        out_ref[...] = (
            (sums_ref[...] / stats_ref[1:2, :]).T.astype(jnp.bfloat16).reshape(out_ref.shape)
        )


def body(
    mixer_in,
    maps_in,
    delta_raw,
    conv_cache,
    maps_cache,
    conv_weight,
    maps_weight,
    decay_log,
    skip_gain,
    state_pool,
    queries,
    suffix_keyvals,
    page_pool,
    prefix_tokens,
    page_place,
    state_place,
    store_place,
):
    peers = lax.axis_size("req")
    me = lax.axis_index("req").astype(jnp.int32).reshape(1)
    requests, length = REQUESTS_PER_IDX, APPENDED_LENGTH
    groups = maps_in.shape[1]
    state = maps_in.shape[2] // 2
    heads = delta_raw.shape[1]
    per_group = heads // groups
    width = mixer_in.shape[1]
    group_width = width // groups
    head_dim = width // heads
    slots, _, page_rows, _ = state_pool.shape
    page_count = state_place.shape[1]
    kv_heads = page_pool.shape[2]
    attend_dim = queries.shape[2]
    per_kv = queries.shape[1] // kv_heads
    page = page_pool.shape[1]
    prefix_pages = page_place.shape[1]
    page_slots = page_pool.shape[0]
    pair_pages = requests * prefix_pages // peers
    taps = conv_weight.shape[0]

    def exchange(pages):
        return lax.all_to_all(pages, "req", split_axis=0, concat_axis=0, tiled=True)

    state_send = route_pages(gather_kernel, "gather_states", me, state_place, state_pool)
    state_got = exchange(state_send)

    counts = tuple(sorted({max(1, pair_pages * share // 16) for share in SHARES}))
    used = jnp.arange(prefix_pages)[None, :] * page < prefix_tokens[:, None]
    holders = page_place // page_slots
    pairs = used[:, :, None] & (holders[:, :, None] == jnp.arange(peers)[None, None, :])
    needs = jnp.sum(pairs.reshape(peers, -1, peers).astype(jnp.int32), axis=1)
    places = jnp.arange(peers)
    both = jnp.sum(needs.reshape(peers // 2, 2, peers), axis=1)
    outside = jnp.arange(peers // 2)[:, None] != places[None, :] // 2
    limit_table = jnp.array(counts, jnp.int32)
    crowded = jnp.max(jnp.where(outside, both, 0)) > 2 * limit_table
    rests = jnp.maximum(needs[None] - limit_table[:, None, None], 0)
    rests = jnp.where(places[:, None] != places[None, :], rests, 0)
    crowded = crowded | (jnp.max(jnp.sum(rests, axis=2), axis=1) > PASSED)
    choice = jnp.sum(crowded.astype(jnp.int32))
    limit = jnp.sum(jnp.where(jnp.arange(len(counts)) == choice, limit_table, 0))
    limits = jnp.stack([me[0], limit, choice])
    pages_by_head = page_pool.transpose(0, 2, 1, 3)
    page_sends = send_used(counts, limits, page_place, prefix_tokens, pages_by_head)

    delta = jax.nn.softplus(delta_raw.T.astype(jnp.float32)).reshape(heads, requests, length)
    log_decay = jnp.cumsum(-delta * jnp.exp(decay_log)[:, None, None], axis=2)
    tail = jnp.exp(log_decay[:, :, -1:] - log_decay) * delta
    growth = jnp.exp(log_decay)

    def by_rows(values):
        return values.reshape(groups, per_group, requests, length).transpose(2, 0, 1, 3)

    def by_columns(values):
        return values.reshape(groups, per_group, requests, length).transpose(2, 0, 3, 1)

    decay_row = by_rows(log_decay)
    maps_split = maps_in.transpose(1, 0, 2)
    empty = 8 - (taps - 1)
    x_cache = jnp.pad(conv_cache.astype(jnp.float32), ((0, 0), (empty, 0), (0, 0)))
    maps_edge = jnp.pad(
        maps_cache.transpose(0, 2, 1, 3).astype(jnp.float32), ((0, 0), (0, 0), (empty, 0), (0, 0))
    )
    row_block = pl.BlockSpec((None, None, per_group, length), lambda r, g: (r, g, 0, 0))
    column_block = pl.BlockSpec((None, None, length, per_group), lambda r, g: (r, g, 0, 0))
    x_block = pl.BlockSpec((length, group_width), lambda r, g: (r, g))
    update_block = pl.BlockSpec((None, None, group_width, state), lambda r, g: (r, g, 0, 0))
    map_block = pl.BlockSpec((None, length, state), lambda r, g: (g, r, 0))
    partial, update, output_map = pl.pallas_call(
        functools.partial(inner_kernel, per_group),
        grid=(requests, groups),
        in_specs=[
            x_block,
            pl.BlockSpec((None, 8, group_width), lambda r, g: (r, 0, g)),
            pl.BlockSpec((taps, group_width), lambda r, g: (0, g)),
            pl.BlockSpec((None, length, 2 * state), lambda r, g: (g, r, 0)),
            pl.BlockSpec((None, None, 8, 2 * state), lambda r, g: (r, g, 0, 0)),
            pl.BlockSpec((None, taps, 2 * state), lambda r, g: (g, 0, 0)),
            row_block,
            column_block,
            row_block,
            column_block,
            pl.BlockSpec((1, group_width), lambda r, g: (0, g)),
        ],
        out_specs=[x_block, update_block, map_block],
        out_shape=[
            jax.ShapeDtypeStruct((requests * length, width), jnp.float32),
            jax.ShapeDtypeStruct((requests, groups, group_width, state), jnp.float32),
            jax.ShapeDtypeStruct((groups, requests * length, state), jnp.bfloat16),
        ],
        scratch_shapes=[
            pltpu.VMEM((8 + length, group_width), jnp.float32),
            pltpu.VMEM((8 + length, 2 * state), jnp.float32),
            pltpu.VMEM((length, group_width), jnp.bfloat16),
            pltpu.VMEM((length, group_width), jnp.bfloat16),
        ],
        cost_estimate=pl.CostEstimate(
            flops=3 * requests * length * width * state,
            bytes_accessed=32 * 2**20,
            transcendentals=requests * heads * length * length,
        ),
        compiler_params=params(),
        name="mix_new_tokens",
    )(
        mixer_in,
        x_cache,
        conv_weight.astype(jnp.float32),
        maps_split,
        maps_edge,
        maps_weight.transpose(1, 0, 2).astype(jnp.float32),
        decay_row,
        by_columns(log_decay),
        by_rows(delta),
        by_columns(tail),
        jnp.repeat(skip_gain, head_dim).reshape(1, width),
    )
    growth_col = by_columns(growth)
    grouped_queries = queries.reshape(requests, length, kv_heads, per_kv, attend_dim).transpose(
        0, 2, 3, 1, 4
    )
    fresh = suffix_keyvals.transpose(1, 0, 2)

    page_sends, state_got, partial, update, output_map, growth_col, decay_row = (
        lax.optimization_barrier(
            (page_sends, state_got, partial, update, output_map, growth_col, decay_row)
        )
    )
    state_block = pl.BlockSpec((None, None, group_width, state), lambda r, g, *_: (r, g, 0, 0))

    def advance(at, sends, state_got, update, decay_row):
        shapes = [pltpu.HBM(sent.shape, sent.dtype) for sent in sends]
        others = list(unwritten(shapes[:at] + shapes[at + 1 :])) if len(shapes) > 1 else []
        gots = tuple(others[:at] + [exchange(sends[at])] + others[at:])
        prior, final_send = pl.pallas_call(
            state_kernel,
            grid_spec=pltpu.PrefetchScalarGridSpec(
                num_scalar_prefetch=3,
                grid=(requests, groups),
                in_specs=[
                    any_spec(),
                    state_block,
                    pl.BlockSpec((None, None, per_group, length), lambda r, g, *_: (r, g, 0, 0)),
                ],
                out_specs=[state_block, hbm_spec()],
                scratch_shapes=[
                    pltpu.VMEM((page_count, per_group, page_rows, state), jnp.bfloat16),
                    pltpu.VMEM((page_count, per_group, page_rows, state), jnp.bfloat16),
                    pltpu.SMEM((requests * page_count,), jnp.int32),
                    pltpu.SMEM((requests * page_count,), jnp.int32),
                    pltpu.SMEM((peers,), jnp.int32),
                    pltpu.SemaphoreType.DMA((page_count,)),
                    pltpu.SemaphoreType.DMA((page_count,)),
                ],
            ),
            out_shape=[
                jax.ShapeDtypeStruct(update.shape, jnp.bfloat16),
                pltpu.HBM(state_pool.shape, jnp.bfloat16),
            ],
            cost_estimate=pl.CostEstimate(
                flops=4 * update.size, bytes_accessed=20 * 2**20, transcendentals=0
            ),
            compiler_params=params(),
            name="advance_states",
        )(me, state_place, store_place, state_got, update, decay_row)
        return gots, prior, final_send

    page_gots, prior, final_send = lax.switch(
        choice,
        [functools.partial(advance, at) for at in range(len(counts))],
        tuple(page_sends),
        state_got,
        update,
        decay_row,
    )
    final_got = exchange(final_send)
    mixer_out = pl.pallas_call(
        functools.partial(output_kernel, per_group),
        grid=(requests, groups),
        in_specs=[
            x_block,
            map_block,
            column_block,
            pl.BlockSpec((None, None, group_width, state), lambda r, g: (r, g, 0, 0)),
        ],
        out_specs=x_block,
        out_shape=jax.ShapeDtypeStruct((requests * length, width), jnp.bfloat16),
        cost_estimate=pl.CostEstimate(
            flops=2 * requests * length * width * state,
            bytes_accessed=18 * 2**20,
            transcendentals=0,
        ),
        compiler_params=params(),
        name="add_carried",
    )(partial, output_map, growth_col, prior)
    passed = pass_on(counts, limits, page_place, prefix_tokens, pages_by_head, page_gots)
    rows = per_kv * length
    head_block = pl.BlockSpec(
        (None, None, per_kv, length, attend_dim), lambda r, e, *_: (r, e, 0, 0, 0)
    )
    sums_block = pl.BlockSpec((None, None, attend_dim, rows), lambda r, e, *_: (r, e, 0, 0))
    stats_block = pl.BlockSpec((None, None, 2, rows), lambda r, e, *_: (r, e, 0, 0))
    lists = [
        pltpu.SMEM((requests * prefix_pages,), jnp.int32),
        pltpu.SMEM((requests * prefix_pages,), jnp.int32),
        pltpu.SMEM((requests,), jnp.int32),
        pltpu.SMEM((requests,), jnp.int32),
        pltpu.SMEM((2, peers), jnp.int32),
    ]
    sums, stats = pl.pallas_call(
        functools.partial(attend_kernel, attend_dim**-0.5, counts),
        grid_spec=pltpu.PrefetchScalarGridSpec(
            num_scalar_prefetch=3,
            grid=(requests, kv_heads),
            in_specs=[any_spec()] * (len(page_gots) + 1)
            + [
                head_block,
                pl.BlockSpec((None, length, 2 * attend_dim), lambda r, e, *_: (e, r, 0)),
            ],
            out_specs=[sums_block, stats_block],
            scratch_shapes=[
                pltpu.VMEM((prefix_pages * page, 2 * attend_dim), jnp.bfloat16),
                *lists,
                pltpu.SemaphoreType.DMA((prefix_pages,)),
            ],
        ),
        out_shape=[
            jax.ShapeDtypeStruct((requests, kv_heads, attend_dim, rows), jnp.float32),
            jax.ShapeDtypeStruct((requests, kv_heads, 2, rows), jnp.float32),
        ],
        cost_estimate=pl.CostEstimate(
            flops=4 * queries.size * (prefix_pages * page + length),
            bytes_accessed=16 * 2**20,
            transcendentals=queries.shape[0] * queries.shape[1] * (prefix_pages * page),
        ),
        compiler_params=params(),
        name="attend",
    )(
        limits,
        page_place,
        prefix_tokens,
        pages_by_head,
        *page_gots,
        grouped_queries,
        fresh,
    )
    attended = pl.pallas_call(
        functools.partial(attend_passed_kernel, attend_dim**-0.5, counts, page_slots),
        grid_spec=pltpu.PrefetchScalarGridSpec(
            num_scalar_prefetch=3,
            grid=(requests, kv_heads),
            in_specs=[any_spec(), head_block, sums_block, stats_block],
            out_specs=head_block,
            scratch_shapes=[
                pltpu.VMEM((-(-PASSED * page // length) * length, 2 * attend_dim), jnp.bfloat16),
                pltpu.VMEM((attend_dim, rows), jnp.float32),
                pltpu.VMEM((2, rows), jnp.float32),
                *lists,
                pltpu.SemaphoreType.DMA((PASSED,)),
            ],
        ),
        out_shape=jax.ShapeDtypeStruct(grouped_queries.shape, jnp.bfloat16),
        cost_estimate=pl.CostEstimate(
            flops=queries.size * PASSED * page,
            bytes_accessed=8 * 2**20,
            transcendentals=queries.shape[0] * queries.shape[1] * PASSED * page // 4,
        ),
        compiler_params=params(),
        name="attend_passed",
    )(limits, page_place, prefix_tokens, passed, grouped_queries, sums, stats)
    attention_out = attended.transpose(0, 3, 1, 2, 4).reshape(queries.shape)
    stored = route_pages(scatter_kernel, "scatter_states", me, store_place, final_got)
    return mixer_out, attention_out, stored


def solution(mesh):
    placed = (
        P(("parts", "req"), "tp"),
        P(("parts", "req"), "tp", None),
        P(("parts", "req"), "tp"),
        P(("parts", "req"), None, "tp"),
        P(("parts", "req"), None, "tp", None),
        P(None, "tp"),
        P(None, "tp", None),
        P("tp"),
        P("tp"),
        P(("parts", "req"), "tp", None, None),
        P(("parts", "req"), "tp", None),
        P(("parts", "req"), "tp", None),
        P(("parts", "req"), None, "tp", None),
        P("parts"),
        P("parts", None),
        P("parts", None),
        P("parts", None),
    )
    return jax.shard_map(
        body,
        mesh=mesh,
        in_specs=placed,
        out_specs=(
            P(("parts", "req"), "tp"),
            P(("parts", "req"), "tp", None),
            P(("parts", "req"), "tp", None, None),
        ),
        check_vma=False,
    )
```

```python
import functools

import jax
import jax.numpy as jnp
from jax import lax
from jax.experimental import pallas as pl
from jax.experimental.pallas import tpu as pltpu
from jax.sharding import PartitionSpec as P

APPENDED_LENGTH = 256
REQUESTS_PER_IDX = 4
VMEM_LIMIT = 48 * 1024 * 1024
SHARES = (6, 7, 8, 9, 10, 11, 16)
PASSED = 8
HIDDEN = (((1,), (1,)), ((), ()))


def params():
    return pltpu.CompilerParams(vmem_limit_bytes=VMEM_LIMIT)


def any_spec():
    return pl.BlockSpec(memory_space=pl.ANY)


def hbm_spec():
    return pl.BlockSpec(memory_space=pltpu.HBM)


def own_entries(place_ref, base, slots, position, row, emit):
    for j in range(place_ref.shape[1]):
        slot = place_ref[row, j] - base
        mine = (slot >= 0) & (slot < slots)

        @pl.when(mine)
        def _(slot=slot, position=position, j=j):
            emit(position, slot)

        position = position + jnp.where(mine, 1, 0)
    return position


def gather_kernel(ends_ref, place_ref, pool_ref, out_ref, staged, in_sem, out_sem):
    slots = pool_ref.shape[0]
    base = ends_ref[0] * slots

    def row_step(offset, position):
        def emit(at, slot):
            pltpu.make_async_copy(pool_ref.at[slot], staged.at[at], in_sem).start()

        row = ends_ref[1] * REQUESTS_PER_IDX + offset
        return own_entries(place_ref, base, slots, position, row, emit)

    lax.fori_loop(0, REQUESTS_PER_IDX, row_step, jnp.int32(0))
    pltpu.make_async_copy(pool_ref.at[pl.ds(0, staged.shape[0])], staged, in_sem).wait()
    forward = pltpu.make_async_copy(staged, out_ref, out_sem)
    forward.start()
    forward.wait()


def gather_for(ends, place, pool, capacity):
    shape = (capacity,) + pool.shape[1:]
    size = 2 * capacity * pool[0].size
    return pl.pallas_call(
        gather_kernel,
        out_shape=pltpu.HBM(shape, pool.dtype),
        grid_spec=pltpu.PrefetchScalarGridSpec(
            num_scalar_prefetch=2,
            grid=(1,),
            in_specs=[hbm_spec()],
            out_specs=hbm_spec(),
            scratch_shapes=[
                pltpu.VMEM(shape, pool.dtype),
                pltpu.SemaphoreType.DMA,
                pltpu.SemaphoreType.DMA,
            ],
        ),
        cost_estimate=pl.CostEstimate(flops=0, bytes_accessed=2 * size, transcendentals=0),
        compiler_params=params(),
        name="gather_states",
    )(ends, place, pltpu.with_memory_space_constraint(pool, pltpu.HBM))


def scatter_kernel(ends_ref, place_ref, got_ref, *rest):
    out_ref, staged, in_sem, out_sem = rest[-4:]
    slots = out_ref.shape[0]
    base = ends_ref[0] * slots
    fetch = pltpu.make_async_copy(got_ref, staged, in_sem)
    fetch.start()
    fetch.wait()

    def row_step(offset, position):
        def emit(at, slot):
            pltpu.make_async_copy(staged.at[at], out_ref.at[slot], out_sem).start()

        row = ends_ref[1] * REQUESTS_PER_IDX + offset
        return own_entries(place_ref, base, slots, position, row, emit)

    lax.fori_loop(0, REQUESTS_PER_IDX, row_step, jnp.int32(0))
    pltpu.make_async_copy(staged, out_ref.at[pl.ds(0, staged.shape[0])], out_sem).wait()


def scatter_from(ends, place, got, stored, shape):
    held = [] if stored is None else [stored]
    return pl.pallas_call(
        scatter_kernel,
        out_shape=pltpu.HBM(shape, got.dtype),
        grid_spec=pltpu.PrefetchScalarGridSpec(
            num_scalar_prefetch=2,
            grid=(1,),
            in_specs=[hbm_spec()] * (1 + len(held)),
            out_specs=hbm_spec(),
            scratch_shapes=[
                pltpu.VMEM(got.shape, got.dtype),
                pltpu.SemaphoreType.DMA,
                pltpu.SemaphoreType.DMA,
            ],
        ),
        input_output_aliases={3: 0} if held else {},
        cost_estimate=pl.CostEstimate(
            flops=0, bytes_accessed=4 * got.size, transcendentals=0
        ),
        compiler_params=params(),
        name="scatter_states",
    )(ends, place, got, *held)


def used_entry(place_ref, prefix_ref, page, slots, owner, row, j):
    slot = place_ref[row, j] - owner * slots
    return slot, (slot >= 0) & (slot < slots) & (j * page < prefix_ref[row])


def count_used(place_ref, entry, owner, server):
    def count_row(offset, total):
        for j in range(place_ref.shape[1]):
            _, wanted = entry(owner, server * REQUESTS_PER_IDX + offset, j)
            total = total + jnp.where(wanted, 1, 0)
        return total

    return lax.fori_loop(0, REQUESTS_PER_IDX, count_row, jnp.int32(0))


def partner_of(device):
    return device + 1 - 2 * (device % 2)


def send_kernel(counts, limits_ref, place_ref, prefix_ref, pool_ref, *rest):
    outs, (staged, needs, filled, in_sems, out_sems) = rest[: len(counts)], rest[len(counts) :]
    slots, page = pool_ref.shape[0], pool_ref.shape[2]
    me, limit, choice = limits_ref[0], limits_ref[1], limits_ref[2]
    columns = place_ref.shape[1]
    servers, room = staged.shape[:2]
    entry = functools.partial(used_entry, place_ref, prefix_ref, page, slots)

    def count_server(server, carry):
        needs[server] = count_used(place_ref, entry, me, server)
        return carry

    lax.fori_loop(0, servers, count_server, jnp.int32(0))

    def fetch(slot, server, position):
        return pltpu.make_async_copy(
            pool_ref.at[slot], staged.at[server, position], in_sems.at[server, position]
        )

    def fetch_server(server, carry):
        partner = partner_of(server)
        start = needs[partner] - limit

        def fetch_row(offset, rank):
            for j in range(columns):
                slot, wanted = entry(me, server * REQUESTS_PER_IDX + offset, j)
                wanted = wanted & (server != me)
                direct = rank < limit

                @pl.when(wanted & (direct | (partner != me)))
                def _(slot=slot, rank=rank, direct=direct):
                    fetch(
                        slot,
                        jnp.where(direct, server, partner),
                        jnp.where(direct, rank, start + rank),
                    ).start()

                rank = rank + jnp.where(wanted, 1, 0)
            return rank

        lax.fori_loop(0, REQUESTS_PER_IDX, fetch_row, jnp.int32(0))
        passed = jnp.where(partner == me, 0, jnp.maximum(needs[partner] - limit, 0))
        own = jnp.minimum(needs[server], limit)
        filled[server] = jnp.where(server == me, 0, own + passed)
        return carry

    lax.fori_loop(0, servers, fetch_server, jnp.int32(0))

    def forward(server, option):
        count = counts[option]
        return pltpu.make_async_copy(
            staged.at[server, pl.ds(0, count)],
            outs[option].at[pl.ds(server * count, count)],
            out_sems.at[server],
        )

    def forward_server(server, carry):
        for position in range(room):

            @pl.when(position < filled[server])
            def _(position=position):
                fetch(0, server, position).wait()

        for option in range(len(counts)):

            @pl.when(choice == option)
            def _(option=option):
                forward(server, option).start()

        return carry

    lax.fori_loop(0, servers, forward_server, jnp.int32(0))

    def finish_server(server, carry):
        for option in range(len(counts)):

            @pl.when(choice == option)
            def _(option=option):
                forward(server, option).wait()

        return carry

    lax.fori_loop(0, servers, finish_server, jnp.int32(0))


def send_used(counts, limits, place, prefix, pages):
    servers = lax.axis_size("req")
    shapes = [
        pltpu.HBM((servers * count,) + pages.shape[1:], pages.dtype) for count in counts
    ]
    return pl.pallas_call(
        functools.partial(send_kernel, counts),
        out_shape=shapes,
        grid_spec=pltpu.PrefetchScalarGridSpec(
            num_scalar_prefetch=3,
            grid=(1,),
            in_specs=[any_spec()],
            out_specs=[hbm_spec()] * len(counts),
            scratch_shapes=[
                pltpu.VMEM((servers, counts[-1]) + pages.shape[1:], pages.dtype),
                pltpu.SMEM((servers,), jnp.int32),
                pltpu.SMEM((servers,), jnp.int32),
                pltpu.SemaphoreType.DMA((servers, counts[-1])),
                pltpu.SemaphoreType.DMA((servers,)),
            ],
        ),
        cost_estimate=pl.CostEstimate(
            flops=0, bytes_accessed=2 * pages.size * 2, transcendentals=0
        ),
        compiler_params=params(),
        name="send_used_pages",
    )(limits, place, prefix, pages)


def pass_kernel(counts, limits_ref, place_ref, prefix_ref, pool_ref, *rest):
    gots, (out_ref, staged, in_sems, out_sem) = rest[: len(counts)], rest[len(counts) :]
    slots, page = pool_ref.shape[0], pool_ref.shape[2]
    me, limit, choice = limits_ref[0], limits_ref[1], limits_ref[2]
    columns = place_ref.shape[1]
    servers = place_ref.shape[0] // REQUESTS_PER_IDX
    partner = partner_of(me)
    entry = functools.partial(used_entry, place_ref, prefix_ref, page, slots)

    def fetch(source, index, at):
        return pltpu.make_async_copy(source.at[index], staged.at[at], in_sems.at[at])

    def own_pages(at):
        def row_step(offset, carry):
            rank, at = carry
            for j in range(columns):
                slot, wanted = entry(me, partner * REQUESTS_PER_IDX + offset, j)
                take = wanted & (rank >= limit)

                @pl.when(take)
                def _(slot=slot, at=at):
                    fetch(pool_ref, slot, at).start()

                rank = rank + jnp.where(wanted, 1, 0)
                at = at + jnp.where(take, 1, 0)
            return rank, at

        return lax.fori_loop(0, REQUESTS_PER_IDX, row_step, (jnp.int32(0), at))[1]

    def relayed_pages(owner, at):
        start = count_used(place_ref, entry, owner, me)
        more = jnp.maximum(count_used(place_ref, entry, owner, partner) - limit, 0)

        def page_step(step, carry):
            index = owner * limit + start + step
            for option in range(len(counts)):

                @pl.when(choice == option)
                def _(option=option):
                    fetch(gots[option], index, at + step).start()

            return carry

        lax.fori_loop(0, more, page_step, jnp.int32(0))
        return at + more

    def owner_step(owner, at):
        at = lax.cond(owner == me, own_pages, lambda at: at, at)
        outside = (owner != me) & (owner != partner)
        return lax.cond(outside, lambda at: relayed_pages(owner, at), lambda at: at, at)

    total = lax.fori_loop(0, servers, owner_step, jnp.int32(0))
    for position in range(staged.shape[0]):

        @pl.when(position < total)
        def _(position=position):
            fetch(pool_ref, 0, position).wait()

    forward = pltpu.make_async_copy(staged, out_ref, out_sem)
    forward.start()
    forward.wait()


def pass_on(counts, limits, place, prefix, pages, gots):
    shape = (PASSED,) + pages.shape[1:]
    collected = pl.pallas_call(
        functools.partial(pass_kernel, counts),
        out_shape=pltpu.HBM(shape, pages.dtype),
        grid_spec=pltpu.PrefetchScalarGridSpec(
            num_scalar_prefetch=3,
            grid=(1,),
            in_specs=[any_spec()] * (1 + len(gots)),
            out_specs=hbm_spec(),
            scratch_shapes=[
                pltpu.VMEM(shape, pages.dtype),
                pltpu.SemaphoreType.DMA((PASSED,)),
                pltpu.SemaphoreType.DMA,
            ],
        ),
        cost_estimate=pl.CostEstimate(flops=0, bytes_accessed=2**20, transcendentals=0),
        compiler_params=params(),
        name="pass_pages_on",
    )(limits, place, prefix, pages, *gots)
    swaps = [(peer, peer ^ 1) for peer in range(lax.axis_size("req"))]
    return lax.ppermute(collected, "req", swaps)


def unwritten(shapes):
    return pl.pallas_call(
        lambda *refs: None,
        out_shape=shapes,
        out_specs=[hbm_spec()] * len(shapes),
        cost_estimate=pl.CostEstimate(flops=0, bytes_accessed=0, transcendentals=0),
        name="unwritten",
    )()


def conv_silu(buffer, cache_ref, values, weight_ref):
    length = values.shape[0]
    taps = weight_ref.shape[-2]
    buffer[0:8, :] = cache_ref[...]
    buffer[8:, :] = values.astype(jnp.float32)
    start = 8 - (taps - 1)
    summed = weight_ref[0:1, :] * buffer[start : start + length, :]
    for tap in range(1, taps):
        at = start + tap
        summed = summed + weight_ref[tap : tap + 1, :] * buffer[at : at + length, :]
    return jax.nn.silu(summed).astype(jnp.bfloat16)


def inner_kernel(
    heads,
    x_ref,
    x_cache_ref,
    x_weight_ref,
    maps_ref,
    maps_cache_ref,
    maps_weight_ref,
    decay_row_ref,
    decay_col_ref,
    delta_row_ref,
    tail_ref,
    skip_ref,
    partial_ref,
    update_ref,
    output_map_ref,
    x_buffer,
    maps_buffer,
    x_values,
    scaled,
):
    length, width = x_ref.shape
    head_dim = width // heads
    state = maps_ref.shape[1] // 2
    x_values[...] = conv_silu(x_buffer, x_cache_ref, x_ref[...], x_weight_ref)
    maps = conv_silu(maps_buffer, maps_cache_ref, maps_ref[...], maps_weight_ref)
    input_map, output_map = maps[:, :state], maps[:, state:]
    output_map_ref[...] = output_map
    intersection = lax.dot_general(
        output_map, input_map, HIDDEN, preferred_element_type=jnp.float32
    )
    rows = lax.broadcasted_iota(jnp.int32, (length, length), 0)
    columns = lax.broadcasted_iota(jnp.int32, (length, length), 1)
    causal = rows >= columns
    for h in range(heads):
        lanes = slice(h * head_dim, (h + 1) * head_dim)
        gap = decay_col_ref[:, h : h + 1] - decay_row_ref[h : h + 1, :]
        decays = jnp.where(causal, jnp.exp(jnp.where(causal, gap, 0.0)), 0.0)
        mixing = (intersection * decays * delta_row_ref[h : h + 1, :]).astype(jnp.bfloat16)
        x_head = x_values[:, lanes]
        x_wide = x_head.astype(jnp.float32)
        within = jnp.dot(mixing, x_head, preferred_element_type=jnp.float32)
        partial_ref[:, lanes] = within + skip_ref[:, lanes] * x_wide
        scaled[:, lanes] = (x_wide * tail_ref[:, h : h + 1]).astype(jnp.bfloat16)
    update_ref[...] = lax.dot_general(
        scaled[...], input_map, (((0,), (0,)), ((), ())), preferred_element_type=jnp.float32
    )


def state_kernel(me_ref, state_place_ref, store_place_ref, update_ref, decay_row_ref, *rest):
    peers = (len(rest) - 10) // 2
    gots, prior_ref, sends = rest[:peers], rest[peers], rest[peers + 1 : 2 * peers + 1]
    pages, finals, from_kind, from_index, to_kind, to_index, counts, in_sems, out_sems = rest[
        2 * peers + 1 :
    ]
    request, group = pl.program_id(0), pl.program_id(1)
    page_count, heads, page_rows, state = pages.shape
    slots = gots[0].shape[0]
    head_dim = page_count * page_rows
    joint = 16 // page_rows
    me = me_ref[0]

    @pl.when((request == 0) & (group == 0))
    def _():
        for peer in range(2 * peers):
            counts[peer] = 0

        def row_step(offset, carry):
            for j in range(page_count):
                entry = offset * page_count + j
                place = state_place_ref[me * REQUESTS_PER_IDX + offset, j]
                owner = place // slots
                rank = counts[owner]
                counts[owner] = rank + 1
                distance = (me - owner + peers) % peers
                from_kind[entry] = distance
                from_index[entry] = jnp.where(distance == 0, place - me * slots, rank)
                target = store_place_ref[me * REQUESTS_PER_IDX + offset, j] // slots
                to_index[entry] = counts[peers + target]
                counts[peers + target] = to_index[entry] + 1
                to_kind[entry] = (target - me + peers) % peers
            return carry

        lax.fori_loop(0, REQUESTS_PER_IDX, row_step, jnp.int32(0))

    half = pl.ds(group * heads, heads)

    def arrive(j, kind):
        index = from_index[request * page_count + j]
        return pltpu.make_async_copy(gots[kind].at[index, half], pages.at[j], in_sems.at[j])

    def depart(j, kind):
        index = to_index[request * page_count + j]
        return pltpu.make_async_copy(finals.at[j], sends[kind].at[index, half], out_sems.at[j])

    def start_arrival(j):
        for kind in range(peers):

            @pl.when(from_kind[request * page_count + j] == kind)
            def _(kind=kind):
                arrive(j, kind).start()

    def start_departure(j):
        for kind in range(peers):

            @pl.when(to_kind[request * page_count + j] == kind)
            def _(kind=kind):
                depart(j, kind).start()

    def each(start, end, act):
        def step(j, carry):
            act(j)
            return carry

        lax.fori_loop(start, end, step, jnp.int32(0))

    each(0, page_count, start_arrival)
    last = decay_row_ref.shape[1] - 1
    growths = [jnp.exp(decay_row_ref[h : h + 1, last : last + 1]) for h in range(heads)]

    def joint_step(step, carry):
        first = step * joint
        each(first, first + joint, lambda j: arrive(j, 0).wait())
        for h in range(heads):
            rows = pl.ds(pl.multiple_of(h * head_dim + step * 16, 16), 16)
            old = jnp.concatenate(
                [pages[first + i, h].astype(jnp.float32) for i in range(joint)], axis=0
            )
            prior_ref[rows, :] = old.astype(jnp.bfloat16)
            new = growths[h] * old + update_ref[rows, :]
            for i in range(joint):
                finals[first + i, h] = new[i * page_rows : (i + 1) * page_rows].astype(
                    jnp.bfloat16
                )
        each(first, first + joint, start_departure)
        return carry

    lax.fori_loop(0, page_count // joint, joint_step, jnp.int32(0))
    each(0, page_count, lambda j: depart(j, 0).wait())


def output_kernel(heads, partial_ref, output_map_ref, growth_ref, prior_ref, out_ref):
    head_dim = out_ref.shape[1] // heads
    carried = lax.dot_general(
        output_map_ref[...], prior_ref[...], HIDDEN, preferred_element_type=jnp.float32
    )
    for h in range(heads):
        lanes = slice(h * head_dim, (h + 1) * head_dim)
        out_ref[:, lanes] = (
            partial_ref[:, lanes] + growth_ref[:, h : h + 1] * carried[:, lanes]
        ).astype(jnp.bfloat16)


def list_pages(
    counts, passed, limits_ref, place_ref, prefix_ref, slots, page, kinds, indices, amounts, sizes, ranks
):
    me, limit, choice = limits_ref[0], limits_ref[1], limits_ref[2]
    page_count = place_ref.shape[1]
    peers = ranks.shape[1]
    start_row = me * REQUESTS_PER_IDX
    for peer in range(peers):
        ranks[0, peer] = 0
    if passed:

        def count_row(offset, carry):
            tokens = prefix_ref[start_row + offset]
            for j in range(page_count):
                owner = place_ref[start_row + offset, j] // slots
                ranks[0, owner] = ranks[0, owner] + jnp.where(j * page < tokens, 1, 0)
            return carry

        lax.fori_loop(0, REQUESTS_PER_IDX, count_row, jnp.int32(0))
        begin = jnp.int32(0)
        for peer in range(peers):
            ranks[1, peer] = begin
            begin = begin + jnp.where(peer == me, 0, jnp.maximum(ranks[0, peer] - limit, 0))
            ranks[0, peer] = 0
    def place_row(offset, carry):
        tokens = prefix_ref[start_row + offset]
        at, size = jnp.int32(0), jnp.int32(0)
        for j in range(page_count):
            place = place_ref[start_row + offset, j]
            owner = place // slots
            rank = ranks[0, owner]
            used = j * page < tokens
            ranks[0, owner] = rank + jnp.where(used, 1, 0)
            here = owner == me
            late = (rank >= limit) & jnp.logical_not(here)
            if passed:
                take = used & late
                kind = jnp.int32(0)
                index = ranks[1, owner] + rank - limit
            else:
                take = used & jnp.logical_not(late)
                kind = jnp.where(here, len(counts), choice)
                index = jnp.where(here, place - me * slots, owner * limit + rank)

            @pl.when(take)
            def _(at=at, kind=kind, index=index):
                kinds[offset * page_count + at] = kind
                indices[offset * page_count + at] = index

            at = at + jnp.where(take, 1, 0)
            size = size + jnp.where(take, jnp.minimum(page, tokens - j * page), 0)
        amounts[offset] = at
        sizes[offset] = size
        return carry

    lax.fori_loop(0, REQUESTS_PER_IDX, place_row, jnp.int32(0))


def score(scale, keys, query):
    return lax.dot_general(keys, query, HIDDEN, preferred_element_type=jnp.float32) * scale


def weigh(values, exponent):
    return lax.dot_general(
        values,
        exponent.astype(jnp.bfloat16),
        (((0,), (0,)), ((), ())),
        preferred_element_type=jnp.float32,
    )


def add_pages(scale, query, size, chunk, cached_kv, stats_ref, sums_ref):
    head_dim = query.shape[1]
    keys_at = lax.broadcasted_iota(jnp.int32, (chunk, query.shape[0]), 0)

    def chunk_step(step, carry):
        start = pl.multiple_of(step * chunk, chunk)
        scores = score(scale, cached_kv[pl.ds(start, chunk), :head_dim], query)
        scores = jnp.where(keys_at < size - start, scores, -jnp.inf)
        old = stats_ref[0:1, :]
        top = jnp.maximum(old, jnp.max(scores, axis=0, keepdims=True))
        fade = jnp.exp(old - top)
        exponent = jnp.exp(scores - top)
        stats_ref[0:1, :] = top
        stats_ref[1:2, :] = stats_ref[1:2, :] * fade + jnp.sum(exponent, axis=0, keepdims=True)
        sums_ref[...] = sums_ref[...] * fade + weigh(
            cached_kv[pl.ds(start, chunk), head_dim:], exponent
        )
        return carry

    lax.fori_loop(0, (size + chunk - 1) // chunk, chunk_step, jnp.int32(0))


def attend_kernel(scale, counts, limits_ref, place_ref, prefix_ref, pool_ref, *rest):
    gots = rest[: len(counts)]
    query_ref, fresh_ref, sums_ref, stats_ref = rest[len(counts) : len(counts) + 4]
    cached_kv, kinds, indices, amounts, sizes, ranks, sems = rest[len(counts) + 4 :]
    request, kv_head = pl.program_id(0), pl.program_id(1)
    per_kv, length, head_dim = query_ref.shape
    slots, page = pool_ref.shape[0], pool_ref.shape[2]
    page_count = place_ref.shape[1]

    @pl.when((request == 0) & (kv_head == 0))
    def _():
        cached_kv[...] = jnp.zeros_like(cached_kv)
        list_pages(
            counts, False, limits_ref, place_ref, prefix_ref, slots, page,
            kinds, indices, amounts, sizes, ranks,
        )

    amount = amounts[request]

    def target(j):
        return cached_kv.at[pl.ds(pl.multiple_of(j * page, page), page)]

    def start_copy(j, carry):
        entry = request * page_count + j
        for kind, source in enumerate(gots + (pool_ref,)):

            @pl.when(kinds[entry] == kind)
            def _(source=source):
                pltpu.make_async_copy(
                    source.at[indices[entry], kv_head], target(j), sems.at[j]
                ).start()

        return carry

    lax.fori_loop(0, amount, start_copy, jnp.int32(0))
    query = query_ref[...].reshape(per_kv * length, head_dim)
    keys_at = lax.broadcasted_iota(jnp.int32, (length, per_kv * length), 0)
    queries_at = lax.broadcasted_iota(jnp.int32, (length, per_kv * length), 1) % length
    scores = score(scale, fresh_ref[:, :head_dim], query)
    scores = jnp.where(keys_at <= queries_at, scores, -jnp.inf)
    top = jnp.max(scores, axis=0, keepdims=True)
    exponent = jnp.exp(scores - top)
    stats_ref[0:1, :] = top
    stats_ref[1:2, :] = jnp.sum(exponent, axis=0, keepdims=True)
    sums_ref[...] = weigh(fresh_ref[:, head_dim:], exponent)

    def wait_copy(j, carry):
        pltpu.make_async_copy(pool_ref.at[0, kv_head], target(j), sems.at[j]).wait()
        return carry

    lax.fori_loop(0, amount, wait_copy, jnp.int32(0))
    add_pages(scale, query, sizes[request], length, cached_kv, stats_ref, sums_ref)


def attend_passed_kernel(
    scale,
    counts,
    slots,
    limits_ref,
    place_ref,
    prefix_ref,
    passed_ref,
    query_ref,
    sums_in_ref,
    stats_in_ref,
    out_ref,
    cached_kv,
    sums_ref,
    stats_ref,
    kinds,
    indices,
    amounts,
    sizes,
    ranks,
    sems,
):
    request, kv_head = pl.program_id(0), pl.program_id(1)
    per_kv, length, head_dim = query_ref.shape
    page = passed_ref.shape[2]
    page_count = place_ref.shape[1]

    @pl.when((request == 0) & (kv_head == 0))
    def _():
        cached_kv[...] = jnp.zeros_like(cached_kv)
        list_pages(
            counts, True, limits_ref, place_ref, prefix_ref, slots, page,
            kinds, indices, amounts, sizes, ranks,
        )

    amount = amounts[request]

    def fetch(j, index):
        target = cached_kv.at[pl.ds(pl.multiple_of(j * page, page), page)]
        return pltpu.make_async_copy(passed_ref.at[index, kv_head], target, sems.at[j])

    def start_copy(j, carry):
        fetch(j, indices[request * page_count + j]).start()
        return carry

    def wait_copy(j, carry):
        fetch(j, 0).wait()
        return carry

    @pl.when(amount == 0)
    def _():
        out_ref[...] = (
            (sums_in_ref[...] / stats_in_ref[1:2, :]).T.astype(jnp.bfloat16).reshape(out_ref.shape)
        )

    @pl.when(amount > 0)
    def _():
        lax.fori_loop(0, amount, start_copy, jnp.int32(0))
        sums_ref[...] = sums_in_ref[...]
        stats_ref[...] = stats_in_ref[...]
        lax.fori_loop(0, amount, wait_copy, jnp.int32(0))
        query = query_ref[...].reshape(per_kv * length, head_dim)
        add_pages(scale, query, sizes[request], length, cached_kv, stats_ref, sums_ref)
        out_ref[...] = (
            (sums_ref[...] / stats_ref[1:2, :]).T.astype(jnp.bfloat16).reshape(out_ref.shape)
        )


def body(
    mixer_in,
    maps_in,
    delta_raw,
    conv_cache,
    maps_cache,
    conv_weight,
    maps_weight,
    decay_log,
    skip_gain,
    state_pool,
    queries,
    suffix_keyvals,
    page_pool,
    prefix_tokens,
    page_place,
    state_place,
    store_place,
):
    peers = lax.axis_size("req")
    me = lax.axis_index("req").astype(jnp.int32).reshape(1)
    requests, length = REQUESTS_PER_IDX, APPENDED_LENGTH
    groups = maps_in.shape[1]
    state = maps_in.shape[2] // 2
    heads = delta_raw.shape[1]
    per_group = heads // groups
    width = mixer_in.shape[1]
    group_width = width // groups
    head_dim = width // heads
    slots, _, page_rows, _ = state_pool.shape
    page_count = state_place.shape[1]
    kv_heads = page_pool.shape[2]
    attend_dim = queries.shape[2]
    per_kv = queries.shape[1] // kv_heads
    page = page_pool.shape[1]
    prefix_pages = page_place.shape[1]
    page_slots = page_pool.shape[0]
    pair_pages = requests * prefix_pages // peers
    taps = conv_weight.shape[0]

    def exchange(pages):
        return lax.all_to_all(pages, "req", split_axis=0, concat_axis=0, tiled=True)

    capacity = requests * page_count // peers
    distances = range(1, peers)

    def send_to(distance, pages):
        return lax.ppermute(
            pages, "req", [(peer, (peer + distance) % peers) for peer in range(peers)]
        )

    def ends(distance):
        return jnp.concatenate([me, (me + distance) % peers])

    state_gots = [state_pool] + [
        send_to(distance, gather_for(ends(distance), state_place, state_pool, capacity))
        for distance in distances
    ]

    counts = tuple(sorted({max(1, pair_pages * share // 16) for share in SHARES}))
    used = jnp.arange(prefix_pages)[None, :] * page < prefix_tokens[:, None]
    holders = page_place // page_slots
    pairs = used[:, :, None] & (holders[:, :, None] == jnp.arange(peers)[None, None, :])
    needs = jnp.sum(pairs.reshape(peers, -1, peers).astype(jnp.int32), axis=1)
    places = jnp.arange(peers)
    both = jnp.sum(needs.reshape(peers // 2, 2, peers), axis=1)
    outside = jnp.arange(peers // 2)[:, None] != places[None, :] // 2
    limit_table = jnp.array(counts, jnp.int32)
    crowded = jnp.max(jnp.where(outside, both, 0)) > 2 * limit_table
    rests = jnp.maximum(needs[None] - limit_table[:, None, None], 0)
    rests = jnp.where(places[:, None] != places[None, :], rests, 0)
    crowded = crowded | (jnp.max(jnp.sum(rests, axis=2), axis=1) > PASSED)
    choice = jnp.sum(crowded.astype(jnp.int32))
    limit = jnp.sum(jnp.where(jnp.arange(len(counts)) == choice, limit_table, 0))
    limits = jnp.stack([me[0], limit, choice])
    pages_by_head = page_pool.transpose(0, 2, 1, 3)
    page_sends = send_used(counts, limits, page_place, prefix_tokens, pages_by_head)

    delta = jax.nn.softplus(delta_raw.T.astype(jnp.float32)).reshape(heads, requests, length)
    log_decay = jnp.cumsum(-delta * jnp.exp(decay_log)[:, None, None], axis=2)
    tail = jnp.exp(log_decay[:, :, -1:] - log_decay) * delta
    growth = jnp.exp(log_decay)

    def by_rows(values):
        return values.reshape(groups, per_group, requests, length).transpose(2, 0, 1, 3)

    def by_columns(values):
        return values.reshape(groups, per_group, requests, length).transpose(2, 0, 3, 1)

    decay_row = by_rows(log_decay)
    maps_split = maps_in.transpose(1, 0, 2)
    empty = 8 - (taps - 1)
    x_cache = jnp.pad(conv_cache.astype(jnp.float32), ((0, 0), (empty, 0), (0, 0)))
    maps_edge = jnp.pad(
        maps_cache.transpose(0, 2, 1, 3).astype(jnp.float32), ((0, 0), (0, 0), (empty, 0), (0, 0))
    )
    row_block = pl.BlockSpec((None, None, per_group, length), lambda r, g: (r, g, 0, 0))
    column_block = pl.BlockSpec((None, None, length, per_group), lambda r, g: (r, g, 0, 0))
    x_block = pl.BlockSpec((length, group_width), lambda r, g: (r, g))
    update_block = pl.BlockSpec((None, None, group_width, state), lambda r, g: (r, g, 0, 0))
    map_block = pl.BlockSpec((None, length, state), lambda r, g: (g, r, 0))
    partial, update, output_map = pl.pallas_call(
        functools.partial(inner_kernel, per_group),
        grid=(requests, groups),
        in_specs=[
            x_block,
            pl.BlockSpec((None, 8, group_width), lambda r, g: (r, 0, g)),
            pl.BlockSpec((taps, group_width), lambda r, g: (0, g)),
            pl.BlockSpec((None, length, 2 * state), lambda r, g: (g, r, 0)),
            pl.BlockSpec((None, None, 8, 2 * state), lambda r, g: (r, g, 0, 0)),
            pl.BlockSpec((None, taps, 2 * state), lambda r, g: (g, 0, 0)),
            row_block,
            column_block,
            row_block,
            column_block,
            pl.BlockSpec((1, group_width), lambda r, g: (0, g)),
        ],
        out_specs=[x_block, update_block, map_block],
        out_shape=[
            jax.ShapeDtypeStruct((requests * length, width), jnp.float32),
            jax.ShapeDtypeStruct((requests, groups, group_width, state), jnp.float32),
            jax.ShapeDtypeStruct((groups, requests * length, state), jnp.bfloat16),
        ],
        scratch_shapes=[
            pltpu.VMEM((8 + length, group_width), jnp.float32),
            pltpu.VMEM((8 + length, 2 * state), jnp.float32),
            pltpu.VMEM((length, group_width), jnp.bfloat16),
            pltpu.VMEM((length, group_width), jnp.bfloat16),
        ],
        cost_estimate=pl.CostEstimate(
            flops=3 * requests * length * width * state,
            bytes_accessed=32 * 2**20,
            transcendentals=requests * heads * length * length,
        ),
        compiler_params=params(),
        name="mix_new_tokens",
    )(
        mixer_in,
        x_cache,
        conv_weight.astype(jnp.float32),
        maps_split,
        maps_edge,
        maps_weight.transpose(1, 0, 2).astype(jnp.float32),
        decay_row,
        by_columns(log_decay),
        by_rows(delta),
        by_columns(tail),
        jnp.repeat(skip_gain, head_dim).reshape(1, width),
    )
    growth_col = by_columns(growth)
    grouped_queries = queries.reshape(requests, length, kv_heads, per_kv, attend_dim).transpose(
        0, 2, 3, 1, 4
    )
    fresh = suffix_keyvals.transpose(1, 0, 2)

    page_sends, state_gots, partial, update, output_map, growth_col, decay_row = (
        lax.optimization_barrier(
            (page_sends, state_gots, partial, update, output_map, growth_col, decay_row)
        )
    )
    state_block = pl.BlockSpec((None, None, group_width, state), lambda r, g, *_: (r, g, 0, 0))

    def advance(at, sends, state_gots, update, decay_row):
        shapes = [pltpu.HBM(sent.shape, sent.dtype) for sent in sends]
        others = list(unwritten(shapes[:at] + shapes[at + 1 :])) if len(shapes) > 1 else []
        gots = tuple(others[:at] + [exchange(sends[at])] + others[at:])
        prior, *final_sends = pl.pallas_call(
            state_kernel,
            grid_spec=pltpu.PrefetchScalarGridSpec(
                num_scalar_prefetch=3,
                grid=(requests, groups),
                in_specs=[
                    state_block,
                    pl.BlockSpec((None, None, per_group, length), lambda r, g, *_: (r, g, 0, 0)),
                ]
                + [any_spec()] * peers,
                out_specs=[state_block] + [hbm_spec()] * peers,
                scratch_shapes=[
                    pltpu.VMEM((page_count, per_group, page_rows, state), jnp.bfloat16),
                    pltpu.VMEM((page_count, per_group, page_rows, state), jnp.bfloat16),
                    *[pltpu.SMEM((requests * page_count,), jnp.int32)] * 4,
                    pltpu.SMEM((2 * peers,), jnp.int32),
                    pltpu.SemaphoreType.DMA((page_count,)),
                    pltpu.SemaphoreType.DMA((page_count,)),
                ],
            ),
            out_shape=[
                jax.ShapeDtypeStruct(update.shape, jnp.bfloat16),
                *[pltpu.HBM((capacity,) + state_pool.shape[1:], jnp.bfloat16)] * peers,
            ],
            cost_estimate=pl.CostEstimate(
                flops=4 * update.size, bytes_accessed=20 * 2**20, transcendentals=0
            ),
            compiler_params=params(),
            name="advance_states",
        )(me, state_place, store_place, update, decay_row, *state_gots)
        return gots, prior, final_sends

    page_gots, prior, final_sends = lax.switch(
        choice,
        [functools.partial(advance, at) for at in range(len(counts))],
        tuple(page_sends),
        state_gots,
        update,
        decay_row,
    )
    final_gots = [final_sends[0]] + [
        send_to(distance, final_sends[distance]) for distance in distances
    ]
    mixer_out = pl.pallas_call(
        functools.partial(output_kernel, per_group),
        grid=(requests, groups),
        in_specs=[
            x_block,
            map_block,
            column_block,
            pl.BlockSpec((None, None, group_width, state), lambda r, g: (r, g, 0, 0)),
        ],
        out_specs=x_block,
        out_shape=jax.ShapeDtypeStruct((requests * length, width), jnp.bfloat16),
        cost_estimate=pl.CostEstimate(
            flops=2 * requests * length * width * state,
            bytes_accessed=18 * 2**20,
            transcendentals=0,
        ),
        compiler_params=params(),
        name="add_carried",
    )(partial, output_map, growth_col, prior)
    passed = pass_on(counts, limits, page_place, prefix_tokens, pages_by_head, page_gots)
    rows = per_kv * length
    head_block = pl.BlockSpec(
        (None, None, per_kv, length, attend_dim), lambda r, e, *_: (r, e, 0, 0, 0)
    )
    sums_block = pl.BlockSpec((None, None, attend_dim, rows), lambda r, e, *_: (r, e, 0, 0))
    stats_block = pl.BlockSpec((None, None, 2, rows), lambda r, e, *_: (r, e, 0, 0))
    lists = [
        pltpu.SMEM((requests * prefix_pages,), jnp.int32),
        pltpu.SMEM((requests * prefix_pages,), jnp.int32),
        pltpu.SMEM((requests,), jnp.int32),
        pltpu.SMEM((requests,), jnp.int32),
        pltpu.SMEM((2, peers), jnp.int32),
    ]
    sums, stats = pl.pallas_call(
        functools.partial(attend_kernel, attend_dim**-0.5, counts),
        grid_spec=pltpu.PrefetchScalarGridSpec(
            num_scalar_prefetch=3,
            grid=(requests, kv_heads),
            in_specs=[any_spec()] * (len(page_gots) + 1)
            + [
                head_block,
                pl.BlockSpec((None, length, 2 * attend_dim), lambda r, e, *_: (e, r, 0)),
            ],
            out_specs=[sums_block, stats_block],
            scratch_shapes=[
                pltpu.VMEM((prefix_pages * page, 2 * attend_dim), jnp.bfloat16),
                *lists,
                pltpu.SemaphoreType.DMA((prefix_pages,)),
            ],
        ),
        out_shape=[
            jax.ShapeDtypeStruct((requests, kv_heads, attend_dim, rows), jnp.float32),
            jax.ShapeDtypeStruct((requests, kv_heads, 2, rows), jnp.float32),
        ],
        cost_estimate=pl.CostEstimate(
            flops=4 * queries.size * (prefix_pages * page + length),
            bytes_accessed=16 * 2**20,
            transcendentals=queries.shape[0] * queries.shape[1] * (prefix_pages * page),
        ),
        compiler_params=params(),
        name="attend",
    )(
        limits,
        page_place,
        prefix_tokens,
        pages_by_head,
        *page_gots,
        grouped_queries,
        fresh,
    )
    attended = pl.pallas_call(
        functools.partial(attend_passed_kernel, attend_dim**-0.5, counts, page_slots),
        grid_spec=pltpu.PrefetchScalarGridSpec(
            num_scalar_prefetch=3,
            grid=(requests, kv_heads),
            in_specs=[any_spec(), head_block, sums_block, stats_block],
            out_specs=head_block,
            scratch_shapes=[
                pltpu.VMEM((-(-PASSED * page // length) * length, 2 * attend_dim), jnp.bfloat16),
                pltpu.VMEM((attend_dim, rows), jnp.float32),
                pltpu.VMEM((2, rows), jnp.float32),
                *lists,
                pltpu.SemaphoreType.DMA((PASSED,)),
            ],
        ),
        out_shape=jax.ShapeDtypeStruct(grouped_queries.shape, jnp.bfloat16),
        cost_estimate=pl.CostEstimate(
            flops=queries.size * PASSED * page,
            bytes_accessed=8 * 2**20,
            transcendentals=queries.shape[0] * queries.shape[1] * PASSED * page // 4,
        ),
        compiler_params=params(),
        name="attend_passed",
    )(limits, page_place, prefix_tokens, passed, grouped_queries, sums, stats)
    attention_out = attended.transpose(0, 3, 1, 2, 4).reshape(queries.shape)
    stored = None
    for distance, got in enumerate(final_gots):
        stored = scatter_from(
            ends(peers - distance), store_place, got, stored, state_pool.shape
        )
    return mixer_out, attention_out, stored


def solution(mesh):
    placed = (
        P(("parts", "req"), "tp"),
        P(("parts", "req"), "tp", None),
        P(("parts", "req"), "tp"),
        P(("parts", "req"), None, "tp"),
        P(("parts", "req"), None, "tp", None),
        P(None, "tp"),
        P(None, "tp", None),
        P("tp"),
        P("tp"),
        P(("parts", "req"), "tp", None, None),
        P(("parts", "req"), "tp", None),
        P(("parts", "req"), "tp", None),
        P(("parts", "req"), None, "tp", None),
        P("parts"),
        P("parts", None),
        P("parts", None),
        P("parts", None),
    )
    return jax.shard_map(
        body,
        mesh=mesh,
        in_specs=placed,
        out_specs=(
            P(("parts", "req"), "tp"),
            P(("parts", "req"), "tp", None),
            P(("parts", "req"), "tp", None, None),
        ),
        check_vma=False,
    )
```

```python
import functools

import jax
import jax.numpy as jnp
from jax import lax
from jax.experimental import pallas as pl
from jax.experimental.pallas import tpu as pltpu
from jax.sharding import PartitionSpec as P

APPENDED_LENGTH = 256
REQUESTS_PER_IDX = 4
VMEM_LIMIT = 48 * 1024 * 1024
SHARES = (6, 7, 8, 9, 10, 11, 16)
PASSED = 8
HIDDEN = (((1,), (1,)), ((), ()))


def params():
    return pltpu.CompilerParams(vmem_limit_bytes=VMEM_LIMIT)


def any_spec():
    return pl.BlockSpec(memory_space=pl.ANY)


def hbm_spec():
    return pl.BlockSpec(memory_space=pltpu.HBM)


def own_entries(place_ref, base, slots, position, row, emit):
    for j in range(place_ref.shape[1]):
        slot = place_ref[row, j] - base
        mine = (slot >= 0) & (slot < slots)

        @pl.when(mine)
        def _(slot=slot, position=position, j=j):
            emit(position, slot)

        position = position + jnp.where(mine, 1, 0)
    return position


def gather_kernel(ends_ref, place_ref, pool_ref, out_ref, staged, in_sem, out_sem):
    slots = pool_ref.shape[0]
    base = ends_ref[0] * slots

    def row_step(offset, position):
        def emit(at, slot):
            pltpu.make_async_copy(pool_ref.at[slot], staged.at[at], in_sem).start()

        row = ends_ref[1] * REQUESTS_PER_IDX + offset
        return own_entries(place_ref, base, slots, position, row, emit)

    lax.fori_loop(0, REQUESTS_PER_IDX, row_step, jnp.int32(0))
    pltpu.make_async_copy(pool_ref.at[pl.ds(0, staged.shape[0])], staged, in_sem).wait()
    forward = pltpu.make_async_copy(staged, out_ref, out_sem)
    forward.start()
    forward.wait()


def gather_for(ends, place, pool, capacity):
    shape = (capacity,) + pool.shape[1:]
    size = 2 * capacity * pool[0].size
    return pl.pallas_call(
        gather_kernel,
        out_shape=pltpu.HBM(shape, pool.dtype),
        grid_spec=pltpu.PrefetchScalarGridSpec(
            num_scalar_prefetch=2,
            grid=(1,),
            in_specs=[hbm_spec()],
            out_specs=hbm_spec(),
            scratch_shapes=[
                pltpu.VMEM(shape, pool.dtype),
                pltpu.SemaphoreType.DMA,
                pltpu.SemaphoreType.DMA,
            ],
        ),
        cost_estimate=pl.CostEstimate(flops=0, bytes_accessed=2 * size, transcendentals=0),
        compiler_params=params(),
        name="gather_states",
    )(ends, place, pltpu.with_memory_space_constraint(pool, pltpu.HBM))


def scatter_kernel(ends_ref, place_ref, got_ref, *rest):
    out_ref, staged, in_sem, out_sem = rest[-4:]
    slots = out_ref.shape[0]
    base = ends_ref[0] * slots
    fetch = pltpu.make_async_copy(got_ref, staged, in_sem)
    fetch.start()
    fetch.wait()

    def row_step(offset, position):
        def emit(at, slot):
            pltpu.make_async_copy(staged.at[at], out_ref.at[slot], out_sem).start()

        row = ends_ref[1] * REQUESTS_PER_IDX + offset
        return own_entries(place_ref, base, slots, position, row, emit)

    lax.fori_loop(0, REQUESTS_PER_IDX, row_step, jnp.int32(0))
    pltpu.make_async_copy(staged, out_ref.at[pl.ds(0, staged.shape[0])], out_sem).wait()


def scatter_from(ends, place, got, stored, shape):
    held = [] if stored is None else [stored]
    return pl.pallas_call(
        scatter_kernel,
        out_shape=pltpu.HBM(shape, got.dtype),
        grid_spec=pltpu.PrefetchScalarGridSpec(
            num_scalar_prefetch=2,
            grid=(1,),
            in_specs=[hbm_spec()] * (1 + len(held)),
            out_specs=hbm_spec(),
            scratch_shapes=[
                pltpu.VMEM(got.shape, got.dtype),
                pltpu.SemaphoreType.DMA,
                pltpu.SemaphoreType.DMA,
            ],
        ),
        input_output_aliases={3: 0} if held else {},
        cost_estimate=pl.CostEstimate(
            flops=0, bytes_accessed=4 * got.size, transcendentals=0
        ),
        compiler_params=params(),
        name="scatter_states",
    )(ends, place, got, *held)


def used_entry(place_ref, prefix_ref, page, slots, owner, row, j):
    slot = place_ref[row, j] - owner * slots
    return slot, (slot >= 0) & (slot < slots) & (j * page < prefix_ref[row])


def count_used(place_ref, entry, owner, server):
    def count_row(offset, total):
        for j in range(place_ref.shape[1]):
            _, wanted = entry(owner, server * REQUESTS_PER_IDX + offset, j)
            total = total + jnp.where(wanted, 1, 0)
        return total

    return lax.fori_loop(0, REQUESTS_PER_IDX, count_row, jnp.int32(0))


def partner_of(device):
    return device + 1 - 2 * (device % 2)


def send_kernel(counts, limits_ref, place_ref, prefix_ref, pool_ref, *rest):
    outs, (staged, needs, filled, in_sems, out_sems) = rest[: len(counts)], rest[len(counts) :]
    slots, page = pool_ref.shape[0], pool_ref.shape[2]
    me, limit, choice = limits_ref[0], limits_ref[1], limits_ref[2]
    columns = place_ref.shape[1]
    servers, room = staged.shape[:2]
    entry = functools.partial(used_entry, place_ref, prefix_ref, page, slots)

    def count_server(server, carry):
        needs[server] = count_used(place_ref, entry, me, server)
        return carry

    lax.fori_loop(0, servers, count_server, jnp.int32(0))

    def fetch(slot, server, position):
        return pltpu.make_async_copy(
            pool_ref.at[slot], staged.at[server, position], in_sems.at[server, position]
        )

    def fetch_server(server, carry):
        partner = partner_of(server)
        start = needs[partner] - limit

        def fetch_row(offset, rank):
            for j in range(columns):
                slot, wanted = entry(me, server * REQUESTS_PER_IDX + offset, j)
                wanted = wanted & (server != me)
                direct = rank < limit

                @pl.when(wanted & (direct | (partner != me)))
                def _(slot=slot, rank=rank, direct=direct):
                    fetch(
                        slot,
                        jnp.where(direct, server, partner),
                        jnp.where(direct, rank, start + rank),
                    ).start()

                rank = rank + jnp.where(wanted, 1, 0)
            return rank

        lax.fori_loop(0, REQUESTS_PER_IDX, fetch_row, jnp.int32(0))
        passed = jnp.where(partner == me, 0, jnp.maximum(needs[partner] - limit, 0))
        own = jnp.minimum(needs[server], limit)
        filled[server] = jnp.where(server == me, 0, own + passed)
        return carry

    lax.fori_loop(0, servers, fetch_server, jnp.int32(0))

    def forward(server, option):
        count = counts[option]
        return pltpu.make_async_copy(
            staged.at[server, pl.ds(0, count)],
            outs[option].at[pl.ds(server * count, count)],
            out_sems.at[server],
        )

    def forward_server(server, carry):
        for position in range(room):

            @pl.when(position < filled[server])
            def _(position=position):
                fetch(0, server, position).wait()

        for option in range(len(counts)):

            @pl.when(choice == option)
            def _(option=option):
                forward(server, option).start()

        return carry

    lax.fori_loop(0, servers, forward_server, jnp.int32(0))

    def finish_server(server, carry):
        for option in range(len(counts)):

            @pl.when(choice == option)
            def _(option=option):
                forward(server, option).wait()

        return carry

    lax.fori_loop(0, servers, finish_server, jnp.int32(0))


def send_used(counts, limits, place, prefix, pages):
    servers = lax.axis_size("req")
    shapes = [
        pltpu.HBM((servers * count,) + pages.shape[1:], pages.dtype) for count in counts
    ]
    return pl.pallas_call(
        functools.partial(send_kernel, counts),
        out_shape=shapes,
        grid_spec=pltpu.PrefetchScalarGridSpec(
            num_scalar_prefetch=3,
            grid=(1,),
            in_specs=[any_spec()],
            out_specs=[hbm_spec()] * len(counts),
            scratch_shapes=[
                pltpu.VMEM((servers, counts[-1]) + pages.shape[1:], pages.dtype),
                pltpu.SMEM((servers,), jnp.int32),
                pltpu.SMEM((servers,), jnp.int32),
                pltpu.SemaphoreType.DMA((servers, counts[-1])),
                pltpu.SemaphoreType.DMA((servers,)),
            ],
        ),
        cost_estimate=pl.CostEstimate(
            flops=0, bytes_accessed=2 * pages.size * 2, transcendentals=0
        ),
        compiler_params=params(),
        name="send_used_pages",
    )(limits, place, prefix, pages)


def pass_kernel(counts, limits_ref, place_ref, prefix_ref, pool_ref, *rest):
    gots, (out_ref, staged, in_sems, out_sem) = rest[: len(counts)], rest[len(counts) :]
    slots, page = pool_ref.shape[0], pool_ref.shape[2]
    me, limit, choice = limits_ref[0], limits_ref[1], limits_ref[2]
    columns = place_ref.shape[1]
    servers = place_ref.shape[0] // REQUESTS_PER_IDX
    partner = partner_of(me)
    entry = functools.partial(used_entry, place_ref, prefix_ref, page, slots)

    def fetch(source, index, at):
        return pltpu.make_async_copy(source.at[index], staged.at[at], in_sems.at[at])

    def own_pages(at):
        def row_step(offset, carry):
            rank, at = carry
            for j in range(columns):
                slot, wanted = entry(me, partner * REQUESTS_PER_IDX + offset, j)
                take = wanted & (rank >= limit)

                @pl.when(take)
                def _(slot=slot, at=at):
                    fetch(pool_ref, slot, at).start()

                rank = rank + jnp.where(wanted, 1, 0)
                at = at + jnp.where(take, 1, 0)
            return rank, at

        return lax.fori_loop(0, REQUESTS_PER_IDX, row_step, (jnp.int32(0), at))[1]

    def relayed_pages(owner, at):
        start = count_used(place_ref, entry, owner, me)
        more = jnp.maximum(count_used(place_ref, entry, owner, partner) - limit, 0)

        def page_step(step, carry):
            index = owner * limit + start + step
            for option in range(len(counts)):

                @pl.when(choice == option)
                def _(option=option):
                    fetch(gots[option], index, at + step).start()

            return carry

        lax.fori_loop(0, more, page_step, jnp.int32(0))
        return at + more

    def owner_step(owner, at):
        at = lax.cond(owner == me, own_pages, lambda at: at, at)
        outside = (owner != me) & (owner != partner)
        return lax.cond(outside, lambda at: relayed_pages(owner, at), lambda at: at, at)

    total = lax.fori_loop(0, servers, owner_step, jnp.int32(0))
    for position in range(staged.shape[0]):

        @pl.when(position < total)
        def _(position=position):
            fetch(pool_ref, 0, position).wait()

    forward = pltpu.make_async_copy(staged, out_ref, out_sem)
    forward.start()
    forward.wait()


def pass_on(counts, limits, place, prefix, pages, gots):
    shape = (PASSED,) + pages.shape[1:]
    collected = pl.pallas_call(
        functools.partial(pass_kernel, counts),
        out_shape=pltpu.HBM(shape, pages.dtype),
        grid_spec=pltpu.PrefetchScalarGridSpec(
            num_scalar_prefetch=3,
            grid=(1,),
            in_specs=[any_spec()] * (1 + len(gots)),
            out_specs=hbm_spec(),
            scratch_shapes=[
                pltpu.VMEM(shape, pages.dtype),
                pltpu.SemaphoreType.DMA((PASSED,)),
                pltpu.SemaphoreType.DMA,
            ],
        ),
        cost_estimate=pl.CostEstimate(flops=0, bytes_accessed=2**20, transcendentals=0),
        compiler_params=params(),
        name="pass_pages_on",
    )(limits, place, prefix, pages, *gots)
    swaps = [(peer, peer ^ 1) for peer in range(lax.axis_size("req"))]
    return lax.ppermute(collected, "req", swaps)


def unwritten(shapes):
    return pl.pallas_call(
        lambda *refs: None,
        out_shape=shapes,
        out_specs=[hbm_spec()] * len(shapes),
        cost_estimate=pl.CostEstimate(flops=0, bytes_accessed=0, transcendentals=0),
        name="unwritten",
    )()


def conv_silu(buffer, cache_ref, values, weight_ref):
    length = values.shape[0]
    taps = weight_ref.shape[-2]
    buffer[0:8, :] = cache_ref[...]
    buffer[8:, :] = values.astype(jnp.float32)
    start = 8 - (taps - 1)
    summed = weight_ref[0:1, :] * buffer[start : start + length, :]
    for tap in range(1, taps):
        at = start + tap
        summed = summed + weight_ref[tap : tap + 1, :] * buffer[at : at + length, :]
    return jax.nn.silu(summed).astype(jnp.bfloat16)


def inner_kernel(
    heads,
    x_ref,
    x_cache_ref,
    x_weight_ref,
    maps_ref,
    maps_cache_ref,
    maps_weight_ref,
    decay_row_ref,
    decay_col_ref,
    delta_row_ref,
    tail_ref,
    skip_ref,
    partial_ref,
    update_ref,
    output_map_ref,
    x_buffer,
    maps_buffer,
    x_values,
    scaled,
):
    length, width = x_ref.shape
    head_dim = width // heads
    state = maps_ref.shape[1] // 2
    x_values[...] = conv_silu(x_buffer, x_cache_ref, x_ref[...], x_weight_ref)
    maps = conv_silu(maps_buffer, maps_cache_ref, maps_ref[...], maps_weight_ref)
    input_map, output_map = maps[:, :state], maps[:, state:]
    output_map_ref[...] = output_map
    intersection = lax.dot_general(
        output_map, input_map, HIDDEN, preferred_element_type=jnp.float32
    )
    rows = lax.broadcasted_iota(jnp.int32, (length, length), 0)
    columns = lax.broadcasted_iota(jnp.int32, (length, length), 1)
    causal = rows >= columns
    for h in range(heads):
        lanes = slice(h * head_dim, (h + 1) * head_dim)
        gap = decay_col_ref[:, h : h + 1] - decay_row_ref[h : h + 1, :]
        decays = jnp.where(causal, jnp.exp(jnp.where(causal, gap, 0.0)), 0.0)
        mixing = (intersection * decays * delta_row_ref[h : h + 1, :]).astype(jnp.bfloat16)
        x_head = x_values[:, lanes]
        x_wide = x_head.astype(jnp.float32)
        within = jnp.dot(mixing, x_head, preferred_element_type=jnp.float32)
        partial_ref[:, lanes] = within + skip_ref[:, lanes] * x_wide
        scaled[:, lanes] = (x_wide * tail_ref[:, h : h + 1]).astype(jnp.bfloat16)
    update_ref[...] = lax.dot_general(
        scaled[...], input_map, (((0,), (0,)), ((), ())), preferred_element_type=jnp.float32
    )


def state_kernel(me_ref, state_place_ref, store_place_ref, update_ref, decay_row_ref, *rest):
    peers = (len(rest) - 10) // 2
    gots, prior_ref, sends = rest[:peers], rest[peers], rest[peers + 1 : 2 * peers + 1]
    pages, finals, from_kind, from_index, to_kind, to_index, counts, in_sems, out_sems = rest[
        2 * peers + 1 :
    ]
    request, group = pl.program_id(0), pl.program_id(1)
    page_count, heads, page_rows, state = pages.shape
    slots = gots[0].shape[0]
    head_dim = page_count * page_rows
    joint = 16 // page_rows
    me = me_ref[0]

    @pl.when((request == 0) & (group == 0))
    def _():
        for peer in range(2 * peers):
            counts[peer] = 0

        def row_step(offset, carry):
            for j in range(page_count):
                entry = offset * page_count + j
                place = state_place_ref[me * REQUESTS_PER_IDX + offset, j]
                owner = place // slots
                rank = counts[owner]
                counts[owner] = rank + 1
                distance = (me - owner + peers) % peers
                from_kind[entry] = distance
                from_index[entry] = jnp.where(distance == 0, place - me * slots, rank)
                target = store_place_ref[me * REQUESTS_PER_IDX + offset, j] // slots
                to_index[entry] = counts[peers + target]
                counts[peers + target] = to_index[entry] + 1
                to_kind[entry] = (target - me + peers) % peers
            return carry

        lax.fori_loop(0, REQUESTS_PER_IDX, row_step, jnp.int32(0))

    half = pl.ds(group * heads, heads)

    def arrive(j, kind):
        index = from_index[request * page_count + j]
        return pltpu.make_async_copy(gots[kind].at[index, half], pages.at[j], in_sems.at[j])

    def depart(j, kind):
        index = to_index[request * page_count + j]
        return pltpu.make_async_copy(finals.at[j], sends[kind].at[index, half], out_sems.at[j])

    def start_arrival(j):
        for kind in range(peers):

            @pl.when(from_kind[request * page_count + j] == kind)
            def _(kind=kind):
                arrive(j, kind).start()

    def start_departure(j):
        for kind in range(peers):

            @pl.when(to_kind[request * page_count + j] == kind)
            def _(kind=kind):
                depart(j, kind).start()

    def each(start, end, act):
        def step(j, carry):
            act(j)
            return carry

        lax.fori_loop(start, end, step, jnp.int32(0))

    each(0, page_count, start_arrival)
    last = decay_row_ref.shape[1] - 1
    growths = [jnp.exp(decay_row_ref[h : h + 1, last : last + 1]) for h in range(heads)]

    def joint_step(step, carry):
        first = step * joint
        each(first, first + joint, lambda j: arrive(j, 0).wait())
        for h in range(heads):
            rows = pl.ds(pl.multiple_of(h * head_dim + step * 16, 16), 16)
            old = jnp.concatenate(
                [pages[first + i, h].astype(jnp.float32) for i in range(joint)], axis=0
            )
            prior_ref[rows, :] = old.astype(jnp.bfloat16)
            new = growths[h] * old + update_ref[rows, :]
            for i in range(joint):
                finals[first + i, h] = new[i * page_rows : (i + 1) * page_rows].astype(
                    jnp.bfloat16
                )
        each(first, first + joint, start_departure)
        return carry

    lax.fori_loop(0, page_count // joint, joint_step, jnp.int32(0))
    each(0, page_count, lambda j: depart(j, 0).wait())


def output_kernel(heads, partial_ref, output_map_ref, growth_ref, prior_ref, out_ref):
    head_dim = out_ref.shape[1] // heads
    carried = lax.dot_general(
        output_map_ref[...], prior_ref[...], HIDDEN, preferred_element_type=jnp.float32
    )
    for h in range(heads):
        lanes = slice(h * head_dim, (h + 1) * head_dim)
        out_ref[:, lanes] = (
            partial_ref[:, lanes] + growth_ref[:, h : h + 1] * carried[:, lanes]
        ).astype(jnp.bfloat16)


def list_pages(
    counts, passed, limits_ref, place_ref, prefix_ref, slots, page, kinds, indices, amounts, sizes, ranks
):
    me, limit, choice = limits_ref[0], limits_ref[1], limits_ref[2]
    page_count = place_ref.shape[1]
    peers = ranks.shape[1]
    start_row = me * REQUESTS_PER_IDX
    for peer in range(peers):
        ranks[0, peer] = 0
    if passed:

        def count_row(offset, carry):
            tokens = prefix_ref[start_row + offset]
            for j in range(page_count):
                owner = place_ref[start_row + offset, j] // slots
                ranks[0, owner] = ranks[0, owner] + jnp.where(j * page < tokens, 1, 0)
            return carry

        lax.fori_loop(0, REQUESTS_PER_IDX, count_row, jnp.int32(0))
        begin = jnp.int32(0)
        for peer in range(peers):
            ranks[1, peer] = begin
            begin = begin + jnp.where(peer == me, 0, jnp.maximum(ranks[0, peer] - limit, 0))
            ranks[0, peer] = 0
    def place_row(offset, carry):
        tokens = prefix_ref[start_row + offset]
        at, size = jnp.int32(0), jnp.int32(0)
        for j in range(page_count):
            place = place_ref[start_row + offset, j]
            owner = place // slots
            rank = ranks[0, owner]
            used = j * page < tokens
            ranks[0, owner] = rank + jnp.where(used, 1, 0)
            here = owner == me
            late = (rank >= limit) & jnp.logical_not(here)
            if passed:
                take = used & late
                kind = jnp.int32(0)
                index = ranks[1, owner] + rank - limit
            else:
                take = used & jnp.logical_not(late)
                kind = jnp.where(here, len(counts), choice)
                index = jnp.where(here, place - me * slots, owner * limit + rank)

            @pl.when(take)
            def _(at=at, kind=kind, index=index):
                kinds[offset * page_count + at] = kind
                indices[offset * page_count + at] = index

            at = at + jnp.where(take, 1, 0)
            size = size + jnp.where(take, jnp.minimum(page, tokens - j * page), 0)
        amounts[offset] = at
        sizes[offset] = size
        return carry

    lax.fori_loop(0, REQUESTS_PER_IDX, place_row, jnp.int32(0))


def score(scale, keys, query):
    return lax.dot_general(keys, query, HIDDEN, preferred_element_type=jnp.float32) * scale


def weigh(values, exponent):
    return lax.dot_general(
        values,
        exponent.astype(jnp.bfloat16),
        (((0,), (0,)), ((), ())),
        preferred_element_type=jnp.float32,
    )


def add_pages(scale, query, size, chunk, cached_kv, stats_ref, sums_ref):
    head_dim = query.shape[1]
    keys_at = lax.broadcasted_iota(jnp.int32, (chunk, query.shape[0]), 0)

    def chunk_step(step, carry):
        start = pl.multiple_of(step * chunk, chunk)
        scores = score(scale, cached_kv[pl.ds(start, chunk), :head_dim], query)
        scores = jnp.where(keys_at < size - start, scores, -jnp.inf)
        old = stats_ref[0:1, :]
        top = jnp.maximum(old, jnp.max(scores, axis=0, keepdims=True))
        fade = jnp.exp(old - top)
        exponent = jnp.exp(scores - top)
        stats_ref[0:1, :] = top
        stats_ref[1:2, :] = stats_ref[1:2, :] * fade + jnp.sum(exponent, axis=0, keepdims=True)
        sums_ref[...] = sums_ref[...] * fade + weigh(
            cached_kv[pl.ds(start, chunk), head_dim:], exponent
        )
        return carry

    lax.fori_loop(0, (size + chunk - 1) // chunk, chunk_step, jnp.int32(0))


def attend_kernel(scale, counts, limits_ref, place_ref, prefix_ref, pool_ref, *rest):
    gots = rest[: len(counts)]
    query_ref, fresh_ref, sums_ref, stats_ref = rest[len(counts) : len(counts) + 4]
    cached_kv, kinds, indices, amounts, sizes, ranks, sems = rest[len(counts) + 4 :]
    request, kv_head = pl.program_id(0), pl.program_id(1)
    per_kv, length, head_dim = query_ref.shape
    slots, page = pool_ref.shape[0], pool_ref.shape[2]
    page_count = place_ref.shape[1]

    @pl.when((request == 0) & (kv_head == 0))
    def _():
        cached_kv[...] = jnp.zeros_like(cached_kv)
        list_pages(
            counts, False, limits_ref, place_ref, prefix_ref, slots, page,
            kinds, indices, amounts, sizes, ranks,
        )

    amount = amounts[request]

    def target(j):
        return cached_kv.at[pl.ds(pl.multiple_of(j * page, page), page)]

    def start_copy(j, carry):
        entry = request * page_count + j
        for kind, source in enumerate(gots + (pool_ref,)):

            @pl.when(kinds[entry] == kind)
            def _(source=source):
                pltpu.make_async_copy(
                    source.at[indices[entry], kv_head], target(j), sems.at[j]
                ).start()

        return carry

    lax.fori_loop(0, amount, start_copy, jnp.int32(0))
    query = query_ref[...].reshape(per_kv * length, head_dim)
    keys_at = lax.broadcasted_iota(jnp.int32, (length, per_kv * length), 0)
    queries_at = lax.broadcasted_iota(jnp.int32, (length, per_kv * length), 1) % length
    scores = score(scale, fresh_ref[:, :head_dim], query)
    scores = jnp.where(keys_at <= queries_at, scores, -jnp.inf)
    top = jnp.max(scores, axis=0, keepdims=True)
    exponent = jnp.exp(scores - top)
    stats_ref[0:1, :] = top
    stats_ref[1:2, :] = jnp.sum(exponent, axis=0, keepdims=True)
    sums_ref[...] = weigh(fresh_ref[:, head_dim:], exponent)

    def wait_copy(j, carry):
        pltpu.make_async_copy(pool_ref.at[0, kv_head], target(j), sems.at[j]).wait()
        return carry

    lax.fori_loop(0, amount, wait_copy, jnp.int32(0))
    add_pages(scale, query, sizes[request], length, cached_kv, stats_ref, sums_ref)


def attend_passed_kernel(
    scale,
    counts,
    slots,
    limits_ref,
    place_ref,
    prefix_ref,
    passed_ref,
    query_ref,
    sums_in_ref,
    stats_in_ref,
    out_ref,
    cached_kv,
    sums_ref,
    stats_ref,
    kinds,
    indices,
    amounts,
    sizes,
    ranks,
    sems,
):
    request, kv_head = pl.program_id(0), pl.program_id(1)
    per_kv, length, head_dim = query_ref.shape
    page = passed_ref.shape[2]
    page_count = place_ref.shape[1]

    @pl.when((request == 0) & (kv_head == 0))
    def _():
        cached_kv[...] = jnp.zeros_like(cached_kv)
        list_pages(
            counts, True, limits_ref, place_ref, prefix_ref, slots, page,
            kinds, indices, amounts, sizes, ranks,
        )

    amount = amounts[request]

    def fetch(j, index):
        target = cached_kv.at[pl.ds(pl.multiple_of(j * page, page), page)]
        return pltpu.make_async_copy(passed_ref.at[index, kv_head], target, sems.at[j])

    def start_copy(j, carry):
        fetch(j, indices[request * page_count + j]).start()
        return carry

    def wait_copy(j, carry):
        fetch(j, 0).wait()
        return carry

    @pl.when(amount == 0)
    def _():
        out_ref[...] = (
            (sums_in_ref[...] / stats_in_ref[1:2, :]).T.astype(jnp.bfloat16).reshape(out_ref.shape)
        )

    @pl.when(amount > 0)
    def _():
        lax.fori_loop(0, amount, start_copy, jnp.int32(0))
        sums_ref[...] = sums_in_ref[...]
        stats_ref[...] = stats_in_ref[...]
        lax.fori_loop(0, amount, wait_copy, jnp.int32(0))
        query = query_ref[...].reshape(per_kv * length, head_dim)
        add_pages(scale, query, sizes[request], length, cached_kv, stats_ref, sums_ref)
        out_ref[...] = (
            (sums_ref[...] / stats_ref[1:2, :]).T.astype(jnp.bfloat16).reshape(out_ref.shape)
        )


def body(
    mixer_in,
    maps_in,
    delta_raw,
    conv_cache,
    maps_cache,
    conv_weight,
    maps_weight,
    decay_log,
    skip_gain,
    state_pool,
    queries,
    suffix_keyvals,
    page_pool,
    prefix_tokens,
    page_place,
    state_place,
    store_place,
):
    peers = lax.axis_size("req")
    me = lax.axis_index("req").astype(jnp.int32).reshape(1)
    requests, length = REQUESTS_PER_IDX, APPENDED_LENGTH
    groups = maps_in.shape[1]
    state = maps_in.shape[2] // 2
    heads = delta_raw.shape[1]
    per_group = heads // groups
    width = mixer_in.shape[1]
    group_width = width // groups
    head_dim = width // heads
    slots, _, page_rows, _ = state_pool.shape
    page_count = state_place.shape[1]
    kv_heads = page_pool.shape[2]
    attend_dim = queries.shape[2]
    per_kv = queries.shape[1] // kv_heads
    page = page_pool.shape[1]
    prefix_pages = page_place.shape[1]
    page_slots = page_pool.shape[0]
    pair_pages = requests * prefix_pages // peers
    taps = conv_weight.shape[0]

    def exchange(pages):
        return lax.all_to_all(pages, "req", split_axis=0, concat_axis=0, tiled=True)

    capacity = requests * page_count // peers
    distances = range(1, peers)

    def send_to(distance, pages):
        return lax.ppermute(
            pages, "req", [(peer, (peer + distance) % peers) for peer in range(peers)]
        )

    def ends(distance):
        return jnp.concatenate([me, (me + distance) % peers])

    state_gots = [state_pool] + [
        send_to(distance, gather_for(ends(distance), state_place, state_pool, capacity))
        for distance in distances
    ]

    counts = tuple(sorted({max(1, pair_pages * share // 16) for share in SHARES}))
    used = jnp.arange(prefix_pages)[None, :] * page < prefix_tokens[:, None]
    holders = page_place // page_slots
    pairs = used[:, :, None] & (holders[:, :, None] == jnp.arange(peers)[None, None, :])
    needs = jnp.sum(pairs.reshape(peers, -1, peers).astype(jnp.int32), axis=1)
    places = jnp.arange(peers)
    both = jnp.sum(needs.reshape(peers // 2, 2, peers), axis=1)
    outside = jnp.arange(peers // 2)[:, None] != places[None, :] // 2
    limit_table = jnp.array(counts, jnp.int32)
    crowded = jnp.max(jnp.where(outside, both, 0)) > 2 * limit_table
    rests = jnp.maximum(needs[None] - limit_table[:, None, None], 0)
    rests = jnp.where(places[:, None] != places[None, :], rests, 0)
    crowded = crowded | (jnp.max(jnp.sum(rests, axis=2), axis=1) > PASSED)
    choice = jnp.sum(crowded.astype(jnp.int32))
    limit = jnp.sum(jnp.where(jnp.arange(len(counts)) == choice, limit_table, 0))
    limits = jnp.stack([me[0], limit, choice])
    pages_by_head = page_pool.transpose(0, 2, 1, 3)
    page_sends = send_used(counts, limits, page_place, prefix_tokens, pages_by_head)

    delta = jax.nn.softplus(delta_raw.T.astype(jnp.float32)).reshape(heads, requests, length)
    log_decay = jnp.cumsum(-delta * jnp.exp(decay_log)[:, None, None], axis=2)
    tail = jnp.exp(log_decay[:, :, -1:] - log_decay) * delta
    growth = jnp.exp(log_decay)

    def by_rows(values):
        return values.reshape(groups, per_group, requests, length).transpose(2, 0, 1, 3)

    def by_columns(values):
        return values.reshape(groups, per_group, requests, length).transpose(2, 0, 3, 1)

    decay_row = by_rows(log_decay)
    maps_split = maps_in.transpose(1, 0, 2)
    empty = 8 - (taps - 1)
    x_cache = jnp.pad(conv_cache.astype(jnp.float32), ((0, 0), (empty, 0), (0, 0)))
    maps_edge = jnp.pad(
        maps_cache.transpose(0, 2, 1, 3).astype(jnp.float32), ((0, 0), (0, 0), (empty, 0), (0, 0))
    )
    row_block = pl.BlockSpec((None, None, per_group, length), lambda r, g: (r, g, 0, 0))
    column_block = pl.BlockSpec((None, None, length, per_group), lambda r, g: (r, g, 0, 0))
    x_block = pl.BlockSpec((length, group_width), lambda r, g: (r, g))
    update_block = pl.BlockSpec((None, None, group_width, state), lambda r, g: (r, g, 0, 0))
    map_block = pl.BlockSpec((None, length, state), lambda r, g: (g, r, 0))
    partial, update, output_map = pl.pallas_call(
        functools.partial(inner_kernel, per_group),
        grid=(requests, groups),
        in_specs=[
            x_block,
            pl.BlockSpec((None, 8, group_width), lambda r, g: (r, 0, g)),
            pl.BlockSpec((taps, group_width), lambda r, g: (0, g)),
            pl.BlockSpec((None, length, 2 * state), lambda r, g: (g, r, 0)),
            pl.BlockSpec((None, None, 8, 2 * state), lambda r, g: (r, g, 0, 0)),
            pl.BlockSpec((None, taps, 2 * state), lambda r, g: (g, 0, 0)),
            row_block,
            column_block,
            row_block,
            column_block,
            pl.BlockSpec((1, group_width), lambda r, g: (0, g)),
        ],
        out_specs=[x_block, update_block, map_block],
        out_shape=[
            jax.ShapeDtypeStruct((requests * length, width), jnp.float32),
            jax.ShapeDtypeStruct((requests, groups, group_width, state), jnp.float32),
            jax.ShapeDtypeStruct((groups, requests * length, state), jnp.bfloat16),
        ],
        scratch_shapes=[
            pltpu.VMEM((8 + length, group_width), jnp.float32),
            pltpu.VMEM((8 + length, 2 * state), jnp.float32),
            pltpu.VMEM((length, group_width), jnp.bfloat16),
            pltpu.VMEM((length, group_width), jnp.bfloat16),
        ],
        cost_estimate=pl.CostEstimate(
            flops=3 * requests * length * width * state,
            bytes_accessed=32 * 2**20,
            transcendentals=requests * heads * length * length,
        ),
        compiler_params=params(),
        name="mix_new_tokens",
    )(
        mixer_in,
        x_cache,
        conv_weight.astype(jnp.float32),
        maps_split,
        maps_edge,
        maps_weight.transpose(1, 0, 2).astype(jnp.float32),
        decay_row,
        by_columns(log_decay),
        by_rows(delta),
        by_columns(tail),
        jnp.repeat(skip_gain, head_dim).reshape(1, width),
    )
    growth_col = by_columns(growth)
    grouped_queries = queries.reshape(requests, length, kv_heads, per_kv, attend_dim).transpose(
        0, 2, 3, 1, 4
    )
    fresh = suffix_keyvals.transpose(1, 0, 2)

    page_sends, state_gots, partial, update, output_map, growth_col, decay_row = (
        lax.optimization_barrier(
            (page_sends, state_gots, partial, update, output_map, growth_col, decay_row)
        )
    )
    state_block = pl.BlockSpec((None, None, group_width, state), lambda r, g, *_: (r, g, 0, 0))

    def advance(at, sends, state_gots, update, decay_row):
        shapes = [pltpu.HBM(sent.shape, sent.dtype) for sent in sends]
        others = list(unwritten(shapes[:at] + shapes[at + 1 :])) if len(shapes) > 1 else []
        gots = tuple(others[:at] + [exchange(sends[at])] + others[at:])
        prior, *final_sends = pl.pallas_call(
            state_kernel,
            grid_spec=pltpu.PrefetchScalarGridSpec(
                num_scalar_prefetch=3,
                grid=(requests, groups),
                in_specs=[
                    state_block,
                    pl.BlockSpec((None, None, per_group, length), lambda r, g, *_: (r, g, 0, 0)),
                ]
                + [any_spec()] * peers,
                out_specs=[state_block] + [hbm_spec()] * peers,
                scratch_shapes=[
                    pltpu.VMEM((page_count, per_group, page_rows, state), jnp.bfloat16),
                    pltpu.VMEM((page_count, per_group, page_rows, state), jnp.bfloat16),
                    *[pltpu.SMEM((requests * page_count,), jnp.int32)] * 4,
                    pltpu.SMEM((2 * peers,), jnp.int32),
                    pltpu.SemaphoreType.DMA((page_count,)),
                    pltpu.SemaphoreType.DMA((page_count,)),
                ],
            ),
            out_shape=[
                jax.ShapeDtypeStruct(update.shape, jnp.bfloat16),
                *[pltpu.HBM((capacity,) + state_pool.shape[1:], jnp.bfloat16)] * peers,
            ],
            cost_estimate=pl.CostEstimate(
                flops=4 * update.size, bytes_accessed=20 * 2**20, transcendentals=0
            ),
            compiler_params=params(),
            name="advance_states",
        )(me, state_place, store_place, update, decay_row, *state_gots)
        return gots, prior, final_sends

    page_gots, prior, final_sends = lax.switch(
        choice,
        [functools.partial(advance, at) for at in range(len(counts))],
        tuple(page_sends),
        state_gots,
        update,
        decay_row,
    )
    final_gots = [final_sends[0]] + [
        send_to(distance, final_sends[distance]) for distance in distances
    ]
    mixer_out = pl.pallas_call(
        functools.partial(output_kernel, per_group),
        grid=(requests, groups),
        in_specs=[
            x_block,
            map_block,
            column_block,
            pl.BlockSpec((None, None, group_width, state), lambda r, g: (r, g, 0, 0)),
        ],
        out_specs=x_block,
        out_shape=jax.ShapeDtypeStruct((requests * length, width), jnp.bfloat16),
        cost_estimate=pl.CostEstimate(
            flops=2 * requests * length * width * state,
            bytes_accessed=18 * 2**20,
            transcendentals=0,
        ),
        compiler_params=params(),
        name="add_carried",
    )(partial, output_map, growth_col, prior)
    passed = pass_on(counts, limits, page_place, prefix_tokens, pages_by_head, page_gots)
    stored = None
    for distance, got in enumerate(final_gots):
        if distance == peers - 1:
            passed, stored = lax.optimization_barrier((passed, stored))
        stored = scatter_from(
            ends(peers - distance), store_place, got, stored, state_pool.shape
        )
    rows = per_kv * length
    head_block = pl.BlockSpec(
        (None, None, per_kv, length, attend_dim), lambda r, e, *_: (r, e, 0, 0, 0)
    )
    sums_block = pl.BlockSpec((None, None, attend_dim, rows), lambda r, e, *_: (r, e, 0, 0))
    stats_block = pl.BlockSpec((None, None, 2, rows), lambda r, e, *_: (r, e, 0, 0))
    lists = [
        pltpu.SMEM((requests * prefix_pages,), jnp.int32),
        pltpu.SMEM((requests * prefix_pages,), jnp.int32),
        pltpu.SMEM((requests,), jnp.int32),
        pltpu.SMEM((requests,), jnp.int32),
        pltpu.SMEM((2, peers), jnp.int32),
    ]
    sums, stats = pl.pallas_call(
        functools.partial(attend_kernel, attend_dim**-0.5, counts),
        grid_spec=pltpu.PrefetchScalarGridSpec(
            num_scalar_prefetch=3,
            grid=(requests, kv_heads),
            in_specs=[any_spec()] * (len(page_gots) + 1)
            + [
                head_block,
                pl.BlockSpec((None, length, 2 * attend_dim), lambda r, e, *_: (e, r, 0)),
            ],
            out_specs=[sums_block, stats_block],
            scratch_shapes=[
                pltpu.VMEM((prefix_pages * page, 2 * attend_dim), jnp.bfloat16),
                *lists,
                pltpu.SemaphoreType.DMA((prefix_pages,)),
            ],
        ),
        out_shape=[
            jax.ShapeDtypeStruct((requests, kv_heads, attend_dim, rows), jnp.float32),
            jax.ShapeDtypeStruct((requests, kv_heads, 2, rows), jnp.float32),
        ],
        cost_estimate=pl.CostEstimate(
            flops=4 * queries.size * (prefix_pages * page + length),
            bytes_accessed=16 * 2**20,
            transcendentals=queries.shape[0] * queries.shape[1] * (prefix_pages * page),
        ),
        compiler_params=params(),
        name="attend",
    )(
        limits,
        page_place,
        prefix_tokens,
        pages_by_head,
        *page_gots,
        grouped_queries,
        fresh,
    )
    attended = pl.pallas_call(
        functools.partial(attend_passed_kernel, attend_dim**-0.5, counts, page_slots),
        grid_spec=pltpu.PrefetchScalarGridSpec(
            num_scalar_prefetch=3,
            grid=(requests, kv_heads),
            in_specs=[any_spec(), head_block, sums_block, stats_block],
            out_specs=head_block,
            scratch_shapes=[
                pltpu.VMEM((-(-PASSED * page // length) * length, 2 * attend_dim), jnp.bfloat16),
                pltpu.VMEM((attend_dim, rows), jnp.float32),
                pltpu.VMEM((2, rows), jnp.float32),
                *lists,
                pltpu.SemaphoreType.DMA((PASSED,)),
            ],
        ),
        out_shape=jax.ShapeDtypeStruct(grouped_queries.shape, jnp.bfloat16),
        cost_estimate=pl.CostEstimate(
            flops=queries.size * PASSED * page,
            bytes_accessed=8 * 2**20,
            transcendentals=queries.shape[0] * queries.shape[1] * PASSED * page // 4,
        ),
        compiler_params=params(),
        name="attend_passed",
    )(limits, page_place, prefix_tokens, passed, grouped_queries, sums, stats)
    attention_out = attended.transpose(0, 3, 1, 2, 4).reshape(queries.shape)
    return mixer_out, attention_out, stored


def solution(mesh):
    placed = (
        P(("parts", "req"), "tp"),
        P(("parts", "req"), "tp", None),
        P(("parts", "req"), "tp"),
        P(("parts", "req"), None, "tp"),
        P(("parts", "req"), None, "tp", None),
        P(None, "tp"),
        P(None, "tp", None),
        P("tp"),
        P("tp"),
        P(("parts", "req"), "tp", None, None),
        P(("parts", "req"), "tp", None),
        P(("parts", "req"), "tp", None),
        P(("parts", "req"), None, "tp", None),
        P("parts"),
        P("parts", None),
        P("parts", None),
        P("parts", None),
    )
    return jax.shard_map(
        body,
        mesh=mesh,
        in_specs=placed,
        out_specs=(
            P(("parts", "req"), "tp"),
            P(("parts", "req"), "tp", None),
            P(("parts", "req"), "tp", None, None),
        ),
        check_vma=False,
    )
```

```python
import functools

import jax
import jax.numpy as jnp
from jax import lax
from jax.experimental import pallas as pl
from jax.experimental.pallas import tpu as pltpu
from jax.sharding import PartitionSpec as P

APPENDED_LENGTH = 256
REQUESTS_PER_IDX = 4
VMEM_LIMIT = 48 * 1024 * 1024
SHARES = (6, 7, 8, 9, 10, 11, 16)
PASSED = 8
HIDDEN = (((1,), (1,)), ((), ()))


def params():
    return pltpu.CompilerParams(vmem_limit_bytes=VMEM_LIMIT)


def any_spec():
    return pl.BlockSpec(memory_space=pl.ANY)


def hbm_spec():
    return pl.BlockSpec(memory_space=pltpu.HBM)


def own_entries(place_ref, base, slots, position, row, emit):
    for j in range(place_ref.shape[1]):
        slot = place_ref[row, j] - base
        mine = (slot >= 0) & (slot < slots)

        @pl.when(mine)
        def _(slot=slot, position=position, j=j):
            emit(position, slot)

        position = position + jnp.where(mine, 1, 0)
    return position


def gather_kernel(ends_ref, place_ref, pool_ref, out_ref, staged, in_sem, out_sem):
    slots = pool_ref.shape[0]
    base = ends_ref[0] * slots

    def row_step(offset, position):
        def emit(at, slot):
            pltpu.make_async_copy(pool_ref.at[slot], staged.at[at], in_sem).start()

        row = ends_ref[1] * REQUESTS_PER_IDX + offset
        return own_entries(place_ref, base, slots, position, row, emit)

    lax.fori_loop(0, REQUESTS_PER_IDX, row_step, jnp.int32(0))
    pltpu.make_async_copy(pool_ref.at[pl.ds(0, staged.shape[0])], staged, in_sem).wait()
    forward = pltpu.make_async_copy(staged, out_ref, out_sem)
    forward.start()
    forward.wait()


def gather_for(ends, place, pool, capacity):
    shape = (capacity,) + pool.shape[1:]
    size = 2 * capacity * pool[0].size
    return pl.pallas_call(
        gather_kernel,
        out_shape=pltpu.HBM(shape, pool.dtype),
        grid_spec=pltpu.PrefetchScalarGridSpec(
            num_scalar_prefetch=2,
            grid=(1,),
            in_specs=[hbm_spec()],
            out_specs=hbm_spec(),
            scratch_shapes=[
                pltpu.VMEM(shape, pool.dtype),
                pltpu.SemaphoreType.DMA,
                pltpu.SemaphoreType.DMA,
            ],
        ),
        cost_estimate=pl.CostEstimate(flops=0, bytes_accessed=2 * size, transcendentals=0),
        compiler_params=params(),
        name="gather_states",
    )(ends, place, pltpu.with_memory_space_constraint(pool, pltpu.HBM))


def scatter_kernel(ends_ref, place_ref, got_ref, *rest):
    out_ref, staged, in_sem, out_sem = rest[-4:]
    slots = out_ref.shape[0]
    base = ends_ref[0] * slots
    fetch = pltpu.make_async_copy(got_ref, staged, in_sem)
    fetch.start()
    fetch.wait()

    def row_step(offset, position):
        def emit(at, slot):
            pltpu.make_async_copy(staged.at[at], out_ref.at[slot], out_sem).start()

        row = ends_ref[1] * REQUESTS_PER_IDX + offset
        return own_entries(place_ref, base, slots, position, row, emit)

    lax.fori_loop(0, REQUESTS_PER_IDX, row_step, jnp.int32(0))
    pltpu.make_async_copy(staged, out_ref.at[pl.ds(0, staged.shape[0])], out_sem).wait()


def scatter_from(ends, place, got, stored, shape):
    held = [] if stored is None else [stored]
    return pl.pallas_call(
        scatter_kernel,
        out_shape=pltpu.HBM(shape, got.dtype),
        grid_spec=pltpu.PrefetchScalarGridSpec(
            num_scalar_prefetch=2,
            grid=(1,),
            in_specs=[hbm_spec()] * (1 + len(held)),
            out_specs=hbm_spec(),
            scratch_shapes=[
                pltpu.VMEM(got.shape, got.dtype),
                pltpu.SemaphoreType.DMA,
                pltpu.SemaphoreType.DMA,
            ],
        ),
        input_output_aliases={3: 0} if held else {},
        cost_estimate=pl.CostEstimate(
            flops=0, bytes_accessed=4 * got.size, transcendentals=0
        ),
        compiler_params=params(),
        name="scatter_states",
    )(ends, place, got, *held)


def used_entry(place_ref, prefix_ref, page, slots, owner, row, j):
    slot = place_ref[row, j] - owner * slots
    return slot, (slot >= 0) & (slot < slots) & (j * page < prefix_ref[row])


def count_used(place_ref, entry, owner, server):
    def count_row(offset, total):
        for j in range(place_ref.shape[1]):
            _, wanted = entry(owner, server * REQUESTS_PER_IDX + offset, j)
            total = total + jnp.where(wanted, 1, 0)
        return total

    return lax.fori_loop(0, REQUESTS_PER_IDX, count_row, jnp.int32(0))


def partner_of(device):
    return device + 1 - 2 * (device % 2)


def send_kernel(counts, limits_ref, place_ref, prefix_ref, pool_ref, *rest):
    outs, (staged, needs, filled, in_sems, out_sems) = rest[: len(counts)], rest[len(counts) :]
    slots, page = pool_ref.shape[0], pool_ref.shape[2]
    me, limit, choice = limits_ref[0], limits_ref[1], limits_ref[2]
    columns = place_ref.shape[1]
    servers, room = staged.shape[:2]
    entry = functools.partial(used_entry, place_ref, prefix_ref, page, slots)

    def count_server(server, carry):
        needs[server] = count_used(place_ref, entry, me, server)
        return carry

    lax.fori_loop(0, servers, count_server, jnp.int32(0))

    def fetch(slot, server, position):
        return pltpu.make_async_copy(
            pool_ref.at[slot], staged.at[server, position], in_sems.at[server, position]
        )

    def fetch_server(server, carry):
        partner = partner_of(server)
        start = needs[partner] - limit

        def fetch_row(offset, rank):
            for j in range(columns):
                slot, wanted = entry(me, server * REQUESTS_PER_IDX + offset, j)
                wanted = wanted & (server != me)
                direct = rank < limit

                @pl.when(wanted & (direct | (partner != me)))
                def _(slot=slot, rank=rank, direct=direct):
                    fetch(
                        slot,
                        jnp.where(direct, server, partner),
                        jnp.where(direct, rank, start + rank),
                    ).start()

                rank = rank + jnp.where(wanted, 1, 0)
            return rank

        lax.fori_loop(0, REQUESTS_PER_IDX, fetch_row, jnp.int32(0))
        passed = jnp.where(partner == me, 0, jnp.maximum(needs[partner] - limit, 0))
        own = jnp.minimum(needs[server], limit)
        filled[server] = jnp.where(server == me, 0, own + passed)
        return carry

    lax.fori_loop(0, servers, fetch_server, jnp.int32(0))

    def forward(server, option):
        count = counts[option]
        return pltpu.make_async_copy(
            staged.at[server, pl.ds(0, count)],
            outs[option].at[pl.ds(server * count, count)],
            out_sems.at[server],
        )

    def forward_server(server, carry):
        for position in range(room):

            @pl.when(position < filled[server])
            def _(position=position):
                fetch(0, server, position).wait()

        for option in range(len(counts)):

            @pl.when(choice == option)
            def _(option=option):
                forward(server, option).start()

        return carry

    lax.fori_loop(0, servers, forward_server, jnp.int32(0))

    def finish_server(server, carry):
        for option in range(len(counts)):

            @pl.when(choice == option)
            def _(option=option):
                forward(server, option).wait()

        return carry

    lax.fori_loop(0, servers, finish_server, jnp.int32(0))


def send_used(counts, limits, place, prefix, pages):
    servers = lax.axis_size("req")
    shapes = [
        pltpu.HBM((servers * count,) + pages.shape[1:], pages.dtype) for count in counts
    ]
    return pl.pallas_call(
        functools.partial(send_kernel, counts),
        out_shape=shapes,
        grid_spec=pltpu.PrefetchScalarGridSpec(
            num_scalar_prefetch=3,
            grid=(1,),
            in_specs=[any_spec()],
            out_specs=[hbm_spec()] * len(counts),
            scratch_shapes=[
                pltpu.VMEM((servers, counts[-1]) + pages.shape[1:], pages.dtype),
                pltpu.SMEM((servers,), jnp.int32),
                pltpu.SMEM((servers,), jnp.int32),
                pltpu.SemaphoreType.DMA((servers, counts[-1])),
                pltpu.SemaphoreType.DMA((servers,)),
            ],
        ),
        cost_estimate=pl.CostEstimate(
            flops=0, bytes_accessed=2 * pages.size * 2, transcendentals=0
        ),
        compiler_params=params(),
        name="send_used_pages",
    )(limits, place, prefix, pages)


def pass_kernel(counts, limits_ref, place_ref, prefix_ref, pool_ref, *rest):
    gots, (out_ref, staged, in_sems, out_sem) = rest[: len(counts)], rest[len(counts) :]
    slots, page = pool_ref.shape[0], pool_ref.shape[2]
    me, limit, choice = limits_ref[0], limits_ref[1], limits_ref[2]
    columns = place_ref.shape[1]
    servers = place_ref.shape[0] // REQUESTS_PER_IDX
    partner = partner_of(me)
    entry = functools.partial(used_entry, place_ref, prefix_ref, page, slots)

    def fetch(source, index, at):
        return pltpu.make_async_copy(source.at[index], staged.at[at], in_sems.at[at])

    def own_pages(at):
        def row_step(offset, carry):
            rank, at = carry
            for j in range(columns):
                slot, wanted = entry(me, partner * REQUESTS_PER_IDX + offset, j)
                take = wanted & (rank >= limit)

                @pl.when(take)
                def _(slot=slot, at=at):
                    fetch(pool_ref, slot, at).start()

                rank = rank + jnp.where(wanted, 1, 0)
                at = at + jnp.where(take, 1, 0)
            return rank, at

        return lax.fori_loop(0, REQUESTS_PER_IDX, row_step, (jnp.int32(0), at))[1]

    def relayed_pages(owner, at):
        start = count_used(place_ref, entry, owner, me)
        more = jnp.maximum(count_used(place_ref, entry, owner, partner) - limit, 0)

        def page_step(step, carry):
            index = owner * limit + start + step
            for option in range(len(counts)):

                @pl.when(choice == option)
                def _(option=option):
                    fetch(gots[option], index, at + step).start()

            return carry

        lax.fori_loop(0, more, page_step, jnp.int32(0))
        return at + more

    def owner_step(owner, at):
        at = lax.cond(owner == me, own_pages, lambda at: at, at)
        outside = (owner != me) & (owner != partner)
        return lax.cond(outside, lambda at: relayed_pages(owner, at), lambda at: at, at)

    total = lax.fori_loop(0, servers, owner_step, jnp.int32(0))
    for position in range(staged.shape[0]):

        @pl.when(position < total)
        def _(position=position):
            fetch(pool_ref, 0, position).wait()

    forward = pltpu.make_async_copy(staged, out_ref, out_sem)
    forward.start()
    forward.wait()


def pass_on(counts, limits, place, prefix, pages, gots):
    shape = (PASSED,) + pages.shape[1:]
    collected = pl.pallas_call(
        functools.partial(pass_kernel, counts),
        out_shape=pltpu.HBM(shape, pages.dtype),
        grid_spec=pltpu.PrefetchScalarGridSpec(
            num_scalar_prefetch=3,
            grid=(1,),
            in_specs=[any_spec()] * (1 + len(gots)),
            out_specs=hbm_spec(),
            scratch_shapes=[
                pltpu.VMEM(shape, pages.dtype),
                pltpu.SemaphoreType.DMA((PASSED,)),
                pltpu.SemaphoreType.DMA,
            ],
        ),
        cost_estimate=pl.CostEstimate(flops=0, bytes_accessed=2**20, transcendentals=0),
        compiler_params=params(),
        name="pass_pages_on",
    )(limits, place, prefix, pages, *gots)
    swaps = [(peer, peer ^ 1) for peer in range(lax.axis_size("req"))]
    return lax.ppermute(collected, "req", swaps)


def unwritten(shapes):
    return pl.pallas_call(
        lambda *refs: None,
        out_shape=shapes,
        out_specs=[hbm_spec()] * len(shapes),
        cost_estimate=pl.CostEstimate(flops=0, bytes_accessed=0, transcendentals=0),
        name="unwritten",
    )()


def conv_silu(buffer, cache_ref, values, weight_ref):
    length = values.shape[0]
    taps = weight_ref.shape[-2]
    buffer[0:8, :] = cache_ref[...]
    buffer[8:, :] = values.astype(jnp.float32)
    start = 8 - (taps - 1)
    summed = weight_ref[0:1, :] * buffer[start : start + length, :]
    for tap in range(1, taps):
        at = start + tap
        summed = summed + weight_ref[tap : tap + 1, :] * buffer[at : at + length, :]
    return jax.nn.silu(summed).astype(jnp.bfloat16)


def inner_kernel(
    heads,
    x_ref,
    x_cache_ref,
    x_weight_ref,
    maps_ref,
    maps_cache_ref,
    maps_weight_ref,
    decay_row_ref,
    decay_col_ref,
    delta_row_ref,
    tail_ref,
    skip_ref,
    partial_ref,
    update_ref,
    output_map_ref,
    x_buffer,
    maps_buffer,
    x_values,
    scaled,
):
    length, width = x_ref.shape
    head_dim = width // heads
    state = maps_ref.shape[1] // 2
    x_values[...] = conv_silu(x_buffer, x_cache_ref, x_ref[...], x_weight_ref)
    maps = conv_silu(maps_buffer, maps_cache_ref, maps_ref[...], maps_weight_ref)
    input_map, output_map = maps[:, :state], maps[:, state:]
    output_map_ref[...] = output_map
    intersection = lax.dot_general(
        output_map, input_map, HIDDEN, preferred_element_type=jnp.float32
    )
    rows = lax.broadcasted_iota(jnp.int32, (length, length), 0)
    columns = lax.broadcasted_iota(jnp.int32, (length, length), 1)
    causal = rows >= columns
    for h in range(heads):
        lanes = slice(h * head_dim, (h + 1) * head_dim)
        gap = decay_col_ref[:, h : h + 1] - decay_row_ref[h : h + 1, :]
        decays = jnp.where(causal, jnp.exp(jnp.where(causal, gap, 0.0)), 0.0)
        mixing = (intersection * decays * delta_row_ref[h : h + 1, :]).astype(jnp.bfloat16)
        x_head = x_values[:, lanes]
        x_wide = x_head.astype(jnp.float32)
        within = jnp.dot(mixing, x_head, preferred_element_type=jnp.float32)
        partial_ref[:, lanes] = within + skip_ref[:, lanes] * x_wide
        scaled[:, lanes] = (x_wide * tail_ref[:, h : h + 1]).astype(jnp.bfloat16)
    update_ref[...] = lax.dot_general(
        scaled[...], input_map, (((0,), (0,)), ((), ())), preferred_element_type=jnp.float32
    )


def state_kernel(me_ref, state_place_ref, store_place_ref, update_ref, decay_row_ref, *rest):
    peers = (len(rest) - 10) // 2
    gots, prior_ref, sends = rest[:peers], rest[peers], rest[peers + 1 : 2 * peers + 1]
    pages, finals, from_kind, from_index, to_kind, to_index, counts, in_sems, out_sems = rest[
        2 * peers + 1 :
    ]
    request, group = pl.program_id(0), pl.program_id(1)
    page_count, heads, page_rows, state = pages.shape
    slots = gots[0].shape[0]
    head_dim = page_count * page_rows
    joint = 16 // page_rows
    me = me_ref[0]

    @pl.when((request == 0) & (group == 0))
    def _():
        for peer in range(2 * peers):
            counts[peer] = 0

        def row_step(offset, carry):
            for j in range(page_count):
                entry = offset * page_count + j
                place = state_place_ref[me * REQUESTS_PER_IDX + offset, j]
                owner = place // slots
                rank = counts[owner]
                counts[owner] = rank + 1
                distance = (me - owner + peers) % peers
                from_kind[entry] = distance
                from_index[entry] = jnp.where(distance == 0, place - me * slots, rank)
                target = store_place_ref[me * REQUESTS_PER_IDX + offset, j] // slots
                to_index[entry] = counts[peers + target]
                counts[peers + target] = to_index[entry] + 1
                to_kind[entry] = (target - me + peers) % peers
            return carry

        lax.fori_loop(0, REQUESTS_PER_IDX, row_step, jnp.int32(0))

    half = pl.ds(group * heads, heads)

    def arrive(j, kind):
        index = from_index[request * page_count + j]
        return pltpu.make_async_copy(gots[kind].at[index, half], pages.at[j], in_sems.at[j])

    def depart(j, kind):
        index = to_index[request * page_count + j]
        return pltpu.make_async_copy(finals.at[j], sends[kind].at[index, half], out_sems.at[j])

    def start_arrival(j):
        for kind in range(peers):

            @pl.when(from_kind[request * page_count + j] == kind)
            def _(kind=kind):
                arrive(j, kind).start()

    def start_departure(j):
        for kind in range(peers):

            @pl.when(to_kind[request * page_count + j] == kind)
            def _(kind=kind):
                depart(j, kind).start()

    def each(start, end, act):
        def step(j, carry):
            act(j)
            return carry

        lax.fori_loop(start, end, step, jnp.int32(0))

    each(0, page_count, start_arrival)
    last = decay_row_ref.shape[1] - 1
    growths = [jnp.exp(decay_row_ref[h : h + 1, last : last + 1]) for h in range(heads)]

    def joint_step(step, carry):
        first = step * joint
        each(first, first + joint, lambda j: arrive(j, 0).wait())
        for h in range(heads):
            rows = pl.ds(pl.multiple_of(h * head_dim + step * 16, 16), 16)
            old = jnp.concatenate(
                [pages[first + i, h].astype(jnp.float32) for i in range(joint)], axis=0
            )
            prior_ref[rows, :] = old.astype(jnp.bfloat16)
            new = growths[h] * old + update_ref[rows, :]
            for i in range(joint):
                finals[first + i, h] = new[i * page_rows : (i + 1) * page_rows].astype(
                    jnp.bfloat16
                )
        each(first, first + joint, start_departure)
        return carry

    lax.fori_loop(0, page_count // joint, joint_step, jnp.int32(0))
    each(0, page_count, lambda j: depart(j, 0).wait())


def output_kernel(heads, partial_ref, output_map_ref, growth_ref, prior_ref, out_ref):
    head_dim = out_ref.shape[1] // heads
    carried = lax.dot_general(
        output_map_ref[...], prior_ref[...], HIDDEN, preferred_element_type=jnp.float32
    )
    for h in range(heads):
        lanes = slice(h * head_dim, (h + 1) * head_dim)
        out_ref[:, lanes] = (
            partial_ref[:, lanes] + growth_ref[:, h : h + 1] * carried[:, lanes]
        ).astype(jnp.bfloat16)


def list_pages(
    counts, passed, limits_ref, place_ref, prefix_ref, slots, page, kinds, indices, amounts, sizes, ranks
):
    me, limit, choice = limits_ref[0], limits_ref[1], limits_ref[2]
    page_count = place_ref.shape[1]
    peers = ranks.shape[1]
    start_row = me * REQUESTS_PER_IDX
    for peer in range(peers):
        ranks[0, peer] = 0
    if passed:

        def count_row(offset, carry):
            tokens = prefix_ref[start_row + offset]
            for j in range(page_count):
                owner = place_ref[start_row + offset, j] // slots
                ranks[0, owner] = ranks[0, owner] + jnp.where(j * page < tokens, 1, 0)
            return carry

        lax.fori_loop(0, REQUESTS_PER_IDX, count_row, jnp.int32(0))
        begin = jnp.int32(0)
        for peer in range(peers):
            ranks[1, peer] = begin
            begin = begin + jnp.where(peer == me, 0, jnp.maximum(ranks[0, peer] - limit, 0))
            ranks[0, peer] = 0
    def place_row(offset, carry):
        tokens = prefix_ref[start_row + offset]
        at, size = jnp.int32(0), jnp.int32(0)
        for j in range(page_count):
            place = place_ref[start_row + offset, j]
            owner = place // slots
            rank = ranks[0, owner]
            used = j * page < tokens
            ranks[0, owner] = rank + jnp.where(used, 1, 0)
            here = owner == me
            late = (rank >= limit) & jnp.logical_not(here)
            if passed:
                take = used & late
                kind = jnp.int32(0)
                index = ranks[1, owner] + rank - limit
            else:
                take = used & jnp.logical_not(late)
                kind = jnp.where(here, len(counts), choice)
                index = jnp.where(here, place - me * slots, owner * limit + rank)

            @pl.when(take)
            def _(at=at, kind=kind, index=index):
                kinds[offset * page_count + at] = kind
                indices[offset * page_count + at] = index

            at = at + jnp.where(take, 1, 0)
            size = size + jnp.where(take, jnp.minimum(page, tokens - j * page), 0)
        amounts[offset] = at
        sizes[offset] = size
        return carry

    lax.fori_loop(0, REQUESTS_PER_IDX, place_row, jnp.int32(0))


def score(scale, keys, query):
    return lax.dot_general(keys, query, HIDDEN, preferred_element_type=jnp.float32) * scale


def weigh(values, exponent):
    return lax.dot_general(
        values,
        exponent.astype(jnp.bfloat16),
        (((0,), (0,)), ((), ())),
        preferred_element_type=jnp.float32,
    )


def add_pages(scale, query, size, chunk, cached_kv, stats_ref, sums_ref):
    head_dim = query.shape[1]
    keys_at = lax.broadcasted_iota(jnp.int32, (chunk, query.shape[0]), 0)

    def chunk_step(step, carry):
        start = pl.multiple_of(step * chunk, chunk)
        scores = score(scale, cached_kv[pl.ds(start, chunk), :head_dim], query)
        scores = jnp.where(keys_at < size - start, scores, -jnp.inf)
        old = stats_ref[0:1, :]
        top = jnp.maximum(old, jnp.max(scores, axis=0, keepdims=True))
        fade = jnp.exp(old - top)
        exponent = jnp.exp(scores - top)
        stats_ref[0:1, :] = top
        stats_ref[1:2, :] = stats_ref[1:2, :] * fade + jnp.sum(exponent, axis=0, keepdims=True)
        sums_ref[...] = sums_ref[...] * fade + weigh(
            cached_kv[pl.ds(start, chunk), head_dim:], exponent
        )
        return carry

    lax.fori_loop(0, (size + chunk - 1) // chunk, chunk_step, jnp.int32(0))


def attend_kernel(scale, counts, limits_ref, place_ref, prefix_ref, pool_ref, *rest):
    gots = rest[: len(counts)]
    query_ref, fresh_ref, sums_ref, stats_ref = rest[len(counts) : len(counts) + 4]
    cached_kv, kinds, indices, amounts, sizes, ranks, sems = rest[len(counts) + 4 :]
    request, kv_head = pl.program_id(0), pl.program_id(1)
    per_kv, length, head_dim = query_ref.shape
    slots, page = pool_ref.shape[0], pool_ref.shape[2]
    page_count = place_ref.shape[1]

    @pl.when((request == 0) & (kv_head == 0))
    def _():
        cached_kv[...] = jnp.zeros_like(cached_kv)
        list_pages(
            counts, False, limits_ref, place_ref, prefix_ref, slots, page,
            kinds, indices, amounts, sizes, ranks,
        )

    amount = amounts[request]

    def target(j):
        return cached_kv.at[pl.ds(pl.multiple_of(j * page, page), page)]

    def start_copy(j, carry):
        entry = request * page_count + j
        for kind, source in enumerate(gots + (pool_ref,)):

            @pl.when(kinds[entry] == kind)
            def _(source=source):
                pltpu.make_async_copy(
                    source.at[indices[entry], kv_head], target(j), sems.at[j]
                ).start()

        return carry

    lax.fori_loop(0, amount, start_copy, jnp.int32(0))
    query = query_ref[...].reshape(per_kv * length, head_dim)
    keys_at = lax.broadcasted_iota(jnp.int32, (length, per_kv * length), 0)
    queries_at = lax.broadcasted_iota(jnp.int32, (length, per_kv * length), 1) % length
    scores = score(scale, fresh_ref[:, :head_dim], query)
    scores = jnp.where(keys_at <= queries_at, scores, -jnp.inf)
    top = jnp.max(scores, axis=0, keepdims=True)
    exponent = jnp.exp(scores - top)
    stats_ref[0:1, :] = top
    stats_ref[1:2, :] = jnp.sum(exponent, axis=0, keepdims=True)
    sums_ref[...] = weigh(fresh_ref[:, head_dim:], exponent)

    def wait_copy(j, carry):
        pltpu.make_async_copy(pool_ref.at[0, kv_head], target(j), sems.at[j]).wait()
        return carry

    lax.fori_loop(0, amount, wait_copy, jnp.int32(0))
    add_pages(scale, query, sizes[request], length, cached_kv, stats_ref, sums_ref)


def attend_passed_kernel(
    scale,
    counts,
    slots,
    limits_ref,
    place_ref,
    prefix_ref,
    passed_ref,
    query_ref,
    sums_in_ref,
    stats_in_ref,
    out_ref,
    cached_kv,
    sums_ref,
    stats_ref,
    kinds,
    indices,
    amounts,
    sizes,
    ranks,
    sems,
):
    request, kv_head = pl.program_id(0), pl.program_id(1)
    per_kv, length, head_dim = query_ref.shape
    page = passed_ref.shape[2]
    page_count = place_ref.shape[1]

    @pl.when((request == 0) & (kv_head == 0))
    def _():
        cached_kv[...] = jnp.zeros_like(cached_kv)
        list_pages(
            counts, True, limits_ref, place_ref, prefix_ref, slots, page,
            kinds, indices, amounts, sizes, ranks,
        )

    amount = amounts[request]

    def fetch(j, index):
        target = cached_kv.at[pl.ds(pl.multiple_of(j * page, page), page)]
        return pltpu.make_async_copy(passed_ref.at[index, kv_head], target, sems.at[j])

    def start_copy(j, carry):
        fetch(j, indices[request * page_count + j]).start()
        return carry

    def wait_copy(j, carry):
        fetch(j, 0).wait()
        return carry

    @pl.when(amount == 0)
    def _():
        out_ref[...] = (
            (sums_in_ref[...] / stats_in_ref[1:2, :]).T.astype(jnp.bfloat16).reshape(out_ref.shape)
        )

    @pl.when(amount > 0)
    def _():
        lax.fori_loop(0, amount, start_copy, jnp.int32(0))
        sums_ref[...] = sums_in_ref[...]
        stats_ref[...] = stats_in_ref[...]
        lax.fori_loop(0, amount, wait_copy, jnp.int32(0))
        query = query_ref[...].reshape(per_kv * length, head_dim)
        add_pages(scale, query, sizes[request], length, cached_kv, stats_ref, sums_ref)
        out_ref[...] = (
            (sums_ref[...] / stats_ref[1:2, :]).T.astype(jnp.bfloat16).reshape(out_ref.shape)
        )


def body(
    mixer_in,
    maps_in,
    delta_raw,
    conv_cache,
    maps_cache,
    conv_weight,
    maps_weight,
    decay_log,
    skip_gain,
    state_pool,
    queries,
    suffix_keyvals,
    page_pool,
    prefix_tokens,
    page_place,
    state_place,
    store_place,
):
    peers = lax.axis_size("req")
    me = lax.axis_index("req").astype(jnp.int32).reshape(1)
    requests, length = REQUESTS_PER_IDX, APPENDED_LENGTH
    groups = maps_in.shape[1]
    state = maps_in.shape[2] // 2
    heads = delta_raw.shape[1]
    per_group = heads // groups
    width = mixer_in.shape[1]
    group_width = width // groups
    head_dim = width // heads
    slots, _, page_rows, _ = state_pool.shape
    page_count = state_place.shape[1]
    kv_heads = page_pool.shape[2]
    attend_dim = queries.shape[2]
    per_kv = queries.shape[1] // kv_heads
    page = page_pool.shape[1]
    prefix_pages = page_place.shape[1]
    page_slots = page_pool.shape[0]
    pair_pages = requests * prefix_pages // peers
    taps = conv_weight.shape[0]

    def exchange(pages):
        return lax.all_to_all(pages, "req", split_axis=0, concat_axis=0, tiled=True)

    capacity = requests * page_count // peers
    distances = range(1, peers)

    def send_to(distance, pages):
        return lax.ppermute(
            pages, "req", [(peer, (peer + distance) % peers) for peer in range(peers)]
        )

    def ends(distance):
        return jnp.concatenate([me, (me + distance) % peers])

    state_gots = [state_pool] + [
        send_to(distance, gather_for(ends(distance), state_place, state_pool, capacity))
        for distance in distances
    ]

    counts = tuple(sorted({max(1, pair_pages * share // 16) for share in SHARES}))
    used = jnp.arange(prefix_pages)[None, :] * page < prefix_tokens[:, None]
    holders = page_place // page_slots
    pairs = used[:, :, None] & (holders[:, :, None] == jnp.arange(peers)[None, None, :])
    needs = jnp.sum(pairs.reshape(peers, -1, peers).astype(jnp.int32), axis=1)
    places = jnp.arange(peers)
    both = jnp.sum(needs.reshape(peers // 2, 2, peers), axis=1)
    outside = jnp.arange(peers // 2)[:, None] != places[None, :] // 2
    limit_table = jnp.array(counts, jnp.int32)
    crowded = jnp.max(jnp.where(outside, both, 0)) > 2 * limit_table
    rests = jnp.maximum(needs[None] - limit_table[:, None, None], 0)
    rests = jnp.where(places[:, None] != places[None, :], rests, 0)
    crowded = crowded | (jnp.max(jnp.sum(rests, axis=2), axis=1) > PASSED)
    choice = jnp.sum(crowded.astype(jnp.int32))
    limit = jnp.sum(jnp.where(jnp.arange(len(counts)) == choice, limit_table, 0))
    limits = jnp.stack([me[0], limit, choice])
    pages_by_head = page_pool.transpose(0, 2, 1, 3)
    page_sends = send_used(counts, limits, page_place, prefix_tokens, pages_by_head)

    delta = jax.nn.softplus(delta_raw.T.astype(jnp.float32)).reshape(heads, requests, length)
    log_decay = jnp.cumsum(-delta * jnp.exp(decay_log)[:, None, None], axis=2)
    tail = jnp.exp(log_decay[:, :, -1:] - log_decay) * delta
    growth = jnp.exp(log_decay)

    def by_rows(values):
        return values.reshape(groups, per_group, requests, length).transpose(2, 0, 1, 3)

    def by_columns(values):
        return values.reshape(groups, per_group, requests, length).transpose(2, 0, 3, 1)

    decay_row = by_rows(log_decay)
    maps_split = maps_in.transpose(1, 0, 2)
    empty = 8 - (taps - 1)
    x_cache = jnp.pad(conv_cache.astype(jnp.float32), ((0, 0), (empty, 0), (0, 0)))
    maps_edge = jnp.pad(
        maps_cache.transpose(0, 2, 1, 3).astype(jnp.float32), ((0, 0), (0, 0), (empty, 0), (0, 0))
    )
    row_block = pl.BlockSpec((None, None, per_group, length), lambda r, g: (r, g, 0, 0))
    column_block = pl.BlockSpec((None, None, length, per_group), lambda r, g: (r, g, 0, 0))
    x_block = pl.BlockSpec((length, group_width), lambda r, g: (r, g))
    update_block = pl.BlockSpec((None, None, group_width, state), lambda r, g: (r, g, 0, 0))
    map_block = pl.BlockSpec((None, length, state), lambda r, g: (g, r, 0))
    partial, update, output_map = pl.pallas_call(
        functools.partial(inner_kernel, per_group),
        grid=(requests, groups),
        in_specs=[
            x_block,
            pl.BlockSpec((None, 8, group_width), lambda r, g: (r, 0, g)),
            pl.BlockSpec((taps, group_width), lambda r, g: (0, g)),
            pl.BlockSpec((None, length, 2 * state), lambda r, g: (g, r, 0)),
            pl.BlockSpec((None, None, 8, 2 * state), lambda r, g: (r, g, 0, 0)),
            pl.BlockSpec((None, taps, 2 * state), lambda r, g: (g, 0, 0)),
            row_block,
            column_block,
            row_block,
            column_block,
            pl.BlockSpec((1, group_width), lambda r, g: (0, g)),
        ],
        out_specs=[x_block, update_block, map_block],
        out_shape=[
            jax.ShapeDtypeStruct((requests * length, width), jnp.float32),
            jax.ShapeDtypeStruct((requests, groups, group_width, state), jnp.float32),
            jax.ShapeDtypeStruct((groups, requests * length, state), jnp.bfloat16),
        ],
        scratch_shapes=[
            pltpu.VMEM((8 + length, group_width), jnp.float32),
            pltpu.VMEM((8 + length, 2 * state), jnp.float32),
            pltpu.VMEM((length, group_width), jnp.bfloat16),
            pltpu.VMEM((length, group_width), jnp.bfloat16),
        ],
        cost_estimate=pl.CostEstimate(
            flops=3 * requests * length * width * state,
            bytes_accessed=32 * 2**20,
            transcendentals=requests * heads * length * length,
        ),
        compiler_params=params(),
        name="mix_new_tokens",
    )(
        mixer_in,
        x_cache,
        conv_weight.astype(jnp.float32),
        maps_split,
        maps_edge,
        maps_weight.transpose(1, 0, 2).astype(jnp.float32),
        decay_row,
        by_columns(log_decay),
        by_rows(delta),
        by_columns(tail),
        jnp.repeat(skip_gain, head_dim).reshape(1, width),
    )
    growth_col = by_columns(growth)
    grouped_queries = queries.reshape(requests, length, kv_heads, per_kv, attend_dim).transpose(
        0, 2, 3, 1, 4
    )
    fresh = suffix_keyvals.transpose(1, 0, 2)

    page_sends, state_gots, partial, update, output_map, growth_col, decay_row = (
        lax.optimization_barrier(
            (page_sends, state_gots, partial, update, output_map, growth_col, decay_row)
        )
    )
    state_block = pl.BlockSpec((None, None, group_width, state), lambda r, g, *_: (r, g, 0, 0))

    def advance(at, sends, state_gots, update, decay_row):
        shapes = [pltpu.HBM(sent.shape, sent.dtype) for sent in sends]
        others = list(unwritten(shapes[:at] + shapes[at + 1 :])) if len(shapes) > 1 else []
        gots = tuple(others[:at] + [exchange(sends[at])] + others[at:])
        prior, *final_sends = pl.pallas_call(
            state_kernel,
            grid_spec=pltpu.PrefetchScalarGridSpec(
                num_scalar_prefetch=3,
                grid=(requests, groups),
                in_specs=[
                    state_block,
                    pl.BlockSpec((None, None, per_group, length), lambda r, g, *_: (r, g, 0, 0)),
                ]
                + [any_spec()] * peers,
                out_specs=[state_block] + [hbm_spec()] * peers,
                scratch_shapes=[
                    pltpu.VMEM((page_count, per_group, page_rows, state), jnp.bfloat16),
                    pltpu.VMEM((page_count, per_group, page_rows, state), jnp.bfloat16),
                    *[pltpu.SMEM((requests * page_count,), jnp.int32)] * 4,
                    pltpu.SMEM((2 * peers,), jnp.int32),
                    pltpu.SemaphoreType.DMA((page_count,)),
                    pltpu.SemaphoreType.DMA((page_count,)),
                ],
            ),
            out_shape=[
                jax.ShapeDtypeStruct(update.shape, jnp.bfloat16),
                *[pltpu.HBM((capacity,) + state_pool.shape[1:], jnp.bfloat16)] * peers,
            ],
            cost_estimate=pl.CostEstimate(
                flops=4 * update.size, bytes_accessed=20 * 2**20, transcendentals=0
            ),
            compiler_params=params(),
            name="advance_states",
        )(me, state_place, store_place, update, decay_row, *state_gots)
        return gots, prior, final_sends

    page_gots, prior, final_sends = lax.switch(
        choice,
        [functools.partial(advance, at) for at in range(len(counts))],
        tuple(page_sends),
        state_gots,
        update,
        decay_row,
    )
    final_gots = [final_sends[0]] + [
        send_to(distance, final_sends[distance]) for distance in distances
    ]
    mixer_out = pl.pallas_call(
        functools.partial(output_kernel, per_group),
        grid=(requests, groups),
        in_specs=[
            x_block,
            map_block,
            column_block,
            pl.BlockSpec((None, None, group_width, state), lambda r, g: (r, g, 0, 0)),
        ],
        out_specs=x_block,
        out_shape=jax.ShapeDtypeStruct((requests * length, width), jnp.bfloat16),
        cost_estimate=pl.CostEstimate(
            flops=2 * requests * length * width * state,
            bytes_accessed=18 * 2**20,
            transcendentals=0,
        ),
        compiler_params=params(),
        name="add_carried",
    )(partial, output_map, growth_col, prior)
    passed = pass_on(counts, limits, page_place, prefix_tokens, pages_by_head, page_gots)
    stored = None
    for distance, got in enumerate(final_gots):
        if distance == min(2, peers - 1):
            passed, stored = lax.optimization_barrier((passed, stored))
        stored = scatter_from(
            ends(peers - distance), store_place, got, stored, state_pool.shape
        )
    rows = per_kv * length
    head_block = pl.BlockSpec(
        (None, None, per_kv, length, attend_dim), lambda r, e, *_: (r, e, 0, 0, 0)
    )
    sums_block = pl.BlockSpec((None, None, attend_dim, rows), lambda r, e, *_: (r, e, 0, 0))
    stats_block = pl.BlockSpec((None, None, 2, rows), lambda r, e, *_: (r, e, 0, 0))
    lists = [
        pltpu.SMEM((requests * prefix_pages,), jnp.int32),
        pltpu.SMEM((requests * prefix_pages,), jnp.int32),
        pltpu.SMEM((requests,), jnp.int32),
        pltpu.SMEM((requests,), jnp.int32),
        pltpu.SMEM((2, peers), jnp.int32),
    ]
    sums, stats = pl.pallas_call(
        functools.partial(attend_kernel, attend_dim**-0.5, counts),
        grid_spec=pltpu.PrefetchScalarGridSpec(
            num_scalar_prefetch=3,
            grid=(requests, kv_heads),
            in_specs=[any_spec()] * (len(page_gots) + 1)
            + [
                head_block,
                pl.BlockSpec((None, length, 2 * attend_dim), lambda r, e, *_: (e, r, 0)),
            ],
            out_specs=[sums_block, stats_block],
            scratch_shapes=[
                pltpu.VMEM((prefix_pages * page, 2 * attend_dim), jnp.bfloat16),
                *lists,
                pltpu.SemaphoreType.DMA((prefix_pages,)),
            ],
        ),
        out_shape=[
            jax.ShapeDtypeStruct((requests, kv_heads, attend_dim, rows), jnp.float32),
            jax.ShapeDtypeStruct((requests, kv_heads, 2, rows), jnp.float32),
        ],
        cost_estimate=pl.CostEstimate(
            flops=4 * queries.size * (prefix_pages * page + length),
            bytes_accessed=16 * 2**20,
            transcendentals=queries.shape[0] * queries.shape[1] * (prefix_pages * page),
        ),
        compiler_params=params(),
        name="attend",
    )(
        limits,
        page_place,
        prefix_tokens,
        pages_by_head,
        *page_gots,
        grouped_queries,
        fresh,
    )
    attended = pl.pallas_call(
        functools.partial(attend_passed_kernel, attend_dim**-0.5, counts, page_slots),
        grid_spec=pltpu.PrefetchScalarGridSpec(
            num_scalar_prefetch=3,
            grid=(requests, kv_heads),
            in_specs=[any_spec(), head_block, sums_block, stats_block],
            out_specs=head_block,
            scratch_shapes=[
                pltpu.VMEM((-(-PASSED * page // length) * length, 2 * attend_dim), jnp.bfloat16),
                pltpu.VMEM((attend_dim, rows), jnp.float32),
                pltpu.VMEM((2, rows), jnp.float32),
                *lists,
                pltpu.SemaphoreType.DMA((PASSED,)),
            ],
        ),
        out_shape=jax.ShapeDtypeStruct(grouped_queries.shape, jnp.bfloat16),
        cost_estimate=pl.CostEstimate(
            flops=queries.size * PASSED * page,
            bytes_accessed=8 * 2**20,
            transcendentals=queries.shape[0] * queries.shape[1] * PASSED * page // 4,
        ),
        compiler_params=params(),
        name="attend_passed",
    )(limits, page_place, prefix_tokens, passed, grouped_queries, sums, stats)
    attention_out = attended.transpose(0, 3, 1, 2, 4).reshape(queries.shape)
    return mixer_out, attention_out, stored


def solution(mesh):
    placed = (
        P(("parts", "req"), "tp"),
        P(("parts", "req"), "tp", None),
        P(("parts", "req"), "tp"),
        P(("parts", "req"), None, "tp"),
        P(("parts", "req"), None, "tp", None),
        P(None, "tp"),
        P(None, "tp", None),
        P("tp"),
        P("tp"),
        P(("parts", "req"), "tp", None, None),
        P(("parts", "req"), "tp", None),
        P(("parts", "req"), "tp", None),
        P(("parts", "req"), None, "tp", None),
        P("parts"),
        P("parts", None),
        P("parts", None),
        P("parts", None),
    )
    return jax.shard_map(
        body,
        mesh=mesh,
        in_specs=placed,
        out_specs=(
            P(("parts", "req"), "tp"),
            P(("parts", "req"), "tp", None),
            P(("parts", "req"), "tp", None, None),
        ),
        check_vma=False,
    )
```
